32 devices in a mesh: lon: 16 (over z, y, core), lat: 2 (over x).
Axes of the slice: x: 2, y: 2, z: 4, core: 2. Of those that a mesh axis runs over, the one named last changes fastest.
Arguments:
- slab_features: bfloat16 [24, 256, 1024], P('lat', 'lon'), may hold values from -5 to 5
- upstream_gradient: bfloat16 [24, 256, 1024], P('lat', 'lon'), may hold values from -4 to 4
- rim_feature_rows: bfloat16 [2, 6, 256, 1024], P(None, None, 'lon'), may hold values from -5 to 5
- rim_presence_flags: int32 [2, 6], replicated, may hold values 0 or 1
- feature_rescaling_coefficients: float32 [1024], replicated, may hold values from 0.1 to 1.9
- triple_projection_matrix: bfloat16 [1024, 3072], replicated, may hold values from -0.1875 to 0.1875
- final_projection_matrix: bfloat16 [1024, 1024], replicated, may hold values from -0.75 to 0.75
- score_sharpness: float32 [16], replicated, may hold values from 3 to 12
- column_group_decoder_longitude: int32 [24, 64], P('lat', 'lon'), may hold values from 0 to 15, as said below
Outputs:
- decoder_rows: bfloat16 [2, 16, 16, 6, 4, 1024], P('lat', 'lon')
- input_grad: bfloat16 [24, 256, 1024], P('lat', 'lon')
The draws below stay inside these ranges and needn't reach their ends.
Inputs may be any that keep to these rules, and one draw needn't show every extreme that they name: `column_group_decoder_longitude`: the 48 segments of one device name any one owner at most 6 times; one owner, drawn anew for every draw, is named exactly 6 times by the segments of every device.
All inputs are finite; a program needn't handle non-finite values.
Results may differ from the reference program's by a relative error of at most 0.0085.
Values may be sent and summed in bfloat16 or wider, within the bound.
No kernel may reach another device: no remote copies, remote signals or barrier semaphores. Data moves between devices by JAX's collectives and lax.ppermute only.
A program may use at most 128 MiB of HBM per device.

```python
import math
import jax
import jax.numpy as jnp
from jax import lax

D = 1024
ATTN_CHANNELS = 16
HALO = 6
ROWS = 12
COLS = 16
SEG = 4
MOST = 6
NLAT = 24
NLON = 256
N_LON = 16
N_LAT = 2


def field_draw(key, full_shape):
    key_base, key_cols = jax.random.split(key, 2)
    columns = jnp.exp(jax.random.uniform(key_cols, (full_shape[-1],), jnp.float32, math.log(0.3), math.log(3.0)))
    base_draw = jnp.clip(jax.random.normal(key_base, full_shape, jnp.float32), -3.0, 3.0)
    return 0.5 * columns * base_draw


def draw_slab_features(key, part):
    return field_draw(jax.random.fold_in(key, 11), (NLAT, NLON, D)).astype(jnp.bfloat16)


def draw_rim_feature_rows(key, part):
    return field_draw(jax.random.fold_in(key, 23), (2, HALO, NLON, D)).astype(jnp.bfloat16)


def draw_column_group_decoder_longitude(key, part):
    key_hot, key_blocks = jax.random.split(jax.random.fold_in(key, 37))
    seg_count = COLS // SEG
    block_size = ROWS * seg_count
    hot_owner = jax.random.randint(key_hot, (), 0, N_LON, dtype=jnp.int32)
    owners = jnp.repeat(jnp.arange(N_LON, dtype=jnp.int32), MOST)

    def one_block(block_key):
        key_deck, key_place = jax.random.split(block_key)
        ranking = jax.random.permutation(key_deck, N_LON * MOST).astype(jnp.int32)
        ranking = jnp.where(owners == hot_owner, -1, ranking)
        picked = owners[jnp.argsort(ranking, stable=True)][:block_size]
        return picked[jax.random.permutation(key_place, block_size)]
    labels = jax.vmap(one_block)(jax.random.split(key_blocks, N_LAT * N_LON))
    labels = labels.reshape(N_LAT, N_LON, ROWS, seg_count)
    return labels.transpose(0, 2, 1, 3).reshape(N_LAT * ROWS, N_LON * seg_count)


def set_ends(array, key, least, largest):
    shape = array.shape
    spot = [jax.random.randint(jax.random.fold_in(key, axis), (), 0, shape[axis]) for axis in range(len(shape))]
    array = array.at[tuple(spot)].set(least)
    longest = shape.index(max(shape))
    spot[longest] = (spot[longest] + 1) % shape[longest]
    return array.at[tuple(spot)].set(largest)


def shard_levels(key, dims, shards, low, top_value):
    loudness, own = 1.0, jax.random.fold_in(key, 6)
    for axis_at, parts in shards:
        steps = jnp.exp(jax.random.uniform(jax.random.fold_in(own, axis_at), (parts,), jnp.float32, low / len(shards), top_value / len(shards)))
        loudness = loudness * jnp.repeat(steps, dims[axis_at] // parts).reshape([-1 if axis == axis_at else 1 for axis in range(len(dims))])
    return loudness


def bell_draw(own_key, dims, width, reach, cuts=(), held_as=jnp.bfloat16):
    drawn = jax.random.normal(own_key, dims, jnp.float32) * width
    if len(cuts) > 0:
        drawn = shard_levels(own_key, dims, cuts, -0.22, 0.18) * drawn
    return jnp.clip(drawn, min=-reach, max=reach).astype(held_as)


def setup_inputs(seed: int = 0) -> dict:
    splits = jax.random.split(jax.random.key(seed), 10)
    return {
        "slab_features": draw_slab_features(jax.random.fold_in(splits[9], 71), 0),
        "upstream_gradient": bell_draw(splits[1], (NLAT, NLON, D), 1.0, 4.0, ((0, 2), (1, 16))),
        "rim_feature_rows": draw_rim_feature_rows(jax.random.fold_in(splits[9], 71), 0),
        "rim_presence_flags": set_ends((jax.random.randint(splits[3], (2, HALO), 0, 2) < 1).astype(jnp.int32), jax.random.fold_in(splits[3], 1), 0, 1),
        "feature_rescaling_coefficients": jnp.clip(1.0 + 0.18 * jax.random.normal(splits[4], (D,), jnp.float32), 0.1, 1.9),
        "triple_projection_matrix": bell_draw(splits[5], (D, 3 * D), D ** -0.5, 0.1875),
        "final_projection_matrix": bell_draw(splits[6], (D, D), (D // 16) ** -0.5, 0.75),
        "score_sharpness": jnp.clip(jnp.exp(jax.random.uniform(splits[7], (ATTN_CHANNELS,), jnp.float32, math.log(3.0), math.log(12.0))), 3.0, 12.0),
        "column_group_decoder_longitude": draw_column_group_decoder_longitude(jax.random.fold_in(splits[9], 71), 0),
    }


def rms_normed(vectors, gain_row):
    return vectors * lax.rsqrt(lax.optimization_barrier(jnp.mean(vectors * vectors, axis=-1, keepdims=True)) + 1e-05) * gain_row

def unit_heads(raw_part, channel_count):
    full_shape = raw_part.shape
    per_head = raw_part.reshape(full_shape[:-1] + (channel_count, full_shape[-1] // channel_count))
    per_head = per_head * lax.rsqrt(lax.optimization_barrier(jnp.mean(per_head * per_head, axis=-1, keepdims=True)) + 1e-06)
    return per_head.reshape(full_shape)

def question_multiplier(score_sharpness, feature_dimension):
    channel_count = score_sharpness.shape[0]
    return jnp.repeat(score_sharpness / (feature_dimension // channel_count), feature_dimension // channel_count)

def window_keep(row_count, col_count, halo_width, row_keep):
    ext_rows = row_count + 2 * halo_width
    ext_cols = col_count + 2 * halo_width
    query_ids = jnp.arange(row_count * col_count, dtype=jnp.int32)
    key_ids = jnp.arange(ext_rows * ext_cols, dtype=jnp.int32)
    near_rows = jnp.abs(key_ids[None, :] // ext_cols - halo_width - query_ids[:, None] // col_count) <= halo_width
    near_cols = jnp.abs(key_ids[None, :] % ext_cols - halo_width - query_ids[:, None] % col_count) <= halo_width
    key_keep = jnp.broadcast_to(row_keep[:, None], (ext_rows, ext_cols)).reshape(-1)
    return jnp.where(near_rows & near_cols, key_keep[None, :], 0.0)

def attend(queries, grad_out, ext_kv, keep_mask, channel_count):
    row_count, col_count, feature_dimension = queries.shape
    ext_rows, ext_cols = (ext_kv.shape[0], ext_kv.shape[1])
    head_dim = feature_dimension // channel_count
    query_mat = queries.reshape(row_count * col_count, channel_count, head_dim).astype(jnp.float32)
    flat_kv = ext_kv.reshape(ext_rows * ext_cols, 2 * feature_dimension).astype(jnp.float32)
    key_heads = flat_kv[:, :feature_dimension].reshape(-1, channel_count, head_dim)
    value_heads = flat_kv[:, feature_dimension:].reshape(-1, channel_count, head_dim)
    scores = jnp.einsum('qhd,khd->hqk', query_mat, key_heads)
    weights = jnp.exp(scores) * keep_mask[None]
    attn_probs = weights / lax.optimization_barrier(jnp.sum(weights, axis=-1, keepdims=True))
    probs_low = attn_probs.astype(jnp.bfloat16).astype(jnp.float32)
    mixed_out = jnp.einsum('hqk,khd->qhd', probs_low, value_heads)
    grad_mat = grad_out.reshape(row_count * col_count, channel_count, head_dim).astype(jnp.float32)
    grad_probs = jnp.einsum('qhd,khd->hqk', grad_mat, value_heads)
    inner_sum = lax.optimization_barrier(jnp.sum(attn_probs * grad_probs, axis=-1, keepdims=True))
    grad_scores = (attn_probs * (grad_probs - inner_sum)).astype(jnp.bfloat16).astype(jnp.float32)
    grad_query = jnp.einsum('hqk,khd->qhd', grad_scores, key_heads)
    grad_keys = jnp.einsum('hqk,qhd->khd', grad_scores, query_mat)
    grad_values = jnp.einsum('hqk,qhd->khd', probs_low, grad_mat)
    grad_ext = jnp.concatenate([grad_keys.reshape(ext_rows, ext_cols, feature_dimension), grad_values.reshape(ext_rows, ext_cols, feature_dimension)], axis=-1)
    return (mixed_out.reshape(row_count, col_count, feature_dimension).astype(jnp.bfloat16), grad_query.reshape(row_count, col_count, feature_dimension), grad_ext)

def assemble(blocks):
    feature_dimension = blocks.shape[-1]
    grid = blocks.reshape(N_LAT, N_LON, ROWS, COLS, feature_dimension).transpose(0, 2, 1, 3, 4)
    return grid.reshape(NLAT, NLON, feature_dimension)

def reference(slab_features, upstream_gradient, rim_feature_rows, rim_presence_flags, feature_rescaling_coefficients, triple_projection_matrix, final_projection_matrix, score_sharpness, column_group_decoder_longitude):
    feature_dimension = D
    token_vals = slab_features.astype(jnp.float32)
    normed = rms_normed(token_vals, feature_rescaling_coefficients).astype(jnp.bfloat16)
    projected = jnp.dot(normed, triple_projection_matrix, preferred_element_type=jnp.float32)
    raw_query = projected[..., :feature_dimension]
    raw_keys = projected[..., feature_dimension:2 * feature_dimension]
    multiplier_array = question_multiplier(score_sharpness, feature_dimension)
    query_hat = (unit_heads(raw_query, ATTN_CHANNELS) * multiplier_array).astype(jnp.bfloat16)
    own_kv = jnp.concatenate([unit_heads(raw_keys, ATTN_CHANNELS).astype(jnp.bfloat16), projected[..., 2 * feature_dimension:].astype(jnp.bfloat16)], axis=-1)
    rim_normed = rms_normed(rim_feature_rows.astype(jnp.float32), feature_rescaling_coefficients).astype(jnp.bfloat16)
    rim_proj = jnp.dot(rim_normed, triple_projection_matrix[:, feature_dimension:], preferred_element_type=jnp.float32)
    rim_kv = jnp.concatenate([unit_heads(rim_proj[..., :feature_dimension], ATTN_CHANNELS).astype(jnp.bfloat16), rim_proj[..., feature_dimension:].astype(jnp.bfloat16)], axis=-1)
    full_kv = jnp.concatenate([rim_kv[0], own_kv, rim_kv[1]], axis=0)
    full_kv = jnp.concatenate([full_kv[:, NLON - HALO:], full_kv, full_kv[:, :HALO]], axis=1)
    rim_keep = rim_presence_flags.astype(jnp.float32)
    row_keep = jnp.concatenate([rim_keep[0], jnp.ones((NLAT,), jnp.float32), rim_keep[1]])
    grad_attended = lax.dot_general(upstream_gradient, final_projection_matrix, (((2,), (1,)), ((), ())), preferred_element_type=jnp.float32).astype(jnp.bfloat16)
    ext_rows = ROWS + 2 * HALO
    ext_cols = COLS + 2 * HALO

    def one_block(grad_full, block_index):
        row_start = block_index // N_LON * ROWS
        col_start = block_index % N_LON * COLS
        zero_index = jnp.zeros((), jnp.int32)
        queries = lax.dynamic_slice(query_hat, (row_start, col_start, zero_index), (ROWS, COLS, feature_dimension))
        grad_out = lax.dynamic_slice(grad_attended, (row_start, col_start, zero_index), (ROWS, COLS, feature_dimension))
        ext_kv = lax.dynamic_slice(full_kv, (row_start, col_start, zero_index), (ext_rows, ext_cols, 2 * feature_dimension))
        block_keep = lax.dynamic_slice(row_keep, (row_start,), (ext_rows,))
        mixed_out, grad_query, grad_ext = attend(queries, grad_out, ext_kv, window_keep(ROWS, COLS, HALO, block_keep), ATTN_CHANNELS)
        current = lax.dynamic_slice(grad_full, (row_start, col_start, zero_index), (ext_rows, ext_cols, 2 * feature_dimension))
        grad_full = lax.dynamic_update_slice(grad_full, current + grad_ext, (row_start, col_start, zero_index))
        return (grad_full, (mixed_out, grad_query))
    grad_zero = jnp.zeros(full_kv.shape, jnp.float32)
    grad_full, (mixed_blocks, query_blocks) = lax.scan(one_block, grad_zero, jnp.arange(N_LAT * N_LON, dtype=jnp.int32))
    attended = assemble(mixed_blocks)
    grad_query = assemble(query_blocks)
    output_rows = (token_vals + jnp.dot(attended, final_projection_matrix, preferred_element_type=jnp.float32)).astype(jnp.bfloat16)
    center = grad_full[:, HALO:HALO + NLON]
    center = center + jnp.pad(grad_full[:, NLON + HALO:], ((0, 0), (0, NLON - HALO), (0, 0)))
    center = center + jnp.pad(grad_full[:, :HALO], ((0, 0), (NLON - HALO, 0), (0, 0)))
    grad_kv = center[HALO:HALO + NLAT]
    unused, query_back = jax.vjp(lambda raw_part: unit_heads(raw_part, ATTN_CHANNELS) * multiplier_array, raw_query)
    grad_raw_query = query_back(grad_query)[0]
    unused, key_back = jax.vjp(lambda raw_part: unit_heads(raw_part, ATTN_CHANNELS), raw_keys)
    grad_raw_keys = key_back(grad_kv[..., :feature_dimension])[0]
    grad_projected = jnp.concatenate([grad_raw_query, grad_raw_keys, grad_kv[..., feature_dimension:]], axis=-1).astype(jnp.bfloat16)
    grad_normed = lax.dot_general(grad_projected, triple_projection_matrix, (((2,), (1,)), ((), ())), preferred_element_type=jnp.float32)
    unused, norm_back = jax.vjp(lambda raw_part: rms_normed(raw_part, feature_rescaling_coefficients), token_vals)
    input_grad = (upstream_gradient.astype(jnp.float32) + norm_back(grad_normed)[0]).astype(jnp.bfloat16)
    seg_count = COLS // SEG
    block_size = ROWS * seg_count
    out_blocks = output_rows.reshape(N_LAT, ROWS, N_LON, COLS, D).transpose(0, 2, 1, 3, 4).reshape(N_LAT, N_LON, block_size, SEG * D)
    owner_blocks = column_group_decoder_longitude.reshape(N_LAT, ROWS, N_LON, seg_count).transpose(0, 2, 1, 3).reshape(N_LAT, N_LON, block_size)
    onehot = (owner_blocks[..., None] == jnp.arange(N_LON, dtype=jnp.int32)).astype(jnp.int32)
    earlier = jnp.cumsum(onehot, axis=2) - onehot
    slot_ids = owner_blocks * MOST + lax.optimization_barrier(jnp.sum(earlier * onehot, axis=-1))
    placing = (slot_ids[:, :, None, :] == jnp.arange(N_LON * MOST, dtype=jnp.int32)[:, None]).astype(jnp.float32)
    sent_slots = jnp.einsum('abst,abtw->absw', placing, out_blocks.astype(jnp.float32))
    decoder_rows = sent_slots.reshape(N_LAT, N_LON, N_LON, MOST, SEG, D).transpose(0, 2, 1, 3, 4, 5).astype(jnp.bfloat16)
    return (decoder_rows, input_grad)
```

```python
import functools

import jax
import jax.numpy as jnp
import numpy as np
from jax import lax
from jax.experimental import pallas as pl
from jax.experimental.pallas import tpu as pltpu
from jax.sharding import PartitionSpec as P

HEADS = 16
HALO = 6
ROWS = 12
COLS = 16
SEG = 4
D = 1024
HEAD_DIM = D // HEADS
TOKENS = ROWS * COLS
HALF = TOKENS // 2
BAND = HALO * COLS
SIDE = ROWS * HALO
CORNER = 40
QUAD = 256
QUAD_HEADS = QUAD // HEAD_DIM
STEPS = D // QUAD
STACK = QUAD_HEADS * HALF
PAD_SIDE = BAND + 2 * CORNER
MIDDLE = TOKENS + 2 * SIDE
SPAN = PAD_SIDE + MIDDLE
KEYS = SPAN + PAD_SIDE
HALO_ROWS = 2 * PAD_SIDE + 2 * SIDE - BAND
VMEM = 40 * 1024 * 1024
BF = jnp.bfloat16
F32 = jnp.float32


def dot(a, b):
    return jnp.dot(a, b, preferred_element_type=F32)


def dot_nt(a, b):
    return lax.dot_general(a, b, (((1,), (1,)), ((), ())), preferred_element_type=F32)


def dot_tn(a, b):
    return lax.dot_general(a, b, (((0,), (0,)), ((), ())), preferred_element_type=F32)


def selection_table():
    table = np.zeros((2, 2 * (SIDE + CORNER) + 2 * CORNER, TOKENS + BAND), np.float32)
    for lat in range(2):
        for side, first in ((0, COLS - HALO), (1, 0)):
            base = side * (SIDE + CORNER)
            for c in range(HALO):
                for r in range(ROWS):
                    table[lat, base + r * HALO + c, r * COLS + first + c] = 1
                for i in range(HALO):
                    table[lat, base + SIDE + i * HALO + c, TOKENS + i * COLS + first + c] = 1
                    row = i + HALO * (1 - lat)
                    corner = 2 * (SIDE + CORNER) + side * CORNER
                    table[lat, corner + i * HALO + c, row * COLS + first + c] = 1
    return table


def key_table():
    far = 1000
    table = np.full((8, KEYS), far, np.int32)
    table[3] = -1

    def put(at, count, width, first_col, kind):
        for k in range(count * width):
            i, c = divmod(k, width)
            for lat in range(2):
                low = {"lat": ROWS if lat == 0 else -HALO, "own": 0, "rim": -HALO if lat == 0 else ROWS}
                table[lat, at + k] = low[kind] + i
            table[2, at + k] = first_col + c
            if kind == "rim":
                table[3, at + k] = i

    put(0, HALO, COLS, 0, "lat")
    put(BAND, HALO, HALO, -HALO, "lat")
    put(BAND + CORNER, HALO, HALO, COLS, "lat")
    put(PAD_SIDE, ROWS, COLS, 0, "own")
    put(PAD_SIDE + TOKENS, ROWS, HALO, -HALO, "own")
    put(PAD_SIDE + TOKENS + SIDE, ROWS, HALO, COLS, "own")
    put(SPAN, HALO, COLS, 0, "rim")
    put(SPAN + BAND, HALO, HALO, -HALO, "rim")
    put(SPAN + BAND + CORNER, HALO, HALO, COLS, "rim")
    return table


def head_mask(h, dtype):
    lane = lax.broadcasted_iota(jnp.int32, (1, QUAD), 1)
    return jnp.where(lane // HEAD_DIM == h, 1.0, 0.0).astype(dtype)


def head_mean(values):
    a = lax.broadcasted_iota(jnp.int32, (QUAD, QUAD), 0) // HEAD_DIM
    b = lax.broadcasted_iota(jnp.int32, (QUAD, QUAD), 1) // HEAD_DIM
    block = jnp.where(a == b, 1.0 / HEAD_DIM, 0.0).astype(BF)
    high = values.astype(BF)
    low = (values - high.astype(F32)).astype(BF)
    return dot(high, block) + dot(low, block)


def inverse_rms(raw):
    return lax.rsqrt(head_mean(raw * raw) + 1e-06)


def normed(tokens, gain):
    tokens = tokens.astype(F32)
    return tokens * lax.rsqrt(jnp.mean(tokens * tokens, axis=-1, keepdims=True) + 1e-05) * gain


def multiplier(sharp_ref, j):
    out = jnp.zeros((1, QUAD), F32)
    for h in range(QUAD_HEADS):
        out = out + head_mask(h, F32) * (sharp_ref[j * QUAD_HEADS + h] / HEAD_DIM)
    return out


def stacked(block):
    return jnp.concatenate([block * head_mask(h, BF) for h in range(QUAD_HEADS)], axis=0)


def unstacked(stack):
    out = jnp.zeros((HALF, QUAD), F32)
    for h in range(QUAD_HEADS):
        out = out + stack[h * HALF : (h + 1) * HALF] * head_mask(h, F32)
    return out


def half_start(lat, half):
    return pl.multiple_of(HALF * ((1 - lat) if half == 0 else lat), 16)


def pack_kernel(lat_ref, x_ref, rim_ref, sel_ref, fwd_ref, bwd_ref, band_ref, cfwd_ref, cbwd_ref):
    lat = lat_ref[0]
    source = jnp.concatenate([x_ref[...], rim_ref[0]], axis=0)
    picked = dot(sel_ref[0], source)
    at = 0
    for ref in (fwd_ref, bwd_ref, cfwd_ref, cbwd_ref):
        count = ref.shape[0]
        ref[...] = picked[at : at + count].astype(BF)
        at += count
    band_ref[...] = x_ref[pl.ds(half_start(lat, 0), BAND), :]


def own_kernel(
    lat_ref, sharp_ref, x_ref, rim_ref, up_ref, gain_ref, wq_ref, wk_ref, wv_ref, wo_ref,
    qhat_ref, rawq_ref, rawk_ref, kv_ref, dout_ref, xn_ref,
):
    j = pl.program_id(0)

    @pl.when(j == 0)
    def _():
        xn_ref[:TOKENS] = normed(x_ref[...], gain_ref[...]).astype(BF)
        xn_ref[TOKENS:] = normed(rim_ref[0], gain_ref[...]).astype(BF)

    xn = xn_ref[...]
    raw_q = dot(xn[:TOKENS], wq_ref[...])
    rawq_ref[...] = raw_q
    qhat_ref[...] = (raw_q * inverse_rms(raw_q) * multiplier(sharp_ref, j)).astype(BF)
    raw_k = dot(xn, wk_ref[...])
    rawk_ref[...] = raw_k[:TOKENS]
    kv_ref[0] = (raw_k * inverse_rms(raw_k)).astype(BF)
    kv_ref[1] = dot(xn, wv_ref[...]).astype(BF)
    dout_ref[...] = dot_nt(up_ref[...], wo_ref[...]).astype(BF)


def forward_kernel(
    lat_ref, owner_ref, flag_ref, x_ref, band_ref, left_ref, right_ref, cleft_ref, cright_ref, gain_ref, tab_ref,
    wk_ref, wv_ref, wo_ref, qhat_ref, kv_ref,
    key_ref, value_ref, weight_ref, mixed_ref, linv_ref, going_ref,
    xn_ref, mask_ref, acc_ref, count_ref,
):
    j = pl.program_id(0)
    lat = lat_ref[0]

    @pl.when(j == 0)
    def _():
        gain = gain_ref[...]
        left, right = normed(left_ref[...], gain), normed(right_ref[...], gain)
        pieces = [
            normed(band_ref[...], gain), normed(cleft_ref[...], gain), normed(cright_ref[...], gain),
            left[:SIDE], right[:SIDE], left[SIDE:], right[SIDE:],
        ]
        xn_ref[...] = jnp.concatenate(pieces, axis=0).astype(BF)
        acc_ref[...] = x_ref[...].astype(F32)
        rows = jnp.where(lat == 0, tab_ref[0:1], tab_ref[1:2])
        cols, place = tab_ref[2:3], tab_ref[3:4]
        keep = jnp.where(place < 0, 1.0, 0.0)
        for i in range(HALO):
            keep = keep + jnp.where(place == i, flag_ref[lat, i].astype(F32), 0.0)
        for half in range(2):
            at = half * PAD_SIDE
            token = lax.broadcasted_iota(jnp.int32, (HALF, SPAN), 0) + half_start(lat, half)
            near = (jnp.abs(rows[:, at : at + SPAN] - token // COLS) <= HALO) & (
                jnp.abs(cols[:, at : at + SPAN] - token % COLS) <= HALO
            )
            mask_ref[half] = jnp.where(near, keep[:, at : at + SPAN], 0.0)

    xn = xn_ref[...]
    raw_k = dot(xn, wk_ref[...])
    halo_k = (raw_k * inverse_rms(raw_k)).astype(BF)
    halo_v = dot(xn, wv_ref[...]).astype(BF)
    for ref, halo, kind in ((key_ref, halo_k, 0), (value_ref, halo_v, 1)):
        ref[:PAD_SIDE] = halo[:PAD_SIDE]
        ref[PAD_SIDE : PAD_SIDE + TOKENS] = kv_ref[kind, :TOKENS]
        ref[PAD_SIDE + TOKENS : SPAN] = halo[PAD_SIDE : PAD_SIDE + 2 * SIDE]
        ref[SPAN : SPAN + BAND] = kv_ref[kind, TOKENS:]
        ref[SPAN + BAND :] = halo[PAD_SIDE + 2 * SIDE :]
    for half in range(2):
        at, start = half * PAD_SIDE, half_start(lat, half)
        scores = dot_nt(stacked(qhat_ref[pl.ds(start, HALF), :]), key_ref[at : at + SPAN])
        weights = jnp.exp(scores) * jnp.concatenate([mask_ref[half]] * QUAD_HEADS, axis=0)
        inverse = 1.0 / jnp.sum(weights, axis=-1, keepdims=True)
        low = weights.astype(BF)
        weight_ref[0, half] = low
        mixed = dot(low, value_ref[at : at + SPAN]) * inverse
        mixed_ref[pl.ds(start, HALF), :] = unstacked(mixed)
        linv_ref[pl.ds(start, HALF), :] = unstacked(jnp.broadcast_to(inverse, (STACK, QUAD)))
    acc_ref[...] += dot(mixed_ref[...].astype(BF), wo_ref[...])

    @pl.when(j == STEPS - 1)
    def _():
        going_ref[...] = jnp.zeros_like(going_ref)
        for o in range(going_ref.shape[0]):
            count_ref[o] = 0
        for s in range(TOKENS // SEG):
            owner = owner_ref[s // (COLS // SEG), s % (COLS // SEG)]
            slot = count_ref[owner]
            count_ref[owner] = slot + 1
            going_ref[owner, slot] = acc_ref[s * SEG : (s + 1) * SEG, :].astype(BF)


def backward_kernel(
    lat_ref, sharp_ref, weight_ref, key_ref, value_ref, qhat_ref, dout_ref, mixed_ref, linv_ref, rawq_ref, wq_ref,
    gqn_ref, own_ref, band_ref, left_ref, right_ref, cleft_ref, cright_ref,
    dq_ref, acc_ref,
):
    j = pl.program_id(0)
    lat = lat_ref[0]
    for half in range(2):
        at, start = half * PAD_SIDE, half_start(lat, half)
        piece = pl.ds(start, HALF)
        query = stacked(qhat_ref[piece, :])
        grad = dout_ref[piece, :].astype(F32) * linv_ref[piece, :]
        inner = grad * mixed_ref[piece, :]
        inner = jnp.concatenate(
            [jnp.sum(inner * head_mask(h, F32), axis=-1, keepdims=True) for h in range(QUAD_HEADS)], axis=0
        )
        grad = stacked(grad.astype(BF))
        keys = key_ref[at : at + SPAN]
        weights = weight_ref[0, half]
        grad_probs = dot_nt(grad, value_ref[at : at + SPAN])
        grad_scores = (weights.astype(F32) * (grad_probs - inner)).astype(BF)
        dq_ref[piece, :] = unstacked(dot(grad_scores, keys))
        if half == 0:
            acc_ref[0] = dot_tn(grad_scores, query)
            acc_ref[1] = dot_tn(weights, grad)
        else:
            used = 384
            acc_ref[0, PAD_SIDE:] += dot_tn(grad_scores[:, :used], query)[:MIDDLE]
            acc_ref[1, PAD_SIDE:] += dot_tn(weights[:, :used], grad)[:MIDDLE]
    own_ref[...] = acc_ref[:, PAD_SIDE : PAD_SIDE + TOKENS]
    at = 0
    for ref in (band_ref, cleft_ref, cright_ref):
        ref[...] = acc_ref[:, at : at + ref.shape[1]].astype(BF)
        at += ref.shape[1]
    left_ref[...] = acc_ref[:, PAD_SIDE + TOKENS : PAD_SIDE + TOKENS + SIDE].astype(BF)
    right_ref[...] = acc_ref[:, PAD_SIDE + TOKENS + SIDE :].astype(BF)
    grad_query = unit_back(rawq_ref[...], dq_ref[...] * multiplier(sharp_ref, j))
    part = dot_nt(grad_query.astype(BF), wq_ref[...])

    @pl.when(j == 0)
    def _():
        gqn_ref[...] = part

    @pl.when(j > 0)
    def _():
        gqn_ref[...] += part


def unit_back(raw, grad):
    inverse = inverse_rms(raw)
    unit = raw * inverse
    return inverse * (grad - unit * head_mean(unit * grad))


def final_kernel(
    lat_ref, x_ref, up_ref, gain_ref, unsel_ref, own_ref, band_ref, left_ref, right_ref, cleft_ref, cright_ref,
    rawk_ref, wk_ref, wv_ref, gqn_ref, out_ref, acc_ref, sum_ref,
):
    j = pl.program_id(0)
    lat = lat_ref[0]

    @pl.when(j == 0)
    def _():
        acc_ref[...] = gqn_ref[...]

    for kind in range(2):
        arrived = [ref[kind].astype(F32) for ref in (right_ref, left_ref, cright_ref, cleft_ref)]
        arrived = jnp.concatenate(arrived, axis=0).astype(BF)
        sum_ref[kind] = own_ref[kind] + dot(unsel_ref[0], arrived)
        piece = pl.ds(half_start(lat, 0), BAND)
        sum_ref[kind, piece, :] += band_ref[kind].astype(F32)
    grad_keys = unit_back(rawk_ref[...], sum_ref[0]).astype(BF)
    acc_ref[...] += dot_nt(grad_keys, wk_ref[...]) + dot_nt(sum_ref[1].astype(BF), wv_ref[...])

    @pl.when(j == STEPS - 1)
    def _():
        tokens = x_ref[...].astype(F32)
        inverse = lax.rsqrt(jnp.mean(tokens * tokens, axis=-1, keepdims=True) + 1e-05)
        grad = acc_ref[...] * gain_ref[...]
        unit = tokens * inverse
        back = inverse * (grad - unit * jnp.mean(unit * grad, axis=-1, keepdims=True))
        out_ref[...] = (up_ref[...].astype(F32) + back).astype(BF)


SMEM = functools.partial(pl.BlockSpec, memory_space=pltpu.SMEM)


def whole(*shape):
    return pl.BlockSpec(shape, lambda j, lat: (0,) * len(shape))


def by_lat(*shape):
    return pl.BlockSpec((1,) + shape, lambda j, lat: (lat[0],) + (0,) * len(shape))


def lanes(*shape, at=0):
    return pl.BlockSpec(shape + (QUAD,), lambda j, lat: (0,) * len(shape) + (at + j,))


def call(kernel, steps, in_specs, out_specs, out_shape, scratch=(), flops=0, name=None):
    return pl.pallas_call(
        kernel,
        grid_spec=pltpu.PrefetchScalarGridSpec(
            num_scalar_prefetch=1, grid=(steps,), in_specs=in_specs, out_specs=out_specs, scratch_shapes=list(scratch)
        ),
        out_shape=out_shape,
        compiler_params=pltpu.CompilerParams(vmem_limit_bytes=VMEM, dimension_semantics=("arbitrary",)),
        cost_estimate=pl.CostEstimate(flops=flops, bytes_accessed=8 << 20, transcendentals=0),
        name=name,
    )


def like(*shape, dtype=BF):
    return jax.ShapeDtypeStruct(shape, dtype)


def exchange(count, forward, backward, band, corner_forward, corner_backward):
    right = [(i, (i + 1) % count) for i in range(count)]
    left = [(b, a) for a, b in right]

    def across(pairs):
        return [(2 * a + lat, 2 * b + 1 - lat) for a, b in pairs for lat in range(2)]

    return (
        lax.ppermute(forward, "lon", right),
        lax.ppermute(backward, "lon", left),
        lax.ppermute(band, "lat", [(0, 1), (1, 0)]),
        lax.ppermute(corner_forward, ("lon", "lat"), across(right)),
        lax.ppermute(corner_backward, ("lon", "lat"), across(left)),
    )


def per_device(
    slab_features, upstream_gradient, rim_feature_rows, rim_presence_flags, feature_rescaling_coefficients,
    triple_projection_matrix, final_projection_matrix, score_sharpness, column_group_decoder_longitude,
):
    count = lax.axis_size("lon")
    cap = max(2, (2 * (TOKENS // SEG) + count - 1) // count)
    lat = lax.axis_index("lat").astype(jnp.int32).reshape(1)
    x = slab_features.reshape(TOKENS, D)
    up = upstream_gradient.reshape(TOKENS, D)
    rim = rim_feature_rows.reshape(2, BAND, D)
    gain = feature_rescaling_coefficients.reshape(1, D)
    w3, wo = triple_projection_matrix, final_projection_matrix
    table = selection_table()
    selection = jnp.asarray(table, BF)
    edge = SIDE + CORNER
    places = np.concatenate([table[:, :SIDE], table[:, edge : edge + SIDE], table[:, 2 * edge :]], axis=1)
    unselection = jnp.asarray(places[:, :, :TOKENS].transpose(0, 2, 1), BF)

    packed = call(
        pack_kernel, 1,
        [whole(TOKENS, D), by_lat(BAND, D), by_lat(*table.shape[1:])],
        [whole(edge, D), whole(edge, D), whole(BAND, D), whole(CORNER, D), whole(CORNER, D)],
        [like(edge, D), like(edge, D), like(BAND, D), like(CORNER, D), like(CORNER, D)],
        name="edge_tokens",
    )(lat, x, rim, selection)
    halo_left, halo_right, halo_band, corner_left, corner_right = exchange(count, *packed)

    qhat, rawq, rawk, kv, dout = call(
        own_kernel, STEPS,
        [SMEM(), whole(TOKENS, D), by_lat(BAND, D), whole(TOKENS, D), whole(1, D),
         lanes(D), lanes(D, at=STEPS), lanes(D, at=2 * STEPS), pl.BlockSpec((QUAD, D), lambda j, lat: (j, 0))],
        [lanes(TOKENS), lanes(TOKENS), lanes(TOKENS), lanes(2, TOKENS + BAND), lanes(TOKENS)],
        [like(TOKENS, D), like(TOKENS, D, dtype=F32), like(TOKENS, D, dtype=F32), like(2, TOKENS + BAND, D), like(TOKENS, D)],
        [pltpu.VMEM((TOKENS + BAND, D), BF)],
        flops=2 * 1024 * 1024 * (192 * 2 + 288 * 2),
        name="own_projections",
    )(lat, score_sharpness, x, rim, up, gain, w3, w3, w3, wo)

    keys, values, weights, mixed, linv, going = call(
        forward_kernel, STEPS,
        [SMEM(), SMEM(), whole(TOKENS, D), whole(BAND, D), whole(edge, D), whole(edge, D), whole(CORNER, D), whole(CORNER, D),
         whole(1, D), whole(8, KEYS), lanes(D, at=STEPS), lanes(D, at=2 * STEPS),
         pl.BlockSpec((QUAD, D), lambda j, lat: (j, 0)), lanes(TOKENS), lanes(2, TOKENS + BAND)],
        [lanes(KEYS), lanes(KEYS), pl.BlockSpec((1, 2, STACK, SPAN), lambda j, lat: (j, 0, 0, 0)), lanes(TOKENS), lanes(TOKENS),
         whole(count, cap, SEG, D)],
        [like(KEYS, D), like(KEYS, D), like(STEPS, 2, STACK, SPAN), like(TOKENS, D, dtype=F32), like(TOKENS, D, dtype=F32),
         like(count, cap, SEG, D)],
        [pltpu.VMEM((HALO_ROWS, D), BF), pltpu.VMEM((2, HALF, SPAN), F32), pltpu.VMEM((TOKENS, D), F32),
         pltpu.SMEM((count,), jnp.int32)],
        flops=2 * 1024 * 1024 * 2000,
        name="attention_forward",
    )(lat, column_group_decoder_longitude, rim_presence_flags, x, halo_band, halo_left, halo_right, corner_left, corner_right,
      gain, jnp.asarray(key_table()), w3, w3, wo, qhat, kv)

    arrived = lax.all_to_all(going, "lon", split_axis=0, concat_axis=0, tiled=True)

    gqn, own, band, left, right, cleft, cright = call(
        backward_kernel, STEPS,
        [SMEM(), pl.BlockSpec((1, 2, STACK, SPAN), lambda j, lat: (j, 0, 0, 0)), lanes(KEYS), lanes(KEYS)]
        + [lanes(TOKENS)] * 5 + [lanes(D)],
        [whole(TOKENS, D), lanes(2, TOKENS), lanes(2, BAND), lanes(2, SIDE), lanes(2, SIDE), lanes(2, CORNER), lanes(2, CORNER)],
        [like(TOKENS, D, dtype=F32), like(2, TOKENS, D, dtype=F32), like(2, BAND, D), like(2, SIDE, D), like(2, SIDE, D),
         like(2, CORNER, D), like(2, CORNER, D)],
        [pltpu.VMEM((TOKENS, QUAD), F32), pltpu.VMEM((2, SPAN, QUAD), F32)],
        flops=2 * 1024 * 1024 * 2000,
        name="attention_backward",
    )(lat, score_sharpness, weights, keys, values, qhat, dout, mixed, linv, rawq, w3)
    from_left, from_right, from_band, from_cleft, from_cright = exchange(count, right, left, band, cright, cleft)

    input_grad = call(
        final_kernel, STEPS,
        [whole(TOKENS, D), whole(TOKENS, D), whole(1, D), by_lat(*unselection.shape[1:]), lanes(2, TOKENS), lanes(2, BAND),
         lanes(2, SIDE), lanes(2, SIDE), lanes(2, CORNER), lanes(2, CORNER), lanes(TOKENS), lanes(D, at=STEPS),
         lanes(D, at=2 * STEPS), whole(TOKENS, D)],
        whole(TOKENS, D),
        like(TOKENS, D),
        [pltpu.VMEM((TOKENS, D), F32), pltpu.VMEM((2, TOKENS, QUAD), F32)],
        flops=2 * 1024 * 1024 * 400,
        name="input_gradient",
    )(lat, x, up, gain, unselection, own, from_band, from_left, from_right, from_cleft, from_cright, rawk, w3, w3, gqn)
    return (
        arrived.reshape(1, 1, count, cap, SEG, D),
        input_grad.reshape(ROWS, COLS, D),
    )


def solution(mesh):
    return jax.shard_map(
        per_device,
        mesh=mesh,
        in_specs=(
            P("lat", "lon", None),
            P("lat", "lon", None),
            P(None, None, "lon", None),
            P(),
            P(),
            P(),
            P(),
            P(),
            P("lat", "lon"),
        ),
        out_specs=(P("lat", "lon", None, None, None, None), P("lat", "lon", None)),
        check_vma=False,
    )
```

```python
import functools

import jax
import jax.numpy as jnp
import numpy as np
from jax import lax
from jax.experimental import pallas as pl
from jax.experimental.pallas import tpu as pltpu
from jax.sharding import PartitionSpec as P

HEADS = 16
HALO = 6
ROWS = 12
COLS = 16
SEG = 4
D = 1024
HEAD_DIM = D // HEADS
TOKENS = ROWS * COLS
HALF = TOKENS // 2
BAND = HALO * COLS
SIDE = ROWS * HALO
CORNER = 40
QUAD = 256
QUAD_HEADS = QUAD // HEAD_DIM
STEPS = D // QUAD
STACK = QUAD_HEADS * HALF
PAD_SIDE = BAND + 2 * CORNER
MIDDLE = TOKENS + 2 * SIDE
SPAN = PAD_SIDE + MIDDLE
KEYS = SPAN + PAD_SIDE
QUERIES = SPAN
HALO_ROWS = 2 * PAD_SIDE + 2 * SIDE - BAND
HALO_QUERIES = PAD_SIDE + 2 * SIDE
EDGE = SIDE + CORNER
STATS = 128
VMEM = 62 * 1024 * 1024
BF = jnp.bfloat16
F32 = jnp.float32


def dot(a, b):
    return jnp.dot(a, b, preferred_element_type=F32)


def dot_nt(a, b):
    return lax.dot_general(a, b, (((1,), (1,)), ((), ())), preferred_element_type=F32)


def dot_tn(a, b):
    return lax.dot_general(a, b, (((0,), (0,)), ((), ())), preferred_element_type=F32)


def first_column(side, parity):
    return COLS - HALO if side == parity else 0


def selection_table():
    table = np.zeros((4, 2 * EDGE + 2 * CORNER, TOKENS + BAND), np.float32)
    for lat in range(2):
        for parity in range(2):
            for side in range(2):
                first, base = first_column(side, parity), side * EDGE
                picks = table[2 * lat + parity]
                for c in range(HALO):
                    for r in range(ROWS):
                        picks[base + r * HALO + c, r * COLS + first + c] = 1
                    for i in range(HALO):
                        picks[base + SIDE + i * HALO + c, TOKENS + i * COLS + first + c] = 1
                        row = i + HALO * (1 - lat)
                        picks[2 * EDGE + side * CORNER + i * HALO + c, row * COLS + first + c] = 1
    return table


def key_table():
    table = np.full((4, 8, KEYS), 1000, np.int32)
    table[:, 2] = -1
    for lat in range(2):
        for parity in range(2):
            picks = table[2 * lat + parity]
            low = {"lat": ROWS if lat == 0 else -HALO, "own": 0, "rim": -HALO if lat == 0 else ROWS}

            def put(at, count, width, first_col, kind):
                for k in range(count * width):
                    i, c = divmod(k, width)
                    picks[0, at + k] = low[kind] + i
                    picks[1, at + k] = first_col + c
                    if kind == "rim":
                        picks[2, at + k] = i

            put(0, HALO, COLS, 0, "lat")
            put(PAD_SIDE, ROWS, COLS, 0, "own")
            put(SPAN, HALO, COLS, 0, "rim")
            for side in range(2):
                col = COLS if side == parity else -HALO
                put(BAND + side * CORNER, HALO, HALO, col, "lat")
                put(PAD_SIDE + TOKENS + side * SIDE, ROWS, HALO, col, "own")
                put(SPAN + BAND + side * CORNER, HALO, HALO, col, "rim")
    return table


def head_mask(h, dtype):
    lane = lax.broadcasted_iota(jnp.int32, (1, QUAD), 1)
    return jnp.where(lane // HEAD_DIM == h, 1.0, 0.0).astype(dtype)


def head_mean(values):
    a = lax.broadcasted_iota(jnp.int32, (QUAD, QUAD), 0) // HEAD_DIM
    b = lax.broadcasted_iota(jnp.int32, (QUAD, QUAD), 1) // HEAD_DIM
    block = jnp.where(a == b, 1.0 / HEAD_DIM, 0.0).astype(BF)
    return dot(values.astype(BF), block)


def unit(raw):
    return raw * lax.rsqrt(head_mean(raw * raw) + 1e-06)


def unit_back(raw, grad):
    inverse = lax.rsqrt(head_mean(raw * raw) + 1e-06)
    value = raw * inverse
    return inverse * (grad - value * head_mean(value * grad))


def normed(tokens, gain):
    tokens = tokens.astype(F32)
    return tokens * lax.rsqrt(jnp.mean(tokens * tokens, axis=-1, keepdims=True) + 1e-05) * gain


def multiplier(sharp_ref, j):
    out = jnp.zeros((1, QUAD), F32)
    for h in range(QUAD_HEADS):
        out = out + head_mask(h, F32) * (sharp_ref[j * QUAD_HEADS + h] / HEAD_DIM)
    return out


def stacked(block):
    return jnp.concatenate([block * head_mask(h, BF) for h in range(QUAD_HEADS)], axis=0)


def unstacked(stack):
    out = stack[:HALF] * head_mask(0, F32)
    for h in range(1, QUAD_HEADS):
        out = out + stack[h * HALF : (h + 1) * HALF] * head_mask(h, F32)
    return out


def repeated(block):
    return jnp.concatenate([block] * QUAD_HEADS, axis=0)


def stat_lane(lane):
    return jnp.where(lax.broadcasted_iota(jnp.int32, (1, STATS), 1) == lane, 1.0, 0.0)


def half_start(lat, half):
    return pl.multiple_of(HALF * ((1 - lat) if half == 0 else lat), 16)


def near_mask(mask_ref, tab_ref, flag_ref, lat):
    rows, cols, place = tab_ref[0, 0:1], tab_ref[0, 1:2], tab_ref[0, 2:3]
    keep = jnp.where(place < 0, 1.0, 0.0)
    for i in range(HALO):
        keep = keep + jnp.where(place == i, flag_ref[lat, i].astype(F32), 0.0)
    for half in range(2):
        at = half * PAD_SIDE
        token = lax.broadcasted_iota(jnp.int32, (HALF, SPAN), 0) + half_start(lat, half)
        near = (jnp.abs(rows[:, at : at + SPAN] - token // COLS) <= HALO) & (
            jnp.abs(cols[:, at : at + SPAN] - token % COLS) <= HALO
        )
        mask_ref[half] = jnp.where(near, keep[:, at : at + SPAN], 0.0)


def lay_keys(ref, own, halo):
    ref[:PAD_SIDE] = halo[:PAD_SIDE]
    ref[PAD_SIDE : PAD_SIDE + TOKENS] = own[:TOKENS]
    ref[PAD_SIDE + TOKENS : SPAN] = halo[PAD_SIDE:HALO_QUERIES]
    ref[SPAN : SPAN + BAND] = own[TOKENS:]
    ref[SPAN + BAND :] = halo[HALO_QUERIES:]


class Copies:
    def __init__(self, sems):
        self.sems, self.used = sems, 0

    def start(self, source, target):
        copy = pltpu.make_async_copy(source, target, self.sems.at[self.used])
        self.used += 1
        copy.start()
        return copy

    def start_steps(self, pair):
        base = self.used
        self.used += STEPS
        for j in range(STEPS):
            pltpu.make_async_copy(*pair(j), self.sems.at[base + j]).start()
        return lambda j: pltpu.make_async_copy(*pair(j), self.sems.at[base + j]).wait()


def lane_block(at, j):
    return pl.ds(pl.multiple_of((at + j) * QUAD, QUAD), QUAD)


def pack_kernel(
    place_ref, x_hbm, up_hbm, rim_hbm, sel_hbm, edge_a_hbm, edge_b_hbm, band_hbm, corner_a_hbm, corner_b_hbm,
    x_ref, up_ref, rim_ref, sel_ref, edge_a_ref, edge_b_ref, corner_a_ref, corner_b_ref, sems,
):
    lat = place_ref[0]
    copies = Copies(sems)
    loads = [
        copies.start(x_hbm, x_ref),
        copies.start(rim_hbm.at[lat], rim_ref),
        copies.start(sel_hbm.at[2 * lat + place_ref[1]], sel_ref),
        copies.start(up_hbm, up_ref),
    ]
    for copy in loads:
        copy.wait()
    piece = pl.ds(half_start(lat, 0), BAND)
    stores = [
        copies.start(x_ref.at[piece], band_hbm.at[pl.ds(0, BAND)]),
        copies.start(up_ref.at[piece], band_hbm.at[pl.ds(BAND, BAND)]),
    ]
    picks = sel_ref[...]
    features = dot(picks, jnp.concatenate([x_ref[...], rim_ref[...]], axis=0))
    grads = dot(picks[:, :TOKENS], up_ref[...])
    for side, (ref, hbm) in enumerate(((edge_a_ref, edge_a_hbm), (edge_b_ref, edge_b_hbm))):
        at = side * EDGE
        ref[...] = jnp.concatenate([features[at : at + EDGE], grads[at : at + SIDE]], axis=0).astype(BF)
        stores.append(copies.start(ref, hbm))
    for side, (ref, hbm) in enumerate(((corner_a_ref, corner_a_hbm), (corner_b_ref, corner_b_hbm))):
        at = 2 * EDGE + side * CORNER
        ref[...] = jnp.concatenate([features[at : at + CORNER], grads[at : at + CORNER]], axis=0).astype(BF)
        stores.append(copies.start(ref, hbm))
    for copy in stores:
        copy.wait()


def own_kernel(
    place_ref, sharp_ref, x_ref, rim_ref, up_ref, gain_ref, wq_ref, wk_ref, wv_ref, wo_ref,
    qhat_ref, rawq_ref, rawk_ref, kv_ref, dout_ref, xn_ref,
):
    j = pl.program_id(0)

    @pl.when(j == 0)
    def _():
        xn_ref[:TOKENS] = normed(x_ref[...], gain_ref[...]).astype(BF)
        xn_ref[TOKENS:] = normed(rim_ref[0], gain_ref[...]).astype(BF)

    xn = xn_ref[...]
    raw_q = dot(xn[:TOKENS], wq_ref[...])
    rawq_ref[0] = raw_q
    qhat_ref[0] = (unit(raw_q) * multiplier(sharp_ref, j)).astype(BF)
    raw_k = dot(xn, wk_ref[...])
    rawk_ref[0] = raw_k[:TOKENS]
    kv_ref[0, 0] = unit(raw_k).astype(BF)
    kv_ref[0, 1] = dot(xn, wv_ref[...]).astype(BF)
    dout_ref[0] = dot_nt(up_ref[...], wo_ref[...]).astype(BF)


def forward_kernel(
    place_ref, flag_ref, band_hbm, edge_a_hbm, edge_b_hbm, corner_a_hbm, corner_b_hbm, gain_hbm, tab_hbm, sel_hbm, w3_hbm,
    qhat_hbm, kv_hbm, dout_hbm,
    halo_hbm, mixed_hbm, stat_hbm, stat_a_hbm, stat_b_hbm, stat_band_hbm, stat_ca_hbm, stat_cb_hbm,
    band_ref, edge_a_ref, edge_b_ref, corner_a_ref, corner_b_ref, gain_ref, tab_ref, sel_ref, wk_ref, wv_ref,
    qhat_ref, kv_ref, dout_ref, halo_ref, mixed_ref, stat_ref, picked_ref, xn_ref, mask_ref, key_ref, value_ref, sems,
):
    lat = place_ref[0]
    spot = 2 * lat + place_ref[1]
    copies = Copies(sems)
    first = [
        copies.start(gain_hbm, gain_ref),
        copies.start(band_hbm.at[pl.ds(0, BAND)], band_ref),
        copies.start(corner_a_hbm, corner_a_ref),
        copies.start(corner_b_hbm, corner_b_ref),
        copies.start(edge_a_hbm.at[pl.ds(0, EDGE)], edge_a_ref),
        copies.start(edge_b_hbm.at[pl.ds(0, EDGE)], edge_b_ref),
        copies.start(tab_hbm.at[spot], tab_ref.at[0]),
    ]
    weight_copies = lambda j: [
        (w3_hbm.at[:, lane_block(STEPS, j)], wk_ref.at[j], 2 * j),
        (w3_hbm.at[:, lane_block(2 * STEPS, j)], wv_ref.at[j], 2 * j + 1),
    ]
    at_weights = copies.used
    copies.used += 2 * STEPS

    def start_weights(j):
        for source, target, k in weight_copies(j):
            pltpu.make_async_copy(source, target, sems.at[at_weights + k]).start()

    start_weights(0)
    second = [copies.start(qhat_hbm, qhat_ref), copies.start(kv_hbm, kv_ref), copies.start(dout_hbm, dout_ref)]
    for j in range(1, STEPS):
        start_weights(j)
    third = copies.start(sel_hbm.at[spot], sel_ref)
    for copy in first:
        copy.wait()
    gain = gain_ref[...]
    edge_a, edge_b = normed(edge_a_ref[...], gain), normed(edge_b_ref[...], gain)
    pieces = [normed(band_ref[...], gain), normed(corner_a_ref[...], gain)[:CORNER], normed(corner_b_ref[...], gain)[:CORNER]]
    pieces += [edge_a[:SIDE], edge_b[:SIDE], edge_a[SIDE:], edge_b[SIDE:]]
    xn_ref[...] = jnp.concatenate(pieces, axis=0).astype(BF)
    stat_ref[...] = jnp.zeros_like(stat_ref)
    near_mask(mask_ref, tab_ref, flag_ref, lat)
    base = copies.used

    def store_halo(j):
        return pltpu.make_async_copy(halo_ref.at[j], halo_hbm.at[j], sems.at[base + j])

    def store_mixed(j):
        return pltpu.make_async_copy(mixed_ref.at[j], mixed_hbm.at[:, lane_block(0, j)], sems.at[base + STEPS + j])

    def step(j, carry):
        for source, target, k in weight_copies(j):
            pltpu.make_async_copy(source, target, sems.at[at_weights + k]).wait()
        xn = xn_ref[...]
        halo_k = unit(dot(xn, wk_ref[j])).astype(BF)
        halo_v = dot(xn, wv_ref[j]).astype(BF)
        halo_ref[j, 0] = halo_k
        halo_ref[j, 1] = halo_v
        store_halo(j).start()

        @pl.when(j == 0)
        def _():
            for copy in second:
                copy.wait()

        lay_keys(key_ref, kv_ref[j, 0], halo_k)
        lay_keys(value_ref, kv_ref[j, 1], halo_v)
        for half in range(2):
            at, piece = half * PAD_SIDE, pl.ds(half_start(lat, half), HALF)
            scores = dot_nt(stacked(qhat_ref[j, piece, :]), key_ref[at : at + SPAN])
            weights = jnp.exp(scores) * repeated(mask_ref[half])
            inverse = 1.0 / jnp.sum(weights, axis=-1, keepdims=True)
            mixed = unstacked(dot(weights.astype(BF), value_ref[at : at + SPAN]) * inverse)
            mixed_ref[j, piece, :] = mixed.astype(BF)
            inner = dout_ref[j, piece, :].astype(F32) * mixed
            stat = stat_ref[piece, :]
            for h in range(QUAD_HEADS):
                head = j * QUAD_HEADS + h
                stat = stat + stat_lane(head) * inverse[h * HALF : (h + 1) * HALF]
                stat = stat + stat_lane(HEADS + head) * jnp.sum(inner * head_mask(h, F32), axis=-1, keepdims=True)
            stat_ref[piece, :] = stat
        store_mixed(j).start()
        return carry

    lax.fori_loop(0, STEPS, step, 0)
    copies.used = base + 2 * STEPS
    third.wait()
    stat = stat_ref[...]
    high = stat.astype(BF)
    low = (stat - high.astype(F32)).astype(BF)
    picks = sel_ref[:, :TOKENS]
    picked_ref[...] = dot(picks, high) + dot(picks, low)
    last = [
        copies.start(stat_ref, stat_hbm),
        copies.start(picked_ref.at[pl.ds(0, SIDE)], stat_a_hbm),
        copies.start(picked_ref.at[pl.ds(EDGE, SIDE)], stat_b_hbm),
        copies.start(stat_ref.at[pl.ds(half_start(lat, 0), BAND)], stat_band_hbm),
        copies.start(picked_ref.at[pl.ds(2 * EDGE, CORNER)], stat_ca_hbm),
        copies.start(picked_ref.at[pl.ds(2 * EDGE + CORNER, CORNER)], stat_cb_hbm),
    ]
    for j in range(STEPS):
        store_halo(j).wait()
        store_mixed(j).wait()
    for copy in last:
        copy.wait()


def output_kernel(place_ref, owner_ref, x_ref, mixed_ref, wo_ref, going_ref, acc_ref, count_ref):
    acc_ref[...] = x_ref[...].astype(F32) + dot(mixed_ref[...], wo_ref[...])
    going_ref[...] = jnp.zeros_like(going_ref)
    for o in range(going_ref.shape[0]):
        count_ref[o] = 0
    for s in range(TOKENS // SEG):
        owner = owner_ref[s // (COLS // SEG), s % (COLS // SEG)]
        slot = count_ref[owner]
        count_ref[owner] = slot + 1
        going_ref[owner, slot] = acc_ref[s * SEG : (s + 1) * SEG, :].astype(BF)


def backward_kernel(
    place_ref, sharp_ref, flag_ref, x_ref, up_ref, band_ref, edge_a_ref, edge_b_ref, corner_a_ref, corner_b_ref, gain_ref,
    tab_ref, wq_ref, wk_ref, wv_ref, wo_ref, qhat_ref, kv_ref, halo_ref, dout_ref, rawq_ref, rawk_ref,
    stat_ref, stat_a_ref, stat_b_ref, stat_band_ref, stat_ca_ref, stat_cb_ref,
    out_ref,
    xn_ref, upn_ref, mask_ref, acc_ref, key_ref, value_ref, query_ref, grad_ref, row_ref, dq_ref, dk_ref, dv_ref,
):
    j = pl.program_id(0)
    lat = place_ref[0]

    @pl.when(j == 0)
    def _():
        gain = gain_ref[...]
        band, edge_a, edge_b = (ref[...].astype(F32) for ref in (band_ref, edge_a_ref, edge_b_ref))
        corner_a, corner_b = (ref[...].astype(F32) for ref in (corner_a_ref, corner_b_ref))
        pieces = [band[:BAND], corner_a[:CORNER], corner_b[:CORNER], edge_a[:SIDE], edge_b[:SIDE]]
        xn_ref[...] = normed(jnp.concatenate(pieces, axis=0), gain).astype(BF)
        pieces = [band[BAND:], corner_a[CORNER:], corner_b[CORNER:], edge_a[EDGE:], edge_b[EDGE:]]
        upn_ref[...] = jnp.concatenate(pieces, axis=0).astype(BF)
        pieces = [stat_band_ref, stat_ca_ref, stat_cb_ref, stat_ref, stat_a_ref, stat_b_ref]
        row_ref[...] = jnp.concatenate([ref[...] for ref in pieces], axis=0).T
        near_mask(mask_ref, tab_ref, flag_ref, lat)

    lay_keys(key_ref, kv_ref[0, 0], halo_ref[0, 0])
    lay_keys(value_ref, kv_ref[0, 1], halo_ref[0, 1])
    halo_q = (unit(dot(xn_ref[...], wq_ref[...])) * multiplier(sharp_ref, j)).astype(BF)
    halo_g = dot_nt(upn_ref[...], wo_ref[...]).astype(BF)
    for ref, own, halo in ((query_ref, qhat_ref, halo_q), (grad_ref, dout_ref, halo_g)):
        ref[:PAD_SIDE] = halo[:PAD_SIDE]
        ref[PAD_SIDE : PAD_SIDE + TOKENS] = own[0]
        ref[PAD_SIDE + TOKENS :] = halo[PAD_SIDE:]

    for half in range(2):
        at, piece = half * PAD_SIDE, pl.ds(half_start(lat, half), HALF)
        stat = stat_ref[piece, :]
        columns = [
            jnp.concatenate(
                [jnp.sum(stat * stat_lane(base + j * QUAD_HEADS + h), axis=-1, keepdims=True) for h in range(QUAD_HEADS)],
                axis=0,
            )
            for base in (0, HEADS)
        ]
        keys = key_ref[at : at + SPAN]
        scores = dot_nt(stacked(qhat_ref[0, piece, :]), keys)
        probs = jnp.exp(scores) * repeated(mask_ref[half]) * columns[0]
        grad_probs = dot_nt(stacked(dout_ref[0, piece, :]), value_ref[at : at + SPAN])
        grad_scores = probs * (grad_probs - columns[1])
        dq_ref[piece, :] = unstacked(dot(grad_scores.astype(BF), keys))

    for half in range(2):
        at, piece = half * PAD_SIDE, pl.ds(half_start(lat, half), HALF)
        width = SPAN - at
        queries, grads = query_ref[at:], grad_ref[at:]
        rows = [
            jnp.concatenate(
                [
                    jnp.broadcast_to(row_ref[pl.ds(base + j * QUAD_HEADS + h, 1), at:], (HALF, width))
                    for h in range(QUAD_HEADS)
                ],
                axis=0,
            )
            for base in (0, HEADS)
        ]
        scores = dot_nt(stacked(kv_ref[0, 0, piece, :]), queries)
        probs = jnp.exp(scores) * repeated(mask_ref[half, :, :width]) * rows[0]
        grad_probs = dot_nt(stacked(kv_ref[0, 1, piece, :]), grads)
        grad_scores = probs * (grad_probs - rows[1])
        dk_ref[piece, :] = unstacked(dot(grad_scores.astype(BF), queries))
        dv_ref[piece, :] = unstacked(dot(probs.astype(BF), grads))

    grad_q = unit_back(rawq_ref[0], dq_ref[...] * multiplier(sharp_ref, j)).astype(BF)
    grad_k = unit_back(rawk_ref[0], dk_ref[...]).astype(BF)
    part = dot_nt(grad_q, wq_ref[...]) + dot_nt(grad_k, wk_ref[...]) + dot_nt(dv_ref[...].astype(BF), wv_ref[...])

    @pl.when(j == 0)
    def _():
        acc_ref[...] = part

    @pl.when(j > 0)
    def _():
        acc_ref[...] += part

    @pl.when(j == STEPS - 1)
    def _():
        tokens = x_ref[...].astype(F32)
        inverse = lax.rsqrt(jnp.mean(tokens * tokens, axis=-1, keepdims=True) + 1e-05)
        grad = acc_ref[...] * gain_ref[...]
        value = tokens * inverse
        back = inverse * (grad - value * jnp.mean(value * grad, axis=-1, keepdims=True))
        out_ref[...] = (up_ref[...].astype(F32) + back).astype(BF)


SMEM = functools.partial(pl.BlockSpec, memory_space=pltpu.SMEM)
HBM = functools.partial(pl.BlockSpec, memory_space=pl.ANY)


def whole(*shape):
    return pl.BlockSpec(shape, lambda j, place: (0,) * len(shape))


def by_lat(*shape):
    return pl.BlockSpec((1,) + shape, lambda j, place: (place[0],) + (0,) * len(shape))


def by_place(*shape):
    return pl.BlockSpec((1,) + shape, lambda j, place: (2 * place[0] + place[1],) + (0,) * len(shape))


def lanes(*shape, at=0):
    return pl.BlockSpec(shape + (QUAD,), lambda j, place: (0,) * len(shape) + (at + j,))


def rows_of(width):
    return pl.BlockSpec((QUAD, width), lambda j, place: (j, 0))


def steps_of(*shape):
    return pl.BlockSpec((1,) + shape + (QUAD,), lambda j, place: (j,) + (0,) * (len(shape) + 1))


def call(kernel, steps, in_specs, out_specs, out_shape, scratch=(), flops=0, name=None):
    return pl.pallas_call(
        kernel,
        grid_spec=pltpu.PrefetchScalarGridSpec(
            num_scalar_prefetch=1, grid=(steps,), in_specs=in_specs, out_specs=out_specs, scratch_shapes=list(scratch)
        ),
        out_shape=out_shape,
        compiler_params=pltpu.CompilerParams(vmem_limit_bytes=VMEM, dimension_semantics=("arbitrary",)),
        cost_estimate=pl.CostEstimate(flops=flops, bytes_accessed=8 << 20, transcendentals=0),
        name=name,
    )


def like(*shape, dtype=BF):
    return jax.ShapeDtypeStruct(shape, dtype)


def exchange(count, edge_a, edge_b, band, corner_a, corner_b):
    pairs_a = [(i, i + 1 - 2 * (i % 2)) for i in range(count)]
    pairs_b = [(i, (i - 1 + 2 * (i % 2)) % count) for i in range(count)]

    def across(pairs):
        return [(2 * a + lat, 2 * b + 1 - lat) for a, b in pairs for lat in range(2)]

    return (
        lax.ppermute(edge_a, "lon", pairs_a),
        lax.ppermute(edge_b, "lon", pairs_b),
        lax.ppermute(band, "lat", [(0, 1), (1, 0)]),
        lax.ppermute(corner_a, ("lon", "lat"), across(pairs_a)),
        lax.ppermute(corner_b, ("lon", "lat"), across(pairs_b)),
    )


def per_device(
    slab_features, upstream_gradient, rim_feature_rows, rim_presence_flags, feature_rescaling_coefficients,
    triple_projection_matrix, final_projection_matrix, score_sharpness, column_group_decoder_longitude,
):
    count = lax.axis_size("lon")
    cap = max(2, (2 * (TOKENS // SEG) + count - 1) // count)
    place = jnp.stack([lax.axis_index("lat"), lax.axis_index("lon") % 2]).astype(jnp.int32)
    x = slab_features.reshape(TOKENS, D)
    up = upstream_gradient.reshape(TOKENS, D)
    rim = rim_feature_rows.reshape(2, BAND, D)
    gain = feature_rescaling_coefficients.reshape(1, D)
    w3, wo = triple_projection_matrix, final_projection_matrix
    table = selection_table()
    selection = jnp.asarray(table, BF)
    keys = jnp.asarray(key_table())
    flags = rim_presence_flags

    sizes = (EDGE + SIDE, EDGE + SIDE, 2 * BAND, 2 * CORNER, 2 * CORNER)
    packed = call(
        pack_kernel, 1, [HBM()] * 4, [HBM()] * 5,
        [like(size, D) for size in sizes],
        [pltpu.VMEM((TOKENS, D), BF), pltpu.VMEM((TOKENS, D), BF), pltpu.VMEM((BAND, D), BF), pltpu.VMEM(table.shape[1:], BF)]
        + [pltpu.VMEM((size, D), BF) for size in sizes if size != 2 * BAND] + [pltpu.SemaphoreType.DMA((10,))],
        name="edge_tokens",
    )(place, x, up, rim, selection)
    edge_a, edge_b, band, corner_a, corner_b = exchange(count, *packed)

    qhat, rawq, rawk, kv, dout = call(
        own_kernel, STEPS,
        [SMEM(), whole(TOKENS, D), by_lat(BAND, D), whole(TOKENS, D), whole(1, D),
         lanes(D), lanes(D, at=STEPS), lanes(D, at=2 * STEPS), rows_of(D)],
        [steps_of(TOKENS), steps_of(TOKENS), steps_of(TOKENS), steps_of(2, TOKENS + BAND), steps_of(TOKENS)],
        [like(STEPS, TOKENS, QUAD), like(STEPS, TOKENS, QUAD, dtype=F32), like(STEPS, TOKENS, QUAD, dtype=F32),
         like(STEPS, 2, TOKENS + BAND, QUAD), like(STEPS, TOKENS, QUAD)],
        [pltpu.VMEM((TOKENS + BAND, D), BF)],
        flops=2 * 1024 * 1024 * (192 * 2 + 288 * 2),
        name="own_projections",
    )(place, score_sharpness, x, rim, up, gain, w3, w3, w3, wo)

    stat_sizes = (TOKENS, SIDE, SIDE, BAND, CORNER, CORNER)
    halo_kv, mixed, stat, *edges = call(
        forward_kernel, 1,
        [SMEM()] + [HBM()] * 12, [HBM()] * 8,
        [like(STEPS, 2, HALO_ROWS, QUAD), like(TOKENS, D)] + [like(size, STATS, dtype=F32) for size in stat_sizes],
        [pltpu.VMEM((BAND, D), BF), pltpu.VMEM((EDGE, D), BF), pltpu.VMEM((EDGE, D), BF), pltpu.VMEM((2 * CORNER, D), BF),
         pltpu.VMEM((2 * CORNER, D), BF), pltpu.VMEM((1, D), F32), pltpu.VMEM((1, 8, KEYS), jnp.int32),
         pltpu.VMEM(table.shape[1:], BF), pltpu.VMEM((STEPS, D, QUAD), BF), pltpu.VMEM((STEPS, D, QUAD), BF),
         pltpu.VMEM((STEPS, TOKENS, QUAD), BF), pltpu.VMEM((STEPS, 2, TOKENS + BAND, QUAD), BF),
         pltpu.VMEM((STEPS, TOKENS, QUAD), BF), pltpu.VMEM((STEPS, 2, HALO_ROWS, QUAD), BF),
         pltpu.VMEM((STEPS, TOKENS, QUAD), BF), pltpu.VMEM((TOKENS, STATS), F32), pltpu.VMEM((table.shape[1], STATS), F32),
         pltpu.VMEM((HALO_ROWS, D), BF), pltpu.VMEM((2, HALF, SPAN), F32), pltpu.VMEM((KEYS, QUAD), BF),
         pltpu.VMEM((KEYS, QUAD), BF), pltpu.SemaphoreType.DMA((33,))],
        flops=2 * 1024 * 1024 * 2000,
        name="attention_forward",
    )(place, flags, band, edge_a, edge_b, corner_a, corner_b, gain, keys, selection, w3, qhat, kv, dout)
    stat_a, stat_b, stat_band, stat_ca, stat_cb = exchange(count, *edges)

    going = call(
        output_kernel, 1,
        [SMEM(), whole(TOKENS, D), whole(TOKENS, D), whole(D, D)], whole(count, cap, SEG, D), like(count, cap, SEG, D),
        [pltpu.VMEM((TOKENS, D), F32), pltpu.SMEM((count,), jnp.int32)],
        flops=2 * 1024 * 1024 * 200,
        name="output_segments",
    )(place, column_group_decoder_longitude, x, mixed, wo)
    going, stat_a, stat_b, stat_band, stat_ca, stat_cb = lax.optimization_barrier(
        (going, stat_a, stat_b, stat_band, stat_ca, stat_cb)
    )
    arrived = lax.all_to_all(going, "lon", split_axis=0, concat_axis=0, tiled=True)

    input_grad = call(
        backward_kernel, STEPS,
        [SMEM(), SMEM(), whole(TOKENS, D), whole(TOKENS, D), whole(2 * BAND, D), whole(EDGE + SIDE, D), whole(EDGE + SIDE, D),
         whole(2 * CORNER, D), whole(2 * CORNER, D), whole(1, D), by_place(8, KEYS), lanes(D), lanes(D, at=STEPS),
         lanes(D, at=2 * STEPS), rows_of(D), steps_of(TOKENS), steps_of(2, TOKENS + BAND), steps_of(2, HALO_ROWS),
         steps_of(TOKENS), steps_of(TOKENS), steps_of(TOKENS)] + [whole(size, STATS) for size in stat_sizes],
        whole(TOKENS, D),
        like(TOKENS, D),
        [pltpu.VMEM((HALO_QUERIES, D), BF), pltpu.VMEM((HALO_QUERIES, D), BF), pltpu.VMEM((2, HALF, SPAN), F32),
         pltpu.VMEM((TOKENS, D), F32), pltpu.VMEM((KEYS, QUAD), BF), pltpu.VMEM((KEYS, QUAD), BF),
         pltpu.VMEM((QUERIES, QUAD), BF), pltpu.VMEM((QUERIES, QUAD), BF), pltpu.VMEM((STATS, QUERIES), F32),
         pltpu.VMEM((TOKENS, QUAD), F32), pltpu.VMEM((TOKENS, QUAD), F32), pltpu.VMEM((TOKENS, QUAD), F32)],
        flops=2 * 1024 * 1024 * 4000,
        name="attention_backward",
    )(place, score_sharpness, flags, x, up, band, edge_a, edge_b, corner_a, corner_b, gain, keys, w3, w3, w3, wo,
      qhat, kv, halo_kv, dout, rawq, rawk, stat, stat_a, stat_b, stat_band, stat_ca, stat_cb)
    return (
        arrived.reshape(1, 1, count, cap, SEG, D),
        input_grad.reshape(ROWS, COLS, D),
    )


def solution(mesh):
    return jax.shard_map(
        per_device,
        mesh=mesh,
        in_specs=(
            P("lat", "lon", None),
            P("lat", "lon", None),
            P(None, None, "lon", None),
            P(),
            P(),
            P(),
            P(),
            P(),
            P("lat", "lon"),
        ),
        out_specs=(P("lat", "lon", None, None, None, None), P("lat", "lon", None)),
        check_vma=False,
    )
```

```python
import functools

import jax
import jax.numpy as jnp
import numpy as np
from jax import lax
from jax.experimental import pallas as pl
from jax.experimental.pallas import tpu as pltpu
from jax.sharding import PartitionSpec as P

HEADS = 16
HALO = 6
ROWS = 12
COLS = 16
SEG = 4
D = 1024
HEAD_DIM = D // HEADS
TOKENS = ROWS * COLS
HALF = TOKENS // 2
BAND = HALO * COLS
SIDE = ROWS * HALO
CORNER = 40
QUAD = 256
QUAD_HEADS = QUAD // HEAD_DIM
STEPS = D // QUAD
STACK = QUAD_HEADS * HALF
PAD_SIDE = BAND + 2 * CORNER
MIDDLE = TOKENS + 2 * SIDE
SPAN = PAD_SIDE + MIDDLE
KEYS = SPAN + PAD_SIDE
HALO_ROWS = 2 * PAD_SIDE + 2 * SIDE - BAND
HALO_QUERIES = PAD_SIDE + 2 * SIDE
EDGE = SIDE + CORNER
STATS = 128
MESSAGE = D + 2 * STATS
MIB = 1024 * 1024
BF = jnp.bfloat16
F32 = jnp.float32


def dot(a, b):
    return jnp.dot(a, b, preferred_element_type=F32)


def dot_nt(a, b):
    return lax.dot_general(a, b, (((1,), (1,)), ((), ())), preferred_element_type=F32)


def dot_tn(a, b):
    return lax.dot_general(a, b, (((0,), (0,)), ((), ())), preferred_element_type=F32)


def first_column(side, parity):
    return COLS - HALO if side == parity else 0


def selection_table():
    table = np.zeros((4, 2 * EDGE + 2 * CORNER, TOKENS + BAND), np.float32)
    for lat in range(2):
        for parity in range(2):
            for side in range(2):
                first, base = first_column(side, parity), side * EDGE
                picks = table[2 * lat + parity]
                for c in range(HALO):
                    for r in range(ROWS):
                        picks[base + r * HALO + c, r * COLS + first + c] = 1
                    for i in range(HALO):
                        picks[base + SIDE + i * HALO + c, TOKENS + i * COLS + first + c] = 1
                        row = i + HALO * (1 - lat)
                        picks[2 * EDGE + side * CORNER + i * HALO + c, row * COLS + first + c] = 1
    return table


def key_table():
    table = np.full((4, 8, KEYS), 1000, np.int32)
    table[:, 2] = -1
    for lat in range(2):
        for parity in range(2):
            picks = table[2 * lat + parity]
            low = {"lat": ROWS if lat == 0 else -HALO, "own": 0, "rim": -HALO if lat == 0 else ROWS}

            def put(at, count, width, first_col, kind):
                for k in range(count * width):
                    i, c = divmod(k, width)
                    picks[0, at + k] = low[kind] + i
                    picks[1, at + k] = first_col + c
                    if kind == "rim":
                        picks[2, at + k] = i

            put(0, HALO, COLS, 0, "lat")
            put(PAD_SIDE, ROWS, COLS, 0, "own")
            put(SPAN, HALO, COLS, 0, "rim")
            for side in range(2):
                col = COLS if side == parity else -HALO
                put(BAND + side * CORNER, HALO, HALO, col, "lat")
                put(PAD_SIDE + TOKENS + side * SIDE, ROWS, HALO, col, "own")
                put(SPAN + BAND + side * CORNER, HALO, HALO, col, "rim")
    return table


def head_mask(h, dtype):
    lane = lax.broadcasted_iota(jnp.int32, (1, QUAD), 1)
    return jnp.where(lane // HEAD_DIM == h, 1.0, 0.0).astype(dtype)


def head_mean(values):
    a = lax.broadcasted_iota(jnp.int32, (QUAD, QUAD), 0) // HEAD_DIM
    b = lax.broadcasted_iota(jnp.int32, (QUAD, QUAD), 1) // HEAD_DIM
    block = jnp.where(a == b, 1.0 / HEAD_DIM, 0.0).astype(BF)
    return dot(values.astype(BF), block)


def unit(raw):
    return raw * lax.rsqrt(head_mean(raw * raw) + 1e-06)


def unit_back(raw, grad):
    inverse = lax.rsqrt(head_mean(raw * raw) + 1e-06)
    value = raw * inverse
    return inverse * (grad - value * head_mean(value * grad))


def normed(tokens, gain):
    tokens = tokens.astype(F32)
    return tokens * lax.rsqrt(jnp.mean(tokens * tokens, axis=-1, keepdims=True) + 1e-05) * gain


def multiplier(sharp_ref, j):
    out = jnp.zeros((1, QUAD), F32)
    for h in range(QUAD_HEADS):
        out = out + head_mask(h, F32) * (sharp_ref[j * QUAD_HEADS + h] / HEAD_DIM)
    return out


def stacked(block):
    return jnp.concatenate([block * head_mask(h, BF) for h in range(QUAD_HEADS)], axis=0)


def unstacked(stack):
    out = stack[:HALF] * head_mask(0, F32)
    for h in range(1, QUAD_HEADS):
        out = out + stack[h * HALF : (h + 1) * HALF] * head_mask(h, F32)
    return out


def repeated(block):
    return jnp.concatenate([block] * QUAD_HEADS, axis=0)


def head_lanes(first, pick_one):
    a = lax.broadcasted_iota(jnp.int32, (QUAD, STATS), 0)
    b = lax.broadcasted_iota(jnp.int32, (QUAD, STATS), 1)
    hit = b == a // HEAD_DIM + first
    if pick_one:
        hit = hit & (a % HEAD_DIM == 0)
    return jnp.where(hit, 1.0, 0.0).astype(BF)


def halves(values):
    high = values.astype(BF)
    return high, (values - high.astype(F32)).astype(BF)


def spread(stat, j):
    a = lax.broadcasted_iota(jnp.int32, (STATS, QUAD), 0)
    b = lax.broadcasted_iota(jnp.int32, (STATS, QUAD), 1)
    picks = jnp.where(a == b // HEAD_DIM + j * QUAD_HEADS, 1.0, 0.0).astype(BF)
    high, low = halves(stat)
    return dot(high, picks) + dot(low, picks)


def half_start(lat, half):
    return pl.multiple_of(HALF * ((1 - lat) if half == 0 else lat), 16)


def near_mask(mask_ref, tab_ref, flag_ref, lat):
    rows, cols, place = tab_ref[0, 0:1], tab_ref[0, 1:2], tab_ref[0, 2:3]
    keep = jnp.where(place < 0, 1.0, 0.0)
    for i in range(HALO):
        keep = keep + jnp.where(place == i, flag_ref[lat, i].astype(F32), 0.0)
    for half in range(2):
        at = half * PAD_SIDE
        token = lax.broadcasted_iota(jnp.int32, (HALF, SPAN), 0) + half_start(lat, half)
        near = (jnp.abs(rows[:, at : at + SPAN] - token // COLS) <= HALO) & (
            jnp.abs(cols[:, at : at + SPAN] - token % COLS) <= HALO
        )
        mask_ref[half] = jnp.where(near, keep[:, at : at + SPAN], 0.0)


def lay_keys(ref, own, halo):
    ref[:PAD_SIDE] = halo[:PAD_SIDE]
    ref[PAD_SIDE : PAD_SIDE + TOKENS] = own[:TOKENS]
    ref[PAD_SIDE + TOKENS : SPAN] = halo[PAD_SIDE:HALO_QUERIES]
    ref[SPAN : SPAN + BAND] = own[TOKENS:]
    ref[SPAN + BAND :] = halo[HALO_QUERIES:]


class Copies:
    def __init__(self, sems):
        self.sems, self.used = sems, 0

    def start(self, source, target):
        copy = pltpu.make_async_copy(source, target, self.sems.at[self.used])
        self.used += 1
        copy.start()
        return copy

    def by_step(self, pairs):
        base, width = self.used, len(pairs(0))
        self.used += STEPS * width

        def copies(j):
            return [pltpu.make_async_copy(a, b, self.sems.at[base + j * width + k]) for k, (a, b) in enumerate(pairs(j))]

        def start(j):
            for copy in copies(j):
                copy.start()

        def wait(j):
            for copy in copies(j):
                copy.wait()

        return start, wait


def wait_all(copies):
    for copy in copies:
        copy.wait()


def lane_block(at, j):
    return pl.ds(pl.multiple_of((at + j) * QUAD, QUAD), QUAD)


def rows_at(j):
    return pl.ds(j * QUAD, QUAD)


def pack_kernel(
    place_ref, x_hbm, up_hbm, rim_hbm, sel_hbm, edge_a_ref, edge_b_ref, band_ref, corner_a_ref, corner_b_ref,
    x_ref, up_ref, rim_ref, sel_ref, sems,
):
    lat = place_ref[0]
    copies = Copies(sems)
    loads = [
        copies.start(x_hbm, x_ref),
        copies.start(sel_hbm.at[2 * lat + place_ref[1]], sel_ref),
        copies.start(rim_hbm.at[lat], rim_ref),
        copies.start(up_hbm, up_ref),
    ]
    wait_all(loads)
    band_ref[...] = x_ref[pl.ds(half_start(lat, 0), BAND), :]
    picks = sel_ref[...]
    features = dot(picks, jnp.concatenate([x_ref[...], rim_ref[...]], axis=0))
    grads = dot(picks[: 2 * EDGE, :TOKENS], up_ref[...])
    for side, (ref, corner_ref) in enumerate(((edge_a_ref, corner_a_ref), (edge_b_ref, corner_b_ref))):
        at = side * EDGE
        ref[...] = jnp.concatenate([features[at : at + EDGE], grads[at : at + SIDE]], axis=0).astype(BF)
        at = 2 * EDGE + side * CORNER
        corner_ref[...] = features[at : at + CORNER].astype(BF)


def own_kernel(
    place_ref, sharp_ref, x_hbm, rim_hbm, up_hbm, gain_hbm, w3_hbm, wo_hbm,
    qhat_ref, dout_ref, wo_ref, x_ref, gain_ref, qhat_hbm, rawq_hbm, rawk_hbm, kv_hbm,
    kv_ref, w3_ref, rim_ref, up_ref, rawq_ref, rawk_ref, xn_ref, sems,
):
    copies = Copies(sems)
    loads = [copies.start(x_hbm, x_ref), copies.start(rim_hbm.at[place_ref[0]], rim_ref), copies.start(gain_hbm, gain_ref)]
    start, wait = copies.by_step(
        lambda j: [(w3_hbm.at[:, lane_block(k * STEPS, j)], w3_ref.at[j, :, pl.ds(k * QUAD, QUAD)]) for k in range(3)]
        + [(wo_hbm.at[rows_at(j)], wo_ref.at[rows_at(j)])]
    )
    start(0)
    up_load = copies.start(up_hbm, up_ref)
    for j in range(1, STEPS):
        start(j)
    outputs = [(qhat_ref, qhat_hbm), (rawq_ref, rawq_hbm), (rawk_ref, rawk_hbm), (kv_ref, kv_hbm)]
    store, stored = copies.by_step(lambda j: [(ref.at[j], hbm.at[j]) for ref, hbm in outputs])
    wait_all(loads)
    xn_ref[:TOKENS] = normed(x_ref[...], gain_ref[...]).astype(BF)
    xn_ref[TOKENS:] = normed(rim_ref[...], gain_ref[...]).astype(BF)
    for j in range(STEPS):
        wait(j)
        raw = dot(xn_ref[...], w3_ref[j])
        raw_q, raw_k = raw[:TOKENS, :QUAD], raw[:, QUAD : 2 * QUAD]
        units = unit(jnp.concatenate([raw_q, raw_k], axis=0))
        rawq_ref[j] = raw_q
        rawk_ref[j] = raw_k[:TOKENS]
        qhat_ref[j] = (units[:TOKENS] * multiplier(sharp_ref, j)).astype(BF)
        kv_ref[j, 0] = units[TOKENS:].astype(BF)
        kv_ref[j, 1] = raw[:, 2 * QUAD :].astype(BF)
        store(j)
        if j == 0:
            up_load.wait()
        dout_ref[j] = dot_nt(up_ref[...], wo_ref[rows_at(j)]).astype(BF)
    for j in range(STEPS):
        stored(j)


def forward_kernel(
    place_ref, flag_ref, tab_hbm, sel_hbm, w3_hbm, kv_hbm, band_ref, edge_a_ref, edge_b_ref, corner_a_ref, corner_b_ref, gain_ref,
    qhat_ref, dout_ref,
    mixed_ref, stat_a_ref, stat_b_ref, halo_hbm, stat_hbm, xn_hbm, upn_hbm, weight_hbm, dprime_hbm,
    tab_ref, sel_ref, wkv_ref, kv_ref, halo_ref, stat_ref, xn_ref, upn_ref, weight_ref, dprime_ref, mask_ref, key_ref, value_ref, linv_ref, sems,
):
    lat = place_ref[0]
    spot = 2 * lat + place_ref[1]
    copies = Copies(sems)
    loads = [copies.start(tab_hbm.at[spot], tab_ref.at[0])]
    start, wait = copies.by_step(
        lambda j: [(w3_hbm.at[:, lane_block(k * STEPS, j)], wkv_ref.at[j, :, pl.ds((k - 1) * QUAD, QUAD)]) for k in (1, 2)]
        + [(kv_hbm.at[j], kv_ref.at[j])]
    )
    for j in range(STEPS):
        start(j)
    loads.append(copies.start(sel_hbm.at[spot], sel_ref))
    store, stored = copies.by_step(
        lambda j: [(halo_ref.at[j], halo_hbm.at[j]), (weight_ref.at[j], weight_hbm.at[j]), (dprime_ref.at[j], dprime_hbm.at[j])]
    )
    gain = gain_ref[...]
    edge_a, edge_b = edge_a_ref[...].astype(F32), edge_b_ref[...].astype(F32)
    pieces = [ref[...].astype(F32) for ref in (band_ref, corner_a_ref, corner_b_ref)]
    pieces += [edge_a[:SIDE], edge_b[:SIDE], edge_a[SIDE:EDGE], edge_b[SIDE:EDGE]]
    xn_ref[...] = normed(jnp.concatenate(pieces, axis=0), gain).astype(BF)
    upn_ref[...] = jnp.concatenate([edge_a[EDGE:], edge_b[EDGE:]], axis=0).astype(BF)
    stores = [copies.start(xn_ref.at[pl.ds(0, HALO_QUERIES)], xn_hbm), copies.start(upn_ref, upn_hbm)]
    loads[0].wait()
    near_mask(mask_ref, tab_ref, flag_ref, lat)
    stat = jnp.zeros((TOKENS, STATS), F32)
    for j in range(STEPS):
        wait(j)
        raw = dot(xn_ref[...], wkv_ref[j])
        halo_k = unit(raw[:, :QUAD]).astype(BF)
        halo_v = raw[:, QUAD:].astype(BF)
        halo_ref[j, 0] = halo_k
        halo_ref[j, 1] = halo_v
        lay_keys(key_ref.at[j % 2], kv_ref[j, 0], halo_k)
        lay_keys(value_ref.at[j % 2], kv_ref[j, 1], halo_v)
        for half in range(2):
            at, piece = half * PAD_SIDE, pl.ds(half_start(lat, half), HALF)
            scores = dot_nt(stacked(qhat_ref[j, piece, :]), key_ref[j % 2, at : at + SPAN])
            weights = jnp.exp(scores) * repeated(mask_ref[half])
            inverse = jnp.broadcast_to(1.0 / jnp.sum(weights, axis=-1, keepdims=True), (STACK, QUAD))
            weights = weights.astype(BF)
            weight_ref[j, half] = weights
            mixed = unstacked(dot(weights, value_ref[j % 2, at : at + SPAN]) * inverse)
            mixed_ref[piece, rows_at(j)] = mixed.astype(BF)
            linv_ref[j, piece, :] = unstacked(inverse)
        dprime = (dout_ref[j].astype(F32) * linv_ref[j]).astype(BF)
        dprime_ref[j] = dprime
        inner = dprime.astype(F32) * mixed_ref[:, rows_at(j)].astype(F32)
        high, low = halves(linv_ref[j])
        picks = head_lanes(j * QUAD_HEADS, True)
        stat = stat + dot(high, picks) + dot(low, picks) + dot(inner.astype(BF), head_lanes(HEADS + j * QUAD_HEADS, False))
        store(j)
    stat_ref[...] = stat
    stores.append(copies.start(stat_ref, stat_hbm))
    loads[1].wait()
    high, low = halves(stat)
    picks = sel_ref[: 2 * EDGE, :TOKENS]
    picked = dot(picks, high) + dot(picks, low)
    stat_a_ref[...] = picked[:SIDE]
    stat_b_ref[...] = picked[EDGE : EDGE + SIDE]
    for j in range(STEPS):
        stored(j)
    wait_all(stores)


def output_kernel(place_ref, owner_ref, x_ref, mixed_ref, wo_ref, going_hbm, acc_ref, going_ref, count_ref, sems):
    acc_ref[...] = x_ref[...].astype(F32) + dot(mixed_ref[...], wo_ref[...])
    going_ref[...] = jnp.zeros_like(going_ref)
    for o in range(going_ref.shape[0]):
        count_ref[o] = 0
    for s in range(TOKENS // SEG):
        owner = owner_ref[s // (COLS // SEG), s % (COLS // SEG)]
        slot = count_ref[owner]
        count_ref[owner] = slot + 1
        going_ref[owner, slot] = acc_ref[s * SEG : (s + 1) * SEG, :].astype(BF)
    Copies(sems).start(going_ref, going_hbm).wait()


def message_kernel(
    place_ref, up_hbm, upn_hbm, stat_hbm, stat_a_hbm, stat_b_hbm, out_ref, up_ref, upn_ref, stat_ref, stat_a_ref, stat_b_ref, sems
):
    lat = place_ref[0]
    piece = pl.ds(half_start(lat, 0), BAND)
    copies = Copies(sems)
    wait_all(
        [
            copies.start(hbm, ref)
            for hbm, ref in (
                (up_hbm.at[piece], up_ref), (upn_hbm, upn_ref), (stat_hbm.at[piece], stat_ref), (stat_a_hbm, stat_a_ref),
                (stat_b_hbm, stat_b_ref),
            )
        ]
    )
    a = lax.broadcasted_iota(jnp.int32, (2 * CORNER, 2 * SIDE), 0)
    b = lax.broadcasted_iota(jnp.int32, (2 * CORNER, 2 * SIDE), 1)
    side, inside = a // CORNER, HALO * HALO
    row = a - side * CORNER
    picks = jnp.where((b == row + inside * (1 - lat) + side * SIDE) & (row < inside), 1.0, 0.0).astype(BF)
    out_ref[:BAND, :D] = up_ref[...]
    out_ref[BAND:, :D] = dot(picks, upn_ref[...]).astype(BF)
    high, low = halves(jnp.concatenate([stat_a_ref[...], stat_b_ref[...]], axis=0))
    stats = jnp.concatenate([stat_ref[...], dot(picks, high) + dot(picks, low)], axis=0)
    high, low = halves(stats)
    out_ref[:, D : D + STATS] = high
    out_ref[:, D + STATS :] = low


def inner_rows(row_ref, j):
    row = HEADS + j * QUAD_HEADS
    width = row_ref.shape[1]
    parts = [jnp.broadcast_to(row_ref[row + h : row + h + 1, :], (HALF, width)) for h in range(QUAD_HEADS)]
    return jnp.concatenate(parts, axis=0)


def key_pass(keys, values, queries, grads, mask, inner):
    weights = jnp.exp(dot_nt(stacked(keys), queries)) * repeated(mask)
    grad_scores = weights * (dot_nt(stacked(values), grads) - inner)
    return unstacked(dot(grad_scores.astype(BF), queries)), unstacked(dot(weights.astype(BF), grads))


def query_kernel(
    place_ref, sharp_ref, flag_ref, xn_hbm, upn_hbm, tab_hbm, w3_hbm, wo_hbm, qhat_hbm, kv_hbm, halo_hbm, weight_hbm, dprime_hbm,
    rawq_hbm, rawk_hbm, stat_hbm, stat_a_hbm, stat_b_hbm,
    gqn_ref, query_ref, grad_ref, far_ref, mask_ref, wkv_ref, wo_ref, kv_ref, rawk_ref, row_ref,
    xn_ref, upn_ref, tab_ref, wq_ref, qhat_ref, halo_ref, weight_ref, dprime_ref, rawq_ref, stat_ref, stat_a_ref, stat_b_ref,
    key_ref, value_ref, dq_ref, sems,
):
    lat = place_ref[0]
    copies = Copies(sems)
    loads = [
        copies.start(hbm, ref)
        for hbm, ref in (
            (xn_hbm, xn_ref), (upn_hbm, upn_ref), (stat_hbm, stat_ref), (stat_a_hbm, stat_a_ref), (stat_b_hbm, stat_b_ref),
            (tab_hbm.at[2 * lat + place_ref[1]], tab_ref.at[0]),
        )
    ]
    start, wait = copies.by_step(
        lambda j: [
            (w3_hbm.at[:, lane_block(0, j)], wq_ref.at[j]),
            (wo_hbm.at[rows_at(j)], wo_ref.at[rows_at(j)]),
            (qhat_hbm.at[j], qhat_ref.at[j]),
            (kv_hbm.at[j], kv_ref.at[j]),
            (halo_hbm.at[j], halo_ref.at[j]),
            (dprime_hbm.at[j], dprime_ref.at[j]),
            (weight_hbm.at[j], weight_ref.at[j]),
            (rawq_hbm.at[j], rawq_ref.at[j]),
        ]
    )
    start_later, wait_later = copies.by_step(
        lambda j: [
            (rawk_hbm.at[j], rawk_ref.at[j]),
            (w3_hbm.at[:, lane_block(STEPS, j)], wkv_ref.at[j, 0]),
            (w3_hbm.at[:, lane_block(2 * STEPS, j)], wkv_ref.at[j, 1]),
        ]
    )
    for j in range(STEPS):
        start(j)
    for j in range(STEPS):
        start_later(j)
    wait_all(loads)
    near_mask(mask_ref, tab_ref, flag_ref, lat)
    edges = jnp.concatenate([stat_a_ref[...], stat_b_ref[...]], axis=0)
    row_ref[...] = jnp.concatenate([stat_ref[...], edges], axis=0).T
    gqn_ref[...] = jnp.zeros_like(gqn_ref)
    for j in range(STEPS):
        wait(j)
        lay_keys(key_ref.at[j % 2], kv_ref[j, 0], halo_ref[j, 0])
        lay_keys(value_ref.at[j % 2], kv_ref[j, 1], halo_ref[j, 1])
        halo_q = (unit(dot(xn_ref[...], wq_ref[j])) * multiplier(sharp_ref, j)).astype(BF)
        query_ref[j, :PAD_SIDE] = halo_q[:PAD_SIDE]
        query_ref[j, PAD_SIDE : PAD_SIDE + TOKENS] = qhat_ref[j]
        query_ref[j, PAD_SIDE + TOKENS :] = halo_q[PAD_SIDE:]
        grad_ref[j, :TOKENS] = dprime_ref[j]
        grad_ref[j, TOKENS:] = (dot_nt(upn_ref[...], wo_ref[rows_at(j)]) * spread(edges, j)).astype(BF)
        for half in range(2):
            at, piece = half * PAD_SIDE, pl.ds(half_start(lat, half), HALF)
            stat = stat_ref[piece, :]
            lane = HEADS + j * QUAD_HEADS
            inner = jnp.concatenate([stat[:, lane + h : lane + h + 1] for h in range(QUAD_HEADS)], axis=0)
            grad_probs = dot_nt(stacked(dprime_ref[j, piece, :]), value_ref[j % 2, at : at + SPAN])
            grad_scores = weight_ref[j, half].astype(F32) * (grad_probs - inner)
            dq_ref[j % 2, piece, :] = unstacked(dot(grad_scores.astype(BF), key_ref[j % 2, at : at + SPAN]))
        piece = pl.ds(half_start(lat, 1), HALF)
        far_ref[j, 0], far_ref[j, 1] = key_pass(
            kv_ref[j, 0, piece, :], kv_ref[j, 1, piece, :], query_ref[j, PAD_SIDE:], grad_ref[j], mask_ref[1, :, :MIDDLE],
            inner_rows(row_ref, j),
        )
        grad_q = unit_back(rawq_ref[j], dq_ref[j % 2] * multiplier(sharp_ref, j)).astype(BF)
        gqn_ref[...] += dot_nt(grad_q, wq_ref[j])
    for j in range(STEPS):
        wait_later(j)


def key_kernel(
    place_ref, x_hbm, up_hbm, gain_hbm, gqn_ref, query_ref, grad_ref, far_ref, mask_ref, wkv_ref, wo_ref, kv_ref, rawk_ref, row_ref,
    message_ref,
    out_hbm,
    x_ref, up_ref, gain_ref, out_ref, all_row_ref, all_ref, dk_ref, dv_ref, acc_ref, sems,
):
    lat = place_ref[0]
    copies = Copies(sems)
    loads = [copies.start(x_hbm, x_ref), copies.start(up_hbm, up_ref), copies.start(gain_hbm, gain_ref)]
    message = message_ref[:, D : D + STATS].astype(F32) + message_ref[:, D + STATS :].astype(F32)
    all_row_ref[...] = jnp.concatenate([message.T, row_ref[...]], axis=1)
    acc_ref[...] = gqn_ref[...]
    for j in range(STEPS):
        slot = j % 2
        all_ref[slot, :PAD_SIDE] = (dot_nt(message_ref[:, :D], wo_ref[rows_at(j)]) * spread(message, j)).astype(BF)
        all_ref[slot, PAD_SIDE:] = grad_ref[j]
        near, far = pl.ds(half_start(lat, 0), HALF), pl.ds(half_start(lat, 1), HALF)
        dk_ref[slot, near, :], dv_ref[slot, near, :] = key_pass(
            kv_ref[j, 0, near, :], kv_ref[j, 1, near, :], query_ref[j], all_ref[slot], mask_ref[0], inner_rows(all_row_ref, j)
        )
        dk_ref[slot, far, :], dv_ref[slot, far, :] = far_ref[j, 0], far_ref[j, 1]
        grad_k = unit_back(rawk_ref[j], dk_ref[slot]).astype(BF)
        acc_ref[...] += dot_nt(grad_k, wkv_ref[j, 0]) + dot_nt(dv_ref[slot].astype(BF), wkv_ref[j, 1])
    wait_all(loads)
    tokens = x_ref[...].astype(F32)
    inverse = lax.rsqrt(jnp.mean(tokens * tokens, axis=-1, keepdims=True) + 1e-05)
    grad = acc_ref[...] * gain_ref[...]
    value = tokens * inverse
    back = inverse * (grad - value * jnp.mean(value * grad, axis=-1, keepdims=True))
    out_ref[...] = (up_ref[...].astype(F32) + back).astype(BF)
    copies.start(out_ref, out_hbm).wait()


def call(kernel, inputs, outputs, scratch=(), limit=32, flops=0, name=None):
    def specs(pairs):
        return [pl.BlockSpec(memory_space=space) for space, _ in pairs]

    def placed(space, array):
        return array if space == pltpu.SMEM else pltpu.with_memory_space_constraint(array, space)

    return pl.pallas_call(
        kernel,
        in_specs=specs(inputs),
        out_specs=specs(outputs),
        out_shape=[space(shape.shape, shape.dtype) for space, shape in outputs],
        scratch_shapes=list(scratch),
        compiler_params=pltpu.CompilerParams(vmem_limit_bytes=limit * MIB),
        cost_estimate=pl.CostEstimate(flops=flops, bytes_accessed=8 << 20, transcendentals=0),
        name=name,
    )(*[placed(space, array) for space, array in inputs])


def hbm(*arrays):
    return [(pltpu.HBM, array) for array in arrays]


def near(*arrays):
    return [(pltpu.VMEM, array) for array in arrays]


def scalars(*arrays):
    return [(pltpu.SMEM, array) for array in arrays]


def like(*shape, dtype=BF):
    return jax.ShapeDtypeStruct(shape, dtype)


def partners(count):
    return (
        [(i, i + 1 - 2 * (i % 2)) for i in range(count)],
        [(i, (i - 1 + 2 * (i % 2)) % count) for i in range(count)],
    )


def across(pairs):
    return [(2 * a + lat, 2 * b + 1 - lat) for a, b in pairs for lat in range(2)]


def per_device(
    slab_features, upstream_gradient, rim_feature_rows, rim_presence_flags, feature_rescaling_coefficients,
    triple_projection_matrix, final_projection_matrix, score_sharpness, column_group_decoder_longitude,
):
    count = lax.axis_size("lon")
    cap = max(2, (2 * (TOKENS // SEG) + count - 1) // count)
    place = jnp.stack([lax.axis_index("lat"), lax.axis_index("lon") % 2]).astype(jnp.int32)
    x = slab_features.reshape(TOKENS, D)
    up = upstream_gradient.reshape(TOKENS, D)
    rim = rim_feature_rows.reshape(2, BAND, D)
    gain = feature_rescaling_coefficients.reshape(1, D)
    w3, wo = triple_projection_matrix, final_projection_matrix
    table = selection_table()
    selection = jnp.asarray(table, BF)
    keys = jnp.asarray(key_table())
    flags = rim_presence_flags

    side_a, side_b = partners(count)

    def vmem(*shape, dtype=BF):
        return pltpu.VMEM(shape, dtype)

    def sems(n):
        return pltpu.SemaphoreType.DMA((n,))

    picks_shape = table.shape[1:]
    edge_a, edge_b, band, corner_a, corner_b = call(
        pack_kernel,
        scalars(place) + hbm(x, up, rim, selection),
        near(like(EDGE + SIDE, D), like(EDGE + SIDE, D), like(BAND, D), like(CORNER, D), like(CORNER, D)),
        [vmem(TOKENS, D), vmem(TOKENS, D), vmem(BAND, D), vmem(*picks_shape), sems(4)],
        limit=24, name="edge_tokens",
    )
    band = lax.ppermute(band, "lat", [(0, 1), (1, 0)])
    corner_a = lax.ppermute(corner_a, ("lon", "lat"), across(side_a))
    corner_b = lax.ppermute(corner_b, ("lon", "lat"), across(side_b))
    edge_b = lax.ppermute(edge_b, "lon", side_b)
    edge_a = lax.ppermute(edge_a, "lon", side_a)

    quads, quads32 = like(STEPS, TOKENS, QUAD), like(STEPS, TOKENS, QUAD, dtype=F32)
    kv_like = like(STEPS, 2, TOKENS + BAND, QUAD)
    qhat_near, dout, wo_near, x_near, gain_near, qhat, rawq, rawk, kv = call(
        own_kernel,
        scalars(place, score_sharpness) + hbm(x, rim, up, gain, w3, wo),
        near(quads, quads, like(D, D), like(TOKENS, D), like(1, D, dtype=F32))
        + hbm(quads, quads32, quads32, kv_like),
        [vmem(STEPS, 2, TOKENS + BAND, QUAD), vmem(STEPS, D, 3 * QUAD), vmem(BAND, D), vmem(TOKENS, D),
         vmem(STEPS, TOKENS, QUAD, dtype=F32), vmem(STEPS, TOKENS, QUAD, dtype=F32), vmem(TOKENS + BAND, D), sems(4 + 4 * STEPS + 4 * STEPS)],
        limit=24, flops=2 * 1024 * 1024 * (192 * 2 + 288 * 2), name="own_projections",
    )

    kv_scratch = vmem(STEPS, 2, TOKENS + BAND, QUAD)
    stat_like, side_like = like(TOKENS, STATS, dtype=F32), like(SIDE, STATS, dtype=F32)
    mixed, stat_a, stat_b, halo_kv, stat, xn_halo, up_halo, weights, dprime = call(
        forward_kernel,
        scalars(place, flags) + hbm(keys, selection, w3, kv)
        + near(band, edge_a, edge_b, corner_a, corner_b, gain_near, qhat_near, dout),
        near(like(TOKENS, D), side_like, side_like)
        + hbm(like(STEPS, 2, HALO_ROWS, QUAD), stat_like, like(HALO_QUERIES, D), like(2 * SIDE, D),
              like(STEPS, 2, STACK, SPAN), quads),
        [vmem(1, 8, KEYS, dtype=jnp.int32), vmem(*picks_shape), vmem(STEPS, D, 2 * QUAD), kv_scratch, vmem(STEPS, 2, HALO_ROWS, QUAD),
         vmem(TOKENS, STATS, dtype=F32),
         vmem(HALO_ROWS, D), vmem(2 * SIDE, D), vmem(STEPS, 2, STACK, SPAN), vmem(STEPS, TOKENS, QUAD),
         vmem(2, HALF, SPAN, dtype=F32), vmem(2, KEYS, QUAD), vmem(2, KEYS, QUAD), vmem(STEPS, TOKENS, QUAD, dtype=F32),
         sems(2 + 3 * STEPS + 3 * STEPS + 3)],
        limit=24, flops=2 * 1024 * 1024 * 2000, name="attention_forward",
    )
    stat_b = lax.ppermute(stat_b, "lon", side_b)
    stat_a = lax.ppermute(stat_a, "lon", side_a)

    (going,) = call(
        output_kernel,
        scalars(place, column_group_decoder_longitude) + near(x_near, mixed, wo_near),
        hbm(like(count, cap, SEG, D)),
        [vmem(TOKENS, D, dtype=F32), vmem(count, cap, SEG, D), pltpu.SMEM((count,), jnp.int32), sems(1)],
        limit=24, flops=2 * 1024 * 1024 * 200, name="output_segments",
    )
    going, stat_a, stat_b = lax.optimization_barrier((going, stat_a, stat_b))
    arrived = lax.all_to_all(going, "lon", split_axis=0, concat_axis=0, tiled=True)

    (message,) = call(
        message_kernel,
        scalars(place) + hbm(up, up_halo, stat, stat_a, stat_b),
        near(like(PAD_SIDE, MESSAGE)),
        [vmem(BAND, D), vmem(2 * SIDE, D), vmem(BAND, STATS, dtype=F32), vmem(SIDE, STATS, dtype=F32), vmem(SIDE, STATS, dtype=F32),
         sems(5)],
        limit=24, flops=1024, name="boundary_message",
    )
    message = lax.ppermute(message, "lat", [(0, 1), (1, 0)])

    handed = call(
        query_kernel,
        scalars(place, score_sharpness, flags)
        + hbm(xn_halo, up_halo, keys, w3, wo, qhat, kv, halo_kv, weights, dprime, rawq, rawk, stat, stat_a, stat_b),
        near(like(TOKENS, D, dtype=F32), like(STEPS, SPAN, QUAD), like(STEPS, MIDDLE, QUAD), like(STEPS, 2, HALF, QUAD, dtype=F32),
             like(2, HALF, SPAN, dtype=F32), like(STEPS, 2, D, QUAD), like(D, D), kv_like, quads32, like(STATS, MIDDLE, dtype=F32)),
        [vmem(HALO_QUERIES, D), vmem(2 * SIDE, D), vmem(1, 8, KEYS, dtype=jnp.int32), vmem(STEPS, D, QUAD),
         vmem(STEPS, TOKENS, QUAD), vmem(STEPS, 2, HALO_ROWS, QUAD), vmem(STEPS, 2, STACK, SPAN), vmem(STEPS, TOKENS, QUAD),
         vmem(STEPS, TOKENS, QUAD, dtype=F32), vmem(TOKENS, STATS, dtype=F32), vmem(SIDE, STATS, dtype=F32),
         vmem(SIDE, STATS, dtype=F32), vmem(2, KEYS, QUAD), vmem(2, KEYS, QUAD), vmem(2, TOKENS, QUAD, dtype=F32),
         sems(6 + 8 * STEPS + 3 * STEPS)],
        limit=24, flops=2 * 1024 * 1024 * 4000, name="query_gradient",
    )

    (input_grad,) = call(
        key_kernel,
        scalars(place) + hbm(x, up, gain) + near(*handed, message),
        hbm(like(TOKENS, D)),
        [vmem(TOKENS, D), vmem(TOKENS, D), vmem(1, D, dtype=F32), vmem(TOKENS, D), vmem(STATS, SPAN, dtype=F32),
         vmem(2, SPAN, QUAD), vmem(2, TOKENS, QUAD, dtype=F32), vmem(2, TOKENS, QUAD, dtype=F32), vmem(TOKENS, D, dtype=F32), sems(4)],
        limit=24, flops=2 * 1024 * 1024 * 2000, name="key_gradient",
    )
    return (
        arrived.reshape(1, 1, count, cap, SEG, D),
        input_grad.reshape(ROWS, COLS, D),
    )


def solution(mesh):
    return jax.shard_map(
        per_device,
        mesh=mesh,
        in_specs=(
            P("lat", "lon", None),
            P("lat", "lon", None),
            P(None, None, "lon", None),
            P(),
            P(),
            P(),
            P(),
            P(),
            P("lat", "lon"),
        ),
        out_specs=(P("lat", "lon", None, None, None, None), P("lat", "lon", None)),
        check_vma=False,
    )
```

```python
import functools

import jax
import jax.numpy as jnp
import numpy as np
from jax import lax
from jax.experimental import pallas as pl
from jax.experimental.pallas import tpu as pltpu
from jax.sharding import PartitionSpec as P

HEADS = 16
HALO = 6
ROWS = 12
COLS = 16
SEG = 4
D = 1024
HEAD_DIM = D // HEADS
TOKENS = ROWS * COLS
HALF = TOKENS // 2
BAND = HALO * COLS
SIDE = ROWS * HALO
CORNER = 40
QUAD = 256
QUAD_HEADS = QUAD // HEAD_DIM
STEPS = D // QUAD
STACK = QUAD_HEADS * HALF
PAD_SIDE = BAND + 2 * CORNER
MIDDLE = TOKENS + 2 * SIDE
SPAN = PAD_SIDE + MIDDLE
KEYS = SPAN + PAD_SIDE
HALO_ROWS = 2 * PAD_SIDE + 2 * SIDE - BAND
HALO_QUERIES = PAD_SIDE + 2 * SIDE
EDGE = SIDE + CORNER
STATS = 128
MESSAGE = D + 2 * STATS
MIB = 1024 * 1024
BF = jnp.bfloat16
F32 = jnp.float32


def dot(a, b):
    return jnp.dot(a, b, preferred_element_type=F32)


def dot_nt(a, b):
    return lax.dot_general(a, b, (((1,), (1,)), ((), ())), preferred_element_type=F32)


def dot_tn(a, b):
    return lax.dot_general(a, b, (((0,), (0,)), ((), ())), preferred_element_type=F32)


def first_column(side, parity):
    return COLS - HALO if side == parity else 0


def inner_row(lat, row):
    return (row + HALO * (1 - lat)) % ROWS


def selection_table():
    table = np.zeros((4, 2 * EDGE + 2 * CORNER, TOKENS + BAND), np.float32)
    for lat in range(2):
        for parity in range(2):
            for side in range(2):
                first, base = first_column(side, parity), side * EDGE
                picks = table[2 * lat + parity]
                for c in range(HALO):
                    for r in range(ROWS):
                        picks[base + r * HALO + c, inner_row(lat, r) * COLS + first + c] = 1
                    for i in range(HALO):
                        picks[base + SIDE + i * HALO + c, TOKENS + i * COLS + first + c] = 1
                        row = i + HALO * (1 - lat)
                        picks[2 * EDGE + side * CORNER + i * HALO + c, inner_row(lat, row) * COLS + first + c] = 1
    return table


def key_table():
    table = np.full((4, 8, KEYS), 1000, np.int32)
    table[:, 2] = -1
    for lat in range(2):
        for parity in range(2):
            picks = table[2 * lat + parity]
            low = {"lat": ROWS if lat == 0 else -HALO, "own": 0, "rim": -HALO if lat == 0 else ROWS}

            def put(at, count, width, first_col, kind):
                for k in range(count * width):
                    i, c = divmod(k, width)
                    picks[0, at + k] = low[kind] + i
                    picks[1, at + k] = first_col + c
                    if kind == "rim":
                        picks[2, at + k] = i

            put(0, HALO, COLS, 0, "lat")
            put(PAD_SIDE, ROWS, COLS, 0, "own")
            picks[0, PAD_SIDE : PAD_SIDE + TOKENS] = np.repeat([r for _, r in sorted((inner_row(lat, r), r) for r in range(ROWS))], COLS)
            put(SPAN, HALO, COLS, 0, "rim")
            for side in range(2):
                col = COLS if side == parity else -HALO
                put(BAND + side * CORNER, HALO, HALO, col, "lat")
                put(PAD_SIDE + TOKENS + side * SIDE, ROWS, HALO, col, "own")
                put(SPAN + BAND + side * CORNER, HALO, HALO, col, "rim")
    return table


def head_mask(h, dtype):
    lane = lax.broadcasted_iota(jnp.int32, (1, QUAD), 1)
    return jnp.where(lane // HEAD_DIM == h, 1.0, 0.0).astype(dtype)


def head_mean(values):
    a = lax.broadcasted_iota(jnp.int32, (QUAD, QUAD), 0) // HEAD_DIM
    b = lax.broadcasted_iota(jnp.int32, (QUAD, QUAD), 1) // HEAD_DIM
    block = jnp.where(a == b, 1.0 / HEAD_DIM, 0.0).astype(BF)
    return dot(values.astype(BF), block)


def unit(raw):
    return raw * lax.rsqrt(head_mean(raw * raw) + 1e-06)


def unit_back(raw, grad):
    raw = raw.astype(F32)
    inverse = lax.rsqrt(head_mean(raw * raw) + 1e-06)
    value = raw * inverse
    return inverse * (grad - value * head_mean(value * grad))


def normed(tokens, gain):
    tokens = tokens.astype(F32)
    return tokens * lax.rsqrt(jnp.mean(tokens * tokens, axis=-1, keepdims=True) + 1e-05) * gain


def multiplier(sharp_ref, j):
    out = jnp.zeros((1, QUAD), F32)
    for h in range(QUAD_HEADS):
        out = out + head_mask(h, F32) * (sharp_ref[j * QUAD_HEADS + h] / HEAD_DIM)
    return out


def stacked(block):
    return jnp.concatenate([block * head_mask(h, BF) for h in range(QUAD_HEADS)], axis=0)


def unstacked(stack):
    out = stack[:HALF] * head_mask(0, F32)
    for h in range(1, QUAD_HEADS):
        out = out + stack[h * HALF : (h + 1) * HALF] * head_mask(h, F32)
    return out


def repeated(block):
    return jnp.concatenate([block] * QUAD_HEADS, axis=0)


def head_lanes(first, pick_one):
    a = lax.broadcasted_iota(jnp.int32, (QUAD, STATS), 0)
    b = lax.broadcasted_iota(jnp.int32, (QUAD, STATS), 1)
    hit = b == a // HEAD_DIM + first
    if pick_one:
        hit = hit & (a % HEAD_DIM == 0)
    return jnp.where(hit, 1.0, 0.0).astype(BF)


def halves(values):
    high = values.astype(BF)
    return high, (values - high.astype(F32)).astype(BF)


def spread(stat, j):
    a = lax.broadcasted_iota(jnp.int32, (STATS, QUAD), 0)
    b = lax.broadcasted_iota(jnp.int32, (STATS, QUAD), 1)
    picks = jnp.where(a == b // HEAD_DIM + j * QUAD_HEADS, 1.0, 0.0).astype(BF)
    high, low = halves(stat)
    return dot(high, picks) + dot(low, picks)


def where():
    lat = lax.axis_index("lat")
    return lat, 2 * lat + lax.axis_index("lon") % 2


def half_start(lat, half):
    return pl.multiple_of(HALF * ((1 - lat) if half == 0 else lat), 16)


def near_mask(mask_ref, tab_ref, flag_ref, lat):
    rows, cols, place = tab_ref[0, 0:1], tab_ref[0, 1:2], tab_ref[0, 2:3]
    keep = jnp.where(place < 0, 1.0, 0.0)
    for i in range(HALO):
        keep = keep + jnp.where(place == i, flag_ref[lat, i].astype(F32), 0.0)
    for half in range(2):
        at = half * PAD_SIDE
        token = lax.broadcasted_iota(jnp.int32, (HALF, SPAN), 0) + half_start(lat, half)
        near = (jnp.abs(rows[:, at : at + SPAN] - token // COLS) <= HALO) & (
            jnp.abs(cols[:, at : at + SPAN] - token % COLS) <= HALO
        )
        mask_ref[half] = jnp.where(near, keep[:, at : at + SPAN], 0.0)


def lay_keys(ref, own, halo):
    ref[:PAD_SIDE] = halo[:PAD_SIDE]
    ref[PAD_SIDE : PAD_SIDE + TOKENS] = own[:TOKENS]
    ref[PAD_SIDE + TOKENS : SPAN] = halo[PAD_SIDE:HALO_QUERIES]
    ref[SPAN : SPAN + BAND] = own[TOKENS:]
    ref[SPAN + BAND :] = halo[HALO_QUERIES:]


class Copies:
    def __init__(self, sems):
        self.sems, self.used = sems, 0

    def start(self, source, target):
        copy = pltpu.make_async_copy(source, target, self.sems.at[self.used])
        self.used += 1
        copy.start()
        return copy

    def load_tokens(self, hbm, ref, lat):
        return [self.start(hbm.at[pl.ds(half_start(lat, k), HALF)], ref.at[pl.ds(k * HALF, HALF)]) for k in range(2)]

    def store_tokens(self, ref, hbm, lat):
        return [self.start(ref.at[pl.ds(k * HALF, HALF)], hbm.at[pl.ds(half_start(lat, k), HALF)]) for k in range(2)]

    def by_step(self, pairs):
        base, width = self.used, len(pairs(0))
        self.used += STEPS * width

        def copies(j):
            return [pltpu.make_async_copy(a, b, self.sems.at[base + j * width + k]) for k, (a, b) in enumerate(pairs(j))]

        def start(j):
            for copy in copies(j):
                copy.start()

        def wait(j):
            for copy in copies(j):
                copy.wait()

        return start, wait


def wait_all(copies):
    for copy in copies:
        copy.wait()


def lane_block(at, j):
    return pl.ds(pl.multiple_of((at + j) * QUAD, QUAD), QUAD)


def rows_at(j):
    return pl.ds(j * QUAD, QUAD)


def pack_kernel(
    x_hbm, up_hbm, rim_hbm, sel_hbm, edge_a_ref, edge_b_ref, band_ref, corner_a_ref, corner_b_ref,
    x_ref, up_ref, rim_ref, sel_ref, sems,
):
    lat, spot = where()
    copies = Copies(sems)
    loads = copies.load_tokens(x_hbm, x_ref, lat)
    loads += [copies.start(sel_hbm.at[spot], sel_ref), copies.start(rim_hbm.at[lat], rim_ref)]
    loads += copies.load_tokens(up_hbm, up_ref, lat)
    wait_all(loads)
    band_ref[...] = x_ref[:BAND]
    picks = sel_ref[...]
    features = dot(picks, jnp.concatenate([x_ref[...], rim_ref[...]], axis=0))
    grads = dot(picks[: 2 * EDGE, :TOKENS], up_ref[...])
    for side, (ref, corner_ref) in enumerate(((edge_a_ref, corner_a_ref), (edge_b_ref, corner_b_ref))):
        at = side * EDGE
        ref[...] = jnp.concatenate([features[at : at + EDGE], grads[at : at + SIDE]], axis=0).astype(BF)
        at = 2 * EDGE + side * CORNER
        corner_ref[...] = features[at : at + CORNER].astype(BF)


def own_kernel(
    sharp_ref, x_hbm, rim_hbm, up_hbm, gain_hbm, w3_hbm, wo_hbm,
    qhat_ref, dout_ref, wo_ref, x_ref, gain_ref, qhat_hbm, rawq_hbm, rawk_hbm, kv_hbm,
    kv_ref, w3_ref, rim_ref, up_ref, rawq_ref, rawk_ref, xn_ref, sems,
):
    copies = Copies(sems)
    lat, spot = where()
    loads = copies.load_tokens(x_hbm, x_ref, lat) + [copies.start(rim_hbm.at[lat], rim_ref), copies.start(gain_hbm, gain_ref)]
    start, wait = copies.by_step(
        lambda j: [(w3_hbm.at[:, lane_block(k * STEPS, j)], w3_ref.at[j, :, pl.ds(k * QUAD, QUAD)]) for k in range(3)]
    )
    grad_loads = copies.load_tokens(up_hbm, up_ref, lat) + [copies.start(wo_hbm, wo_ref)]
    for j in range(STEPS):
        start(j)
    outputs = [(qhat_ref, qhat_hbm), (rawq_ref, rawq_hbm), (rawk_ref, rawk_hbm), (kv_ref, kv_hbm)]
    store, stored = copies.by_step(lambda j: [(ref.at[j], hbm.at[j]) for ref, hbm in outputs])
    wait_all(loads)
    xn_ref[:TOKENS] = normed(x_ref[...], gain_ref[...]).astype(BF)
    xn_ref[TOKENS:] = normed(rim_ref[...], gain_ref[...]).astype(BF)
    wait_all(grad_loads)
    dout = dot_nt(up_ref[...], wo_ref[...]).astype(BF)
    for j in range(STEPS):
        dout_ref[j] = dout[:, j * QUAD : (j + 1) * QUAD]
    for j in range(STEPS):
        wait(j)
        raw = dot(xn_ref[...], w3_ref[j])
        raw_q, raw_k = raw[:TOKENS, :QUAD], raw[:, QUAD : 2 * QUAD]
        units = unit(jnp.concatenate([raw_q, raw_k], axis=0))
        rawq_ref[j] = raw_q.astype(BF)
        rawk_ref[j] = raw_k[:TOKENS].astype(BF)
        qhat_ref[j] = (units[:TOKENS] * multiplier(sharp_ref, j)).astype(BF)
        kv_ref[j, 0] = units[TOKENS:].astype(BF)
        kv_ref[j, 1] = raw[:, 2 * QUAD :].astype(BF)
        store(j)
    for j in range(STEPS):
        stored(j)


def forward_kernel(
    flag_ref, tab_hbm, sel_hbm, w3_hbm, kv_hbm, band_ref, edge_a_ref, edge_b_ref, corner_a_ref, corner_b_ref, gain_ref,
    qhat_ref, dout_ref,
    mixed_ref, stat_a_ref, stat_b_ref, halo_hbm, stat_hbm, xn_hbm, upn_hbm, weight_hbm, dprime_hbm,
    tab_ref, sel_ref, wkv_ref, kv_ref, halo_ref, stat_ref, xn_ref, upn_ref, weight_ref, dprime_ref, mask_ref, key_ref, value_ref, linv_ref, sems,
):
    lat, spot = where()
    copies = Copies(sems)
    loads = [copies.start(tab_hbm.at[spot], tab_ref.at[0])]
    start, wait = copies.by_step(
        lambda j: [(w3_hbm.at[:, lane_block(k * STEPS, j)], wkv_ref.at[j, :, pl.ds((k - 1) * QUAD, QUAD)]) for k in (1, 2)]
    )
    start_kv, wait_kv = copies.by_step(lambda j: [(kv_hbm.at[j], kv_ref.at[j])])
    for j in range(STEPS):
        start(j)
        start_kv(j)
    loads.append(copies.start(sel_hbm.at[spot], sel_ref))
    store, stored = copies.by_step(
        lambda j: [(halo_ref.at[j], halo_hbm.at[j]), (dprime_ref.at[j], dprime_hbm.at[j])]
    )
    weight_stores = []
    gain = gain_ref[...]
    edge_a, edge_b = edge_a_ref[...].astype(F32), edge_b_ref[...].astype(F32)
    pieces = [ref[...].astype(F32) for ref in (band_ref, corner_a_ref, corner_b_ref)]
    pieces += [edge_a[:SIDE], edge_b[:SIDE], edge_a[SIDE:EDGE], edge_b[SIDE:EDGE]]
    xn_ref[...] = normed(jnp.concatenate(pieces, axis=0), gain).astype(BF)
    upn_ref[...] = jnp.concatenate([edge_a[EDGE:], edge_b[EDGE:]], axis=0).astype(BF)
    stores = [copies.start(xn_ref.at[pl.ds(0, HALO_QUERIES)], xn_hbm), copies.start(upn_ref, upn_hbm)]
    loads[0].wait()
    near_mask(mask_ref, tab_ref, flag_ref, lat)
    stat = jnp.zeros((TOKENS, STATS), F32)
    for j in range(STEPS):
        wait(j)
        raw = dot(xn_ref[...], wkv_ref[j])
        halo_k = unit(raw[:, :QUAD]).astype(BF)
        halo_v = raw[:, QUAD:].astype(BF)
        halo_ref[j, 0] = halo_k
        halo_ref[j, 1] = halo_v
        wait_kv(j)
        lay_keys(key_ref.at[j % 2], kv_ref[j, 0], halo_k)
        lay_keys(value_ref.at[j % 2], kv_ref[j, 1], halo_v)
        for half in range(2):
            at, piece = half * PAD_SIDE, slice(half * HALF, (half + 1) * HALF)
            scores = dot_nt(stacked(qhat_ref[j, piece, :]), key_ref[j % 2, at : at + SPAN])
            weights = jnp.exp(scores) * repeated(mask_ref[half])
            inverse = jnp.broadcast_to(1.0 / jnp.sum(weights, axis=-1, keepdims=True), (STACK, QUAD))
            weights = weights.astype(BF)
            weight_ref[j, half] = weights
            weight_stores.append(copies.start(weight_ref.at[j, half], weight_hbm.at[j, half]))
            mixed = unstacked(dot(weights, value_ref[j % 2, at : at + SPAN]) * inverse)
            mixed_ref[piece, rows_at(j)] = mixed.astype(BF)
            linv_ref[j, piece, :] = unstacked(inverse)
        dprime = (dout_ref[j].astype(F32) * linv_ref[j]).astype(BF)
        dprime_ref[j] = dprime
        inner = dprime.astype(F32) * mixed_ref[:, rows_at(j)].astype(F32)
        high, low = halves(linv_ref[j])
        picks = head_lanes(j * QUAD_HEADS, True)
        stat = stat + dot(high, picks) + dot(low, picks) + dot(inner.astype(BF), head_lanes(HEADS + j * QUAD_HEADS, False))
        store(j)
    stat_ref[...] = stat
    stores.append(copies.start(stat_ref, stat_hbm))
    loads[1].wait()
    high, low = halves(stat)
    picks = sel_ref[: 2 * EDGE, :TOKENS]
    picked = dot(picks, high) + dot(picks, low)
    stat_a_ref[...] = picked[:SIDE]
    stat_b_ref[...] = picked[EDGE : EDGE + SIDE]
    for j in range(STEPS):
        stored(j)
    wait_all(stores + weight_stores)


def output_kernel(owner_ref, x_ref, mixed_ref, wo_ref, going_hbm, acc_ref, going_ref, count_ref, sems):
    lat, spot = where()
    rows = x_ref[...].astype(F32) + dot(mixed_ref[...], wo_ref[...])
    for half in range(2):
        acc_ref[pl.ds(half_start(lat, half), HALF), :] = rows[half * HALF : (half + 1) * HALF]
    going_ref[...] = jnp.zeros_like(going_ref)
    for o in range(going_ref.shape[0]):
        count_ref[o] = 0
    for s in range(TOKENS // SEG):
        owner = owner_ref[s // (COLS // SEG), s % (COLS // SEG)]
        slot = count_ref[owner]
        count_ref[owner] = slot + 1
        going_ref[owner, slot] = acc_ref[s * SEG : (s + 1) * SEG, :].astype(BF)
    Copies(sems).start(going_ref, going_hbm).wait()


def message_kernel(
    up_hbm, upn_hbm, stat_hbm, stat_a_hbm, stat_b_hbm, out_ref, up_ref, upn_ref, stat_ref, stat_a_ref, stat_b_ref, sems
):
    lat, spot = where()
    piece = pl.ds(half_start(lat, 0), BAND)
    copies = Copies(sems)
    wait_all(
        [
            copies.start(hbm, ref)
            for hbm, ref in (
                (up_hbm.at[piece], up_ref), (upn_hbm, upn_ref), (stat_hbm.at[pl.ds(0, BAND)], stat_ref), (stat_a_hbm, stat_a_ref),
                (stat_b_hbm, stat_b_ref),
            )
        ]
    )
    a = lax.broadcasted_iota(jnp.int32, (2 * CORNER, 2 * SIDE), 0)
    b = lax.broadcasted_iota(jnp.int32, (2 * CORNER, 2 * SIDE), 1)
    side, inside = a // CORNER, HALO * HALO
    row = a - side * CORNER
    picks = jnp.where((b == row + inside * (1 - lat) + side * SIDE) & (row < inside), 1.0, 0.0).astype(BF)
    out_ref[:BAND, :D] = up_ref[...]
    out_ref[BAND:, :D] = dot(picks, upn_ref[...]).astype(BF)
    high, low = halves(jnp.concatenate([stat_a_ref[...], stat_b_ref[...]], axis=0))
    stats = jnp.concatenate([stat_ref[...], dot(picks, high) + dot(picks, low)], axis=0)
    high, low = halves(stats)
    out_ref[:, D : D + STATS] = high
    out_ref[:, D + STATS :] = low


def inner_rows(row_ref, j):
    row = HEADS + j * QUAD_HEADS
    width = row_ref.shape[1]
    parts = [jnp.broadcast_to(row_ref[row + h : row + h + 1, :], (HALF, width)) for h in range(QUAD_HEADS)]
    return jnp.concatenate(parts, axis=0)


def key_pass(keys, values, queries, grads, mask, inner):
    weights = jnp.exp(dot_nt(stacked(keys), queries)) * repeated(mask)
    grad_scores = weights * (dot_nt(stacked(values), grads) - inner)
    return unstacked(dot(grad_scores.astype(BF), queries)), unstacked(dot(weights.astype(BF), grads))


def query_kernel(
    sharp_ref, flag_ref, xn_hbm, upn_hbm, tab_hbm, w3_hbm, wo_hbm, qhat_hbm, kv_hbm, halo_hbm, weight_hbm, dprime_hbm,
    rawq_hbm, rawk_hbm, stat_hbm, stat_a_hbm, stat_b_hbm,
    gqn_ref, query_ref, grad_ref, far_ref, mask_ref, wk_ref, wv_ref, wo_ref, kv_ref, rawk_ref, row_ref,
    xn_ref, upn_ref, tab_ref, wq_ref, qhat_ref, halo_ref, weight_ref, dprime_ref, rawq_ref, stat_ref, stat_a_ref, stat_b_ref,
    key_ref, value_ref, dq_ref, raw_ref, dout_ref, grad_q_ref, sems,
):
    lat, spot = where()
    copies = Copies(sems)
    first = [copies.start(xn_hbm, xn_ref), copies.start(w3_hbm.at[:, pl.ds(0, D)], wq_ref)]
    second = [copies.start(upn_hbm, upn_ref), copies.start(wo_hbm, wo_ref)]
    start, wait = copies.by_step(
        lambda j: [
            (qhat_hbm.at[j], qhat_ref.at[j]),
            (dprime_hbm.at[j], dprime_ref.at[j]),
            (kv_hbm.at[j], kv_ref.at[j]),
            (halo_hbm.at[j], halo_ref.at[j]),
            (weight_hbm.at[j], weight_ref.at[j]),
            (rawq_hbm.at[j], rawq_ref.at[j]),
        ]
    )
    start(0)
    third = [
        copies.start(hbm, ref)
        for hbm, ref in (
            (stat_hbm, stat_ref), (stat_a_hbm, stat_a_ref), (stat_b_hbm, stat_b_ref), (tab_hbm.at[spot], tab_ref.at[0]),
        )
    ]
    for j in range(1, STEPS):
        start(j)
    later = [
        copies.start(rawk_hbm, rawk_ref),
        copies.start(w3_hbm.at[:, pl.ds(D, D)], wk_ref),
        copies.start(w3_hbm.at[:, pl.ds(2 * D, D)], wv_ref),
    ]
    wait_all(first)
    raw_ref[...] = dot(xn_ref[...], wq_ref[...])
    wait_all(second)
    dout_ref[...] = dot_nt(upn_ref[...], wo_ref[...]).astype(BF)
    wait_all(third)
    near_mask(mask_ref, tab_ref, flag_ref, lat)
    edges = jnp.concatenate([stat_a_ref[...], stat_b_ref[...]], axis=0)
    row_ref[...] = jnp.concatenate([stat_ref[...], edges], axis=0).T
    for j in range(STEPS):
        halo_q = (unit(raw_ref[:, rows_at(j)]) * multiplier(sharp_ref, j)).astype(BF)
        query_ref[j, :PAD_SIDE] = halo_q[:PAD_SIDE]
        query_ref[j, PAD_SIDE + TOKENS :] = halo_q[PAD_SIDE:]
        grad_ref[j, TOKENS:] = (dout_ref[:, rows_at(j)].astype(F32) * spread(edges, j)).astype(BF)
        wait(j)
        query_ref[j, PAD_SIDE : PAD_SIDE + TOKENS] = qhat_ref[j]
        grad_ref[j, :TOKENS] = dprime_ref[j]
        lay_keys(key_ref.at[j % 2], kv_ref[j, 0], halo_ref[j, 0])
        lay_keys(value_ref.at[j % 2], kv_ref[j, 1], halo_ref[j, 1])
        for half in range(2):
            at, piece = half * PAD_SIDE, slice(half * HALF, (half + 1) * HALF)
            stat = stat_ref[piece, :]
            lane = HEADS + j * QUAD_HEADS
            inner = jnp.concatenate([stat[:, lane + h : lane + h + 1] for h in range(QUAD_HEADS)], axis=0)
            grad_probs = dot_nt(stacked(dprime_ref[j, piece, :]), value_ref[j % 2, at : at + SPAN])
            grad_scores = weight_ref[j, half].astype(F32) * (grad_probs - inner)
            dq_ref[j % 2, piece, :] = unstacked(dot(grad_scores.astype(BF), key_ref[j % 2, at : at + SPAN]))
        piece = slice(HALF, TOKENS)
        far_ref[j, 0], far_ref[j, 1] = key_pass(
            kv_ref[j, 0, piece, :], kv_ref[j, 1, piece, :], query_ref[j, PAD_SIDE:], grad_ref[j], mask_ref[1, :, :MIDDLE],
            inner_rows(row_ref, j),
        )
        grad_q = unit_back(rawq_ref[j], dq_ref[j % 2] * multiplier(sharp_ref, j))
        grad_q_ref[:, rows_at(j)] = grad_q.astype(BF)
    gqn_ref[...] = dot_nt(grad_q_ref[...], wq_ref[...])
    wait_all(later)


def key_kernel(
    x_hbm, up_hbm, gain_hbm, gqn_ref, query_ref, grad_ref, far_ref, mask_ref, wk_ref, wv_ref, wo_ref, kv_ref, rawk_ref, row_ref,
    message_ref,
    out_hbm,
    x_ref, up_ref, gain_ref, out_ref, all_row_ref, all_ref, dk_ref, dout_ref, grad_k_ref, grad_v_ref, sems,
):
    lat, spot = where()
    copies = Copies(sems)
    loads = copies.load_tokens(x_hbm, x_ref, lat) + copies.load_tokens(up_hbm, up_ref, lat)
    loads.append(copies.start(gain_hbm, gain_ref))
    message = message_ref[:, D : D + STATS].astype(F32) + message_ref[:, D + STATS :].astype(F32)
    all_row_ref[...] = jnp.concatenate([message.T, row_ref[...]], axis=1)
    dout_ref[...] = dot_nt(message_ref[:, :D], wo_ref[...]).astype(BF)
    for j in range(STEPS):
        slot = j % 2
        all_ref[slot, :PAD_SIDE] = (dout_ref[:, rows_at(j)].astype(F32) * spread(message, j)).astype(BF)
        all_ref[slot, PAD_SIDE:] = grad_ref[j]
        dk_ref[slot, :HALF, :], near_dv = key_pass(
            kv_ref[j, 0, :HALF, :], kv_ref[j, 1, :HALF, :], query_ref[j], all_ref[slot], mask_ref[0], inner_rows(all_row_ref, j)
        )
        dk_ref[slot, HALF:, :] = far_ref[j, 0]
        grad_k_ref[:, rows_at(j)] = unit_back(rawk_ref[j], dk_ref[slot]).astype(BF)
        grad_v_ref[:HALF, rows_at(j)] = near_dv.astype(BF)
        grad_v_ref[HALF:, rows_at(j)] = far_ref[j, 1].astype(BF)
    total = gqn_ref[...] + dot_nt(grad_k_ref[...], wk_ref[...]) + dot_nt(grad_v_ref[...], wv_ref[...])
    wait_all(loads)
    tokens = x_ref[...].astype(F32)
    inverse = lax.rsqrt(jnp.mean(tokens * tokens, axis=-1, keepdims=True) + 1e-05)
    grad = total * gain_ref[...]
    value = tokens * inverse
    back = inverse * (grad - value * jnp.mean(value * grad, axis=-1, keepdims=True))
    out_ref[...] = (up_ref[...].astype(F32) + back).astype(BF)
    wait_all(copies.store_tokens(out_ref, out_hbm, lat))


def call(kernel, inputs, outputs, scratch=(), limit=32, flops=0, name=None):
    def specs(pairs):
        return [pl.BlockSpec(memory_space=space) for space, _ in pairs]

    def placed(space, array):
        return array if space == pltpu.SMEM else pltpu.with_memory_space_constraint(array, space)

    return pl.pallas_call(
        kernel,
        in_specs=specs(inputs),
        out_specs=specs(outputs),
        out_shape=[space(shape.shape, shape.dtype) for space, shape in outputs],
        scratch_shapes=list(scratch),
        compiler_params=pltpu.CompilerParams(vmem_limit_bytes=limit * MIB),
        cost_estimate=pl.CostEstimate(flops=flops, bytes_accessed=8 << 20, transcendentals=0),
        name=name,
    )(*[placed(space, array) for space, array in inputs])


def hbm(*arrays):
    return [(pltpu.HBM, array) for array in arrays]


def near(*arrays):
    return [(pltpu.VMEM, array) for array in arrays]


def scalars(*arrays):
    return [(pltpu.SMEM, array) for array in arrays]


def like(*shape, dtype=BF):
    return jax.ShapeDtypeStruct(shape, dtype)


def partners(count):
    return (
        [(i, i + 1 - 2 * (i % 2)) for i in range(count)],
        [(i, (i - 1 + 2 * (i % 2)) % count) for i in range(count)],
    )


def across(pairs):
    return [(2 * a + lat, 2 * b + 1 - lat) for a, b in pairs for lat in range(2)]


def per_device(
    slab_features, upstream_gradient, rim_feature_rows, rim_presence_flags, feature_rescaling_coefficients,
    triple_projection_matrix, final_projection_matrix, score_sharpness, column_group_decoder_longitude,
):
    count = lax.axis_size("lon")
    cap = max(2, (2 * (TOKENS // SEG) + count - 1) // count)
    x = slab_features.reshape(TOKENS, D)
    up = upstream_gradient.reshape(TOKENS, D)
    rim = rim_feature_rows.reshape(2, BAND, D)
    gain = feature_rescaling_coefficients.reshape(1, D)
    w3, wo = triple_projection_matrix, final_projection_matrix
    table = selection_table()
    selection = jnp.asarray(table, BF)
    keys = jnp.asarray(key_table())
    flags = rim_presence_flags

    side_a, side_b = partners(count)

    def vmem(*shape, dtype=BF):
        return pltpu.VMEM(shape, dtype)

    def sems(n):
        return pltpu.SemaphoreType.DMA((n,))

    picks_shape = table.shape[1:]
    edge_a, edge_b, band, corner_a, corner_b = call(
        pack_kernel,
        hbm(x, up, rim, selection),
        near(like(EDGE + SIDE, D), like(EDGE + SIDE, D), like(BAND, D), like(CORNER, D), like(CORNER, D)),
        [vmem(TOKENS, D), vmem(TOKENS, D), vmem(BAND, D), vmem(*picks_shape), sems(6)],
        limit=24, name="edge_tokens",
    )
    band = lax.ppermute(band, "lat", [(0, 1), (1, 0)])
    corner_a = lax.ppermute(corner_a, ("lon", "lat"), across(side_a))
    corner_b = lax.ppermute(corner_b, ("lon", "lat"), across(side_b))
    edge_b = lax.ppermute(edge_b, "lon", side_b)
    edge_a = lax.ppermute(edge_a, "lon", side_a)

    quads = like(STEPS, TOKENS, QUAD)
    kv_like = like(STEPS, 2, TOKENS + BAND, QUAD)
    qhat_near, dout, wo_near, x_near, gain_near, qhat, rawq, rawk, kv = call(
        own_kernel,
        scalars(score_sharpness) + hbm(x, rim, up, gain, w3, wo),
        near(quads, quads, like(D, D), like(TOKENS, D), like(1, D, dtype=F32))
        + hbm(quads, quads, quads, kv_like),
        [vmem(STEPS, 2, TOKENS + BAND, QUAD), vmem(STEPS, D, 3 * QUAD), vmem(BAND, D), vmem(TOKENS, D),
         vmem(STEPS, TOKENS, QUAD), vmem(STEPS, TOKENS, QUAD), vmem(TOKENS + BAND, D), sems(6 + 4 * STEPS + 4 * STEPS)],
        limit=24, flops=2 * 1024 * 1024 * (192 * 2 + 288 * 2), name="own_projections",
    )

    kv_scratch = vmem(STEPS, 2, TOKENS + BAND, QUAD)
    stat_like, side_like = like(TOKENS, STATS, dtype=F32), like(SIDE, STATS, dtype=F32)
    mixed, stat_a, stat_b, halo_kv, stat, xn_halo, up_halo, weights, dprime = call(
        forward_kernel,
        scalars(flags) + hbm(keys, selection, w3, kv)
        + near(band, edge_a, edge_b, corner_a, corner_b, gain_near, qhat_near, dout),
        near(like(TOKENS, D), side_like, side_like)
        + hbm(like(STEPS, 2, HALO_ROWS, QUAD), stat_like, like(HALO_QUERIES, D), like(2 * SIDE, D),
              like(STEPS, 2, STACK, SPAN), quads),
        [vmem(1, 8, KEYS, dtype=jnp.int32), vmem(*picks_shape), vmem(STEPS, D, 2 * QUAD), kv_scratch, vmem(STEPS, 2, HALO_ROWS, QUAD),
         vmem(TOKENS, STATS, dtype=F32),
         vmem(HALO_ROWS, D), vmem(2 * SIDE, D), vmem(STEPS, 2, STACK, SPAN), vmem(STEPS, TOKENS, QUAD),
         vmem(2, HALF, SPAN, dtype=F32), vmem(2, KEYS, QUAD), vmem(2, KEYS, QUAD), vmem(STEPS, TOKENS, QUAD, dtype=F32),
         sems(2 + 3 * STEPS + 4 * STEPS + 3)],
        limit=24, flops=2 * 1024 * 1024 * 2000, name="attention_forward",
    )
    stat_b = lax.ppermute(stat_b, "lon", side_b)
    stat_a = lax.ppermute(stat_a, "lon", side_a)

    (going,) = call(
        output_kernel,
        scalars(column_group_decoder_longitude) + near(x_near, mixed, wo_near),
        hbm(like(count, cap, SEG, D)),
        [vmem(TOKENS, D, dtype=F32), vmem(count, cap, SEG, D), pltpu.SMEM((count,), jnp.int32), sems(1)],
        limit=24, flops=2 * 1024 * 1024 * 200, name="output_segments",
    )
    going, stat_a, stat_b = lax.optimization_barrier((going, stat_a, stat_b))
    arrived = lax.all_to_all(going, "lon", split_axis=0, concat_axis=0, tiled=True)

    (message,) = call(
        message_kernel,
        hbm(up, up_halo, stat, stat_a, stat_b),
        near(like(PAD_SIDE, MESSAGE)),
        [vmem(BAND, D), vmem(2 * SIDE, D), vmem(BAND, STATS, dtype=F32), vmem(SIDE, STATS, dtype=F32), vmem(SIDE, STATS, dtype=F32),
         sems(5)],
        limit=24, flops=1024, name="boundary_message",
    )
    message = lax.ppermute(message, "lat", [(0, 1), (1, 0)])

    handed = call(
        query_kernel,
        scalars(score_sharpness, flags)
        + hbm(xn_halo, up_halo, keys, w3, wo, qhat, kv, halo_kv, weights, dprime, rawq, rawk, stat, stat_a, stat_b),
        near(like(TOKENS, D, dtype=F32), like(STEPS, SPAN, QUAD), like(STEPS, MIDDLE, QUAD), like(STEPS, 2, HALF, QUAD, dtype=F32),
             like(2, HALF, SPAN, dtype=F32), like(D, D), like(D, D), like(D, D), kv_like, quads, like(STATS, MIDDLE, dtype=F32)),
        [vmem(HALO_QUERIES, D), vmem(2 * SIDE, D), vmem(1, 8, KEYS, dtype=jnp.int32), vmem(D, D),
         vmem(STEPS, TOKENS, QUAD), vmem(STEPS, 2, HALO_ROWS, QUAD), vmem(STEPS, 2, STACK, SPAN), vmem(STEPS, TOKENS, QUAD),
         vmem(STEPS, TOKENS, QUAD), vmem(TOKENS, STATS, dtype=F32), vmem(SIDE, STATS, dtype=F32),
         vmem(SIDE, STATS, dtype=F32), vmem(2, KEYS, QUAD), vmem(2, KEYS, QUAD), vmem(2, TOKENS, QUAD, dtype=F32),
         vmem(HALO_QUERIES, D, dtype=F32), vmem(2 * SIDE, D), vmem(TOKENS, D), sems(4 + 6 * STEPS + 4 + 3)],
        limit=24, flops=2 * 1024 * 1024 * 4000, name="query_gradient",
    )

    (input_grad,) = call(
        key_kernel,
        hbm(x, up, gain) + near(*handed, message),
        hbm(like(TOKENS, D)),
        [vmem(TOKENS, D), vmem(TOKENS, D), vmem(1, D, dtype=F32), vmem(TOKENS, D), vmem(STATS, SPAN, dtype=F32),
         vmem(2, SPAN, QUAD), vmem(2, TOKENS, QUAD, dtype=F32), vmem(PAD_SIDE, D), vmem(TOKENS, D), vmem(TOKENS, D), sems(7)],
        limit=24, flops=2 * 1024 * 1024 * 2000, name="key_gradient",
    )
    return (
        arrived.reshape(1, 1, count, cap, SEG, D),
        input_grad.reshape(ROWS, COLS, D),
    )


def solution(mesh):
    return jax.shard_map(
        per_device,
        mesh=mesh,
        in_specs=(
            P("lat", "lon", None),
            P("lat", "lon", None),
            P(None, None, "lon", None),
            P(),
            P(),
            P(),
            P(),
            P(),
            P("lat", "lon"),
        ),
        out_specs=(P("lat", "lon", None, None, None, None), P("lat", "lon", None)),
        check_vma=False,
    )
```

```python
import functools

import jax
import jax.numpy as jnp
import numpy as np
from jax import lax
from jax.experimental import pallas as pl
from jax.experimental.pallas import tpu as pltpu
from jax.sharding import PartitionSpec as P

HEADS = 16
HALO = 6
ROWS = 12
COLS = 16
SEG = 4
D = 1024
HEAD_DIM = D // HEADS
TOKENS = ROWS * COLS
HALF = TOKENS // 2
BAND = HALO * COLS
SIDE = ROWS * HALO
CORNER = 40
QUAD = 256
QUAD_HEADS = QUAD // HEAD_DIM
STEPS = D // QUAD
STACK = QUAD_HEADS * HALF
PAD_SIDE = BAND + 2 * CORNER
MIDDLE = TOKENS + 2 * SIDE
SPAN = PAD_SIDE + MIDDLE
KEYS = SPAN + PAD_SIDE
HALO_ROWS = 2 * PAD_SIDE + 2 * SIDE - BAND
HALO_QUERIES = PAD_SIDE + 2 * SIDE
EDGE = SIDE + CORNER
STATS = 128
MESSAGE = D + STATS
MIB = 1024 * 1024
BF = jnp.bfloat16
F32 = jnp.float32


def dot(a, b):
    return jnp.dot(a, b, preferred_element_type=F32)


def dot_nt(a, b):
    return lax.dot_general(a, b, (((1,), (1,)), ((), ())), preferred_element_type=F32)


def dot_tn(a, b):
    return lax.dot_general(a, b, (((0,), (0,)), ((), ())), preferred_element_type=F32)


def first_column(side, parity):
    return COLS - HALO if side == parity else 0


def inner_row(lat, row):
    return (row + HALO * (1 - lat)) % ROWS


def selection_table():
    table = np.zeros((4, 2 * EDGE + 2 * CORNER, TOKENS + BAND), np.float32)
    for lat in range(2):
        for parity in range(2):
            for side in range(2):
                first, base = first_column(side, parity), side * EDGE
                picks = table[2 * lat + parity]
                for c in range(HALO):
                    for r in range(ROWS):
                        picks[base + r * HALO + c, inner_row(lat, r) * COLS + first + c] = 1
                    for i in range(HALO):
                        picks[base + SIDE + i * HALO + c, TOKENS + i * COLS + first + c] = 1
                        row = i + HALO * (1 - lat)
                        picks[2 * EDGE + side * CORNER + i * HALO + c, inner_row(lat, row) * COLS + first + c] = 1
    return table


def key_table():
    table = np.full((4, 8, KEYS), 1000, np.int32)
    table[:, 2] = -1
    for lat in range(2):
        for parity in range(2):
            picks = table[2 * lat + parity]
            low = {"lat": ROWS if lat == 0 else -HALO, "own": 0, "rim": -HALO if lat == 0 else ROWS}

            def put(at, count, width, first_col, kind):
                for k in range(count * width):
                    i, c = divmod(k, width)
                    picks[0, at + k] = low[kind] + i
                    picks[1, at + k] = first_col + c
                    if kind == "rim":
                        picks[2, at + k] = i

            put(0, HALO, COLS, 0, "lat")
            put(PAD_SIDE, ROWS, COLS, 0, "own")
            picks[0, PAD_SIDE : PAD_SIDE + TOKENS] = np.repeat([r for _, r in sorted((inner_row(lat, r), r) for r in range(ROWS))], COLS)
            put(SPAN, HALO, COLS, 0, "rim")
            for side in range(2):
                col = COLS if side == parity else -HALO
                put(BAND + side * CORNER, HALO, HALO, col, "lat")
                put(PAD_SIDE + TOKENS + side * SIDE, ROWS, HALO, col, "own")
                put(SPAN + BAND + side * CORNER, HALO, HALO, col, "rim")
    return table


def head_mask(h, dtype):
    lane = lax.broadcasted_iota(jnp.int32, (1, QUAD), 1)
    return jnp.where(lane // HEAD_DIM == h, 1.0, 0.0).astype(dtype)


def head_mean(values):
    a = lax.broadcasted_iota(jnp.int32, (QUAD, QUAD), 0) // HEAD_DIM
    b = lax.broadcasted_iota(jnp.int32, (QUAD, QUAD), 1) // HEAD_DIM
    block = jnp.where(a == b, 1.0 / HEAD_DIM, 0.0).astype(BF)
    return dot(values.astype(BF), block)


def unit(raw):
    return raw * lax.rsqrt(head_mean(raw * raw) + 1e-06)


def unit_back(raw, grad):
    raw = raw.astype(F32)
    inverse = lax.rsqrt(head_mean(raw * raw) + 1e-06)
    value = raw * inverse
    return inverse * (grad - value * head_mean(value * grad))


def normed(tokens, gain):
    tokens = tokens.astype(F32)
    return tokens * lax.rsqrt(jnp.mean(tokens * tokens, axis=-1, keepdims=True) + 1e-05) * gain


def multiplier(sharp_ref, j):
    out = jnp.zeros((1, QUAD), F32)
    for h in range(QUAD_HEADS):
        out = out + head_mask(h, F32) * (sharp_ref[j * QUAD_HEADS + h] / HEAD_DIM)
    return out


def stacked(block):
    return jnp.concatenate([block * head_mask(h, BF) for h in range(QUAD_HEADS)], axis=0)


def unstacked(stack):
    out = stack[:HALF] * head_mask(0, F32)
    for h in range(1, QUAD_HEADS):
        out = out + stack[h * HALF : (h + 1) * HALF] * head_mask(h, F32)
    return out


def repeated(block):
    return jnp.concatenate([block] * QUAD_HEADS, axis=0)


def head_lanes(first, pick_one):
    a = lax.broadcasted_iota(jnp.int32, (QUAD, STATS), 0)
    b = lax.broadcasted_iota(jnp.int32, (QUAD, STATS), 1)
    hit = b == a // HEAD_DIM + first
    if pick_one:
        hit = hit & (a % HEAD_DIM == 0)
    return jnp.where(hit, 1.0, 0.0).astype(BF)


def spread(stat, j):
    a = lax.broadcasted_iota(jnp.int32, (STATS, QUAD), 0)
    b = lax.broadcasted_iota(jnp.int32, (STATS, QUAD), 1)
    picks = jnp.where(a == b // HEAD_DIM + j * QUAD_HEADS, 1.0, 0.0).astype(BF)
    return dot(stat.astype(BF), picks)


def where():
    lat = lax.axis_index("lat")
    return lat, 2 * lat + lax.axis_index("lon") % 2


def half_start(lat, half):
    return pl.multiple_of(HALF * ((1 - lat) if half == 0 else lat), 16)


def near_mask(mask_ref, tab_ref, flag_ref, lat):
    rows, cols, place = tab_ref[0, 0:1], tab_ref[0, 1:2], tab_ref[0, 2:3]
    keep = jnp.where(place < 0, 1.0, 0.0)
    for i in range(HALO):
        keep = keep + jnp.where(place == i, flag_ref[lat, i].astype(F32), 0.0)
    for half in range(2):
        at = half * PAD_SIDE
        token = lax.broadcasted_iota(jnp.int32, (HALF, SPAN), 0) + half_start(lat, half)
        near = (jnp.abs(rows[:, at : at + SPAN] - token // COLS) <= HALO) & (
            jnp.abs(cols[:, at : at + SPAN] - token % COLS) <= HALO
        )
        mask_ref[half] = jnp.where(near, keep[:, at : at + SPAN], 0.0)


def lay_keys(ref, own, halo):
    ref[:PAD_SIDE] = halo[:PAD_SIDE]
    ref[PAD_SIDE : PAD_SIDE + TOKENS] = own[:TOKENS]
    ref[PAD_SIDE + TOKENS : SPAN] = halo[PAD_SIDE:HALO_QUERIES]
    ref[SPAN : SPAN + BAND] = own[TOKENS:]
    ref[SPAN + BAND :] = halo[HALO_QUERIES:]


class Copies:
    def __init__(self, sems):
        self.sems, self.used = sems, 0

    def start(self, source, target):
        copy = pltpu.make_async_copy(source, target, self.sems.at[self.used])
        self.used += 1
        copy.start()
        return copy

    def load_tokens(self, hbm, ref, lat):
        return [self.start(hbm.at[pl.ds(half_start(lat, k), HALF)], ref.at[pl.ds(k * HALF, HALF)]) for k in range(2)]

    def store_tokens(self, ref, hbm, lat):
        return [self.start(ref.at[pl.ds(k * HALF, HALF)], hbm.at[pl.ds(half_start(lat, k), HALF)]) for k in range(2)]

    def by_step(self, pairs):
        base, width = self.used, len(pairs(0))
        self.used += STEPS * width

        def copies(j):
            return [pltpu.make_async_copy(a, b, self.sems.at[base + j * width + k]) for k, (a, b) in enumerate(pairs(j))]

        def start(j):
            for copy in copies(j):
                copy.start()

        def wait(j):
            for copy in copies(j):
                copy.wait()

        return start, wait


def wait_all(copies):
    for copy in copies:
        copy.wait()


def lane_block(at, j):
    return pl.ds(pl.multiple_of((at + j) * QUAD, QUAD), QUAD)


def rows_at(j):
    return pl.ds(j * QUAD, QUAD)


def pack_kernel(
    x_hbm, up_hbm, rim_hbm, sel_hbm, edge_a_ref, edge_b_ref, band_ref, corner_a_ref, corner_b_ref,
    x_ref, up_ref, rim_ref, sel_ref, sems,
):
    lat, spot = where()
    copies = Copies(sems)
    loads = copies.load_tokens(x_hbm, x_ref, lat)
    loads += [copies.start(sel_hbm.at[spot], sel_ref), copies.start(rim_hbm.at[lat], rim_ref)]
    loads += copies.load_tokens(up_hbm, up_ref, lat)
    wait_all(loads)
    band_ref[...] = x_ref[:BAND]
    picks = sel_ref[...]
    features = dot(picks, jnp.concatenate([x_ref[...], rim_ref[...]], axis=0))
    grads = dot(picks[: 2 * EDGE, :TOKENS], up_ref[...])
    for side, (ref, corner_ref) in enumerate(((edge_a_ref, corner_a_ref), (edge_b_ref, corner_b_ref))):
        at = side * EDGE
        ref[...] = jnp.concatenate([features[at : at + EDGE], grads[at : at + SIDE]], axis=0).astype(BF)
        at = 2 * EDGE + side * CORNER
        corner_ref[...] = features[at : at + CORNER].astype(BF)


def own_kernel(
    sharp_ref, x_hbm, rim_hbm, up_hbm, gain_hbm, w3_hbm, wo_hbm,
    qhat_ref, dout_ref, wo_ref, x_ref, gain_ref, qhat_hbm, rawq_hbm, rawk_hbm, kv_hbm,
    kv_ref, w3_ref, rim_ref, up_ref, rawq_ref, rawk_ref, xn_ref, sems,
):
    copies = Copies(sems)
    lat, spot = where()
    loads = copies.load_tokens(x_hbm, x_ref, lat) + [copies.start(rim_hbm.at[lat], rim_ref), copies.start(gain_hbm, gain_ref)]
    start, wait = copies.by_step(
        lambda j: [(w3_hbm.at[:, lane_block(k * STEPS, j)], w3_ref.at[j, :, pl.ds(k * QUAD, QUAD)]) for k in range(3)]
    )
    for j in range(STEPS):
        start(j)
    grad_loads = copies.load_tokens(up_hbm, up_ref, lat) + [copies.start(wo_hbm, wo_ref)]
    outputs = [(qhat_ref, qhat_hbm), (rawq_ref, rawq_hbm), (rawk_ref, rawk_hbm), (kv_ref, kv_hbm)]
    store, stored = copies.by_step(lambda j: [(ref.at[j], hbm.at[j]) for ref, hbm in outputs])
    wait_all(loads)
    xn_ref[:TOKENS] = normed(x_ref[...], gain_ref[...]).astype(BF)
    xn_ref[TOKENS:] = normed(rim_ref[...], gain_ref[...]).astype(BF)
    for j in range(STEPS):
        wait(j)
        raw = dot(xn_ref[...], w3_ref[j])
        raw_q, raw_k = raw[:TOKENS, :QUAD], raw[:, QUAD : 2 * QUAD]
        units = unit(jnp.concatenate([raw_q, raw_k], axis=0))
        rawq_ref[j] = raw_q.astype(BF)
        rawk_ref[j] = raw_k[:TOKENS].astype(BF)
        qhat_ref[j] = (units[:TOKENS] * multiplier(sharp_ref, j)).astype(BF)
        kv_ref[j, 0] = units[TOKENS:].astype(BF)
        kv_ref[j, 1] = raw[:, 2 * QUAD :].astype(BF)
        store(j)
    wait_all(grad_loads)
    dout = dot_nt(up_ref[...], wo_ref[...]).astype(BF)
    for j in range(STEPS):
        dout_ref[j] = dout[:, j * QUAD : (j + 1) * QUAD]
    for j in range(STEPS):
        stored(j)


def forward_kernel(
    flag_ref, tab_hbm, sel_hbm, w3_hbm, kv_hbm, band_ref, edge_a_ref, edge_b_ref, corner_a_ref, corner_b_ref, gain_ref,
    qhat_ref, dout_ref,
    mixed_ref, stat_a_ref, stat_b_ref, halo_hbm, stat_hbm, xn_hbm, upn_hbm, weight_hbm, dprime_hbm,
    tab_ref, sel_ref, wkv_ref, kv_ref, halo_ref, stat_ref, xn_ref, upn_ref, weight_ref, dprime_ref, mask_ref, key_ref, value_ref, linv_ref, sems,
):
    lat, spot = where()
    copies = Copies(sems)
    loads = [copies.start(tab_hbm.at[spot], tab_ref.at[0])]
    start, wait = copies.by_step(
        lambda j: [(w3_hbm.at[:, lane_block(k * STEPS, j)], wkv_ref.at[j, :, pl.ds((k - 1) * QUAD, QUAD)]) for k in (1, 2)]
    )
    start_kv, wait_kv = copies.by_step(lambda j: [(kv_hbm.at[j], kv_ref.at[j])])
    for j in range(STEPS):
        start(j)
        start_kv(j)
    loads.append(copies.start(sel_hbm.at[spot], sel_ref))
    store, stored = copies.by_step(
        lambda j: [(halo_ref.at[j], halo_hbm.at[j]), (dprime_ref.at[j], dprime_hbm.at[j])]
    )
    weight_stores = []
    gain = gain_ref[...]
    edge_a, edge_b = edge_a_ref[...].astype(F32), edge_b_ref[...].astype(F32)
    pieces = [ref[...].astype(F32) for ref in (band_ref, corner_a_ref, corner_b_ref)]
    pieces += [edge_a[:SIDE], edge_b[:SIDE], edge_a[SIDE:EDGE], edge_b[SIDE:EDGE]]
    xn_ref[...] = normed(jnp.concatenate(pieces, axis=0), gain).astype(BF)
    upn_ref[...] = jnp.concatenate([edge_a[EDGE:], edge_b[EDGE:]], axis=0).astype(BF)
    stores = [copies.start(xn_ref.at[pl.ds(0, HALO_QUERIES)], xn_hbm), copies.start(upn_ref, upn_hbm)]
    loads[0].wait()
    near_mask(mask_ref, tab_ref, flag_ref, lat)
    stat = jnp.zeros((TOKENS, STATS), F32)
    for j in range(STEPS):
        wait(j)
        raw = dot(xn_ref[...], wkv_ref[j])
        halo_k = unit(raw[:, :QUAD]).astype(BF)
        halo_v = raw[:, QUAD:].astype(BF)
        halo_ref[j, 0] = halo_k
        halo_ref[j, 1] = halo_v
        wait_kv(j)
        lay_keys(key_ref.at[j % 2], kv_ref[j, 0], halo_k)
        lay_keys(value_ref.at[j % 2], kv_ref[j, 1], halo_v)
        for half in range(2):
            at, piece = half * PAD_SIDE, slice(half * HALF, (half + 1) * HALF)
            scores = dot_nt(stacked(qhat_ref[j, piece, :]), key_ref[j % 2, at : at + SPAN])
            weights = jnp.exp(scores) * repeated(mask_ref[half])
            inverse = jnp.broadcast_to(1.0 / jnp.sum(weights, axis=-1, keepdims=True), (STACK, QUAD))
            weights = weights.astype(BF)
            weight_ref[j, half] = weights
            weight_stores.append(copies.start(weight_ref.at[j, half], weight_hbm.at[j, half]))
            mixed = unstacked(dot(weights, value_ref[j % 2, at : at + SPAN]) * inverse)
            mixed_ref[piece, rows_at(j)] = mixed.astype(BF)
            linv_ref[j, piece, :] = unstacked(inverse)
        dprime = (dout_ref[j].astype(F32) * linv_ref[j]).astype(BF)
        dprime_ref[j] = dprime
        inner = dprime.astype(F32) * mixed_ref[:, rows_at(j)].astype(F32)
        stat = stat + dot(linv_ref[j].astype(BF), head_lanes(j * QUAD_HEADS, True))
        stat = stat + dot(inner.astype(BF), head_lanes(HEADS + j * QUAD_HEADS, False))
        store(j)
    stat_ref[...] = stat
    stores.append(copies.start(stat_ref, stat_hbm))
    loads[1].wait()
    picked = dot(sel_ref[: 2 * EDGE, :TOKENS], stat.astype(BF))
    stat_a_ref[...] = picked[:SIDE]
    stat_b_ref[...] = picked[EDGE : EDGE + SIDE]
    for j in range(STEPS):
        stored(j)
    wait_all(stores + weight_stores)


def output_kernel(owner_ref, x_ref, mixed_ref, wo_ref, going_hbm, acc_ref, going_ref, count_ref, sems):
    lat, spot = where()
    rows = x_ref[...].astype(F32) + dot(mixed_ref[...], wo_ref[...])
    for half in range(2):
        acc_ref[pl.ds(half_start(lat, half), HALF), :] = rows[half * HALF : (half + 1) * HALF]
    going_ref[...] = jnp.zeros_like(going_ref)
    for o in range(going_ref.shape[0]):
        count_ref[o] = 0
    for s in range(TOKENS // SEG):
        owner = owner_ref[s // (COLS // SEG), s % (COLS // SEG)]
        slot = count_ref[owner]
        count_ref[owner] = slot + 1
        going_ref[owner, slot] = acc_ref[s * SEG : (s + 1) * SEG, :].astype(BF)
    Copies(sems).start(going_ref, going_hbm).wait()


def message_kernel(
    up_hbm, upn_hbm, stat_hbm, stat_a_hbm, stat_b_hbm, out_ref, up_ref, upn_ref, stat_ref, stat_a_ref, stat_b_ref, sems
):
    lat, spot = where()
    piece = pl.ds(half_start(lat, 0), BAND)
    copies = Copies(sems)
    wait_all(
        [
            copies.start(hbm, ref)
            for hbm, ref in (
                (up_hbm.at[piece], up_ref), (upn_hbm, upn_ref), (stat_hbm.at[pl.ds(0, BAND)], stat_ref), (stat_a_hbm, stat_a_ref),
                (stat_b_hbm, stat_b_ref),
            )
        ]
    )
    a = lax.broadcasted_iota(jnp.int32, (2 * CORNER, 2 * SIDE), 0)
    b = lax.broadcasted_iota(jnp.int32, (2 * CORNER, 2 * SIDE), 1)
    side, inside = a // CORNER, HALO * HALO
    row = a - side * CORNER
    picks = jnp.where((b == row + inside * (1 - lat) + side * SIDE) & (row < inside), 1.0, 0.0).astype(BF)
    out_ref[:BAND, :D] = up_ref[...]
    out_ref[BAND:, :D] = dot(picks, upn_ref[...]).astype(BF)
    edges = jnp.concatenate([stat_a_ref[...], stat_b_ref[...]], axis=0).astype(BF)
    out_ref[:BAND, D:] = stat_ref[...].astype(BF)
    out_ref[BAND:, D:] = dot(picks, edges).astype(BF)


def inner_rows(row_ref, j):
    row = HEADS + j * QUAD_HEADS
    width = row_ref.shape[1]
    parts = [jnp.broadcast_to(row_ref[row + h : row + h + 1, :], (HALF, width)) for h in range(QUAD_HEADS)]
    return jnp.concatenate(parts, axis=0)


def key_pass(keys, values, queries, grads, mask, inner):
    weights = jnp.exp(dot_nt(stacked(keys), queries)) * repeated(mask)
    grad_scores = weights * (dot_nt(stacked(values), grads) - inner)
    return unstacked(dot(grad_scores.astype(BF), queries)), unstacked(dot(weights.astype(BF), grads))


def query_kernel(
    sharp_ref, flag_ref, xn_hbm, upn_hbm, tab_hbm, w3_hbm, wo_hbm, qhat_hbm, kv_hbm, halo_hbm, weight_hbm, dprime_hbm,
    rawq_hbm, rawk_hbm, stat_hbm, stat_a_hbm, stat_b_hbm,
    gqn_ref, query_ref, grad_ref, far_ref, mask_ref, wkv_ref, wo_ref, kv_ref, rawk_ref, row_ref,
    xn_ref, upn_ref, tab_ref, wq_ref, qhat_ref, halo_ref, weight_ref, dprime_ref, rawq_ref, stat_ref, stat_a_ref, stat_b_ref,
    key_ref, value_ref, dq_ref, raw_ref, dout_ref, grad_q_ref, sems,
):
    lat, spot = where()
    copies = Copies(sems)
    early = [
        copies.start(hbm, ref)
        for hbm, ref in (
            (tab_hbm.at[spot], tab_ref.at[0]), (stat_hbm, stat_ref), (stat_a_hbm, stat_a_ref), (stat_b_hbm, stat_b_ref),
        )
    ]
    first = [copies.start(xn_hbm, xn_ref)]
    pieces = [pl.ds(k * D // 2, D // 2) for k in range(2)]
    query_loads = [copies.start(w3_hbm.at[:, piece], wq_ref.at[:, piece]) for piece in pieces]
    first.append(copies.start(upn_hbm, upn_ref))
    output_load = copies.start(wo_hbm, wo_ref)
    start, wait = copies.by_step(
        lambda j: [
            (qhat_hbm.at[j], qhat_ref.at[j]),
            (dprime_hbm.at[j], dprime_ref.at[j]),
            (kv_hbm.at[j], kv_ref.at[j]),
            (halo_hbm.at[j], halo_ref.at[j]),
            (weight_hbm.at[j], weight_ref.at[j]),
            (rawq_hbm.at[j], rawq_ref.at[j]),
        ]
    )
    start(0)
    for j in range(1, STEPS):
        start(j)
    later = [
        copies.start(rawk_hbm, rawk_ref),
        copies.start(w3_hbm.at[:, pl.ds(D, 2 * D)], wkv_ref),
    ]
    wait_all(early)
    near_mask(mask_ref, tab_ref, flag_ref, lat)
    edges = jnp.concatenate([stat_a_ref[...], stat_b_ref[...]], axis=0)
    row_ref[...] = jnp.concatenate([stat_ref[...], edges], axis=0).T
    wait_all(first)
    for piece, load in zip(pieces, query_loads):
        load.wait()
        raw_ref[:, piece] = dot(xn_ref[...], wq_ref[:, piece])
    output_load.wait()
    dout_ref[...] = dot_nt(upn_ref[...], wo_ref[...]).astype(BF)
    for j in range(STEPS):
        halo_q = (unit(raw_ref[:, rows_at(j)]) * multiplier(sharp_ref, j)).astype(BF)
        query_ref[j, :PAD_SIDE] = halo_q[:PAD_SIDE]
        query_ref[j, PAD_SIDE + TOKENS :] = halo_q[PAD_SIDE:]
        grad_ref[j, TOKENS:] = (dout_ref[:, rows_at(j)].astype(F32) * spread(edges, j)).astype(BF)
        wait(j)
        query_ref[j, PAD_SIDE : PAD_SIDE + TOKENS] = qhat_ref[j]
        grad_ref[j, :TOKENS] = dprime_ref[j]
        lay_keys(key_ref.at[j % 2], kv_ref[j, 0], halo_ref[j, 0])
        lay_keys(value_ref.at[j % 2], kv_ref[j, 1], halo_ref[j, 1])
        for half in range(2):
            at, piece = half * PAD_SIDE, slice(half * HALF, (half + 1) * HALF)
            stat = stat_ref[piece, :]
            lane = HEADS + j * QUAD_HEADS
            inner = jnp.concatenate([stat[:, lane + h : lane + h + 1] for h in range(QUAD_HEADS)], axis=0)
            grad_probs = dot_nt(stacked(dprime_ref[j, piece, :]), value_ref[j % 2, at : at + SPAN])
            grad_scores = weight_ref[j, half].astype(F32) * (grad_probs - inner)
            dq_ref[j % 2, piece, :] = unstacked(dot(grad_scores.astype(BF), key_ref[j % 2, at : at + SPAN]))
        piece = slice(HALF, TOKENS)
        far_ref[j, 0], far_ref[j, 1] = key_pass(
            kv_ref[j, 0, piece, :], kv_ref[j, 1, piece, :], query_ref[j, PAD_SIDE:], grad_ref[j], mask_ref[1, :, :MIDDLE],
            inner_rows(row_ref, j),
        )
        grad_q = unit_back(rawq_ref[j], dq_ref[j % 2] * multiplier(sharp_ref, j))
        grad_q_ref[:, rows_at(j)] = grad_q.astype(BF)
    gqn_ref[...] = dot_nt(grad_q_ref[...], wq_ref[...])
    wait_all(later)


def key_kernel(
    x_hbm, up_hbm, gain_hbm, gqn_ref, query_ref, grad_ref, far_ref, mask_ref, wkv_ref, wo_ref, kv_ref, rawk_ref, row_ref,
    message_ref,
    out_hbm,
    x_ref, up_ref, gain_ref, out_ref, all_row_ref, all_ref, dk_ref, dout_ref, grad_kv_ref, sems,
):
    lat, spot = where()
    copies = Copies(sems)
    loads = copies.load_tokens(x_hbm, x_ref, lat) + copies.load_tokens(up_hbm, up_ref, lat)
    loads.append(copies.start(gain_hbm, gain_ref))
    message = message_ref[:, D:].astype(F32)
    all_row_ref[...] = jnp.concatenate([message.T, row_ref[...]], axis=1)
    dout_ref[...] = dot_nt(message_ref[:, :D], wo_ref[...]).astype(BF)
    for j in range(STEPS):
        slot = j % 2
        all_ref[slot, :PAD_SIDE] = (dout_ref[:, rows_at(j)].astype(F32) * spread(message, j)).astype(BF)
        all_ref[slot, PAD_SIDE:] = grad_ref[j]
        dk_ref[slot, :HALF, :], near_dv = key_pass(
            kv_ref[j, 0, :HALF, :], kv_ref[j, 1, :HALF, :], query_ref[j], all_ref[slot], mask_ref[0], inner_rows(all_row_ref, j)
        )
        dk_ref[slot, HALF:, :] = far_ref[j, 0]
        grad_kv_ref[:, rows_at(j)] = unit_back(rawk_ref[j], dk_ref[slot]).astype(BF)
        grad_kv_ref[:HALF, rows_at(STEPS + j)] = near_dv.astype(BF)
        grad_kv_ref[HALF:, rows_at(STEPS + j)] = far_ref[j, 1].astype(BF)
    total = gqn_ref[...] + dot_nt(grad_kv_ref[...], wkv_ref[...])
    wait_all(loads)
    tokens = x_ref[...].astype(F32)
    inverse = lax.rsqrt(jnp.mean(tokens * tokens, axis=-1, keepdims=True) + 1e-05)
    grad = total * gain_ref[...]
    value = tokens * inverse
    back = inverse * (grad - value * jnp.mean(value * grad, axis=-1, keepdims=True))
    out_ref[...] = (up_ref[...].astype(F32) + back).astype(BF)
    wait_all(copies.store_tokens(out_ref, out_hbm, lat))


def call(kernel, inputs, outputs, scratch=(), limit=32, flops=0, name=None):
    def specs(pairs):
        return [pl.BlockSpec(memory_space=space) for space, _ in pairs]

    def placed(space, array):
        return array if space == pltpu.SMEM else pltpu.with_memory_space_constraint(array, space)

    return pl.pallas_call(
        kernel,
        in_specs=specs(inputs),
        out_specs=specs(outputs),
        out_shape=[space(shape.shape, shape.dtype) for space, shape in outputs],
        scratch_shapes=list(scratch),
        compiler_params=pltpu.CompilerParams(vmem_limit_bytes=limit * MIB),
        cost_estimate=pl.CostEstimate(flops=flops, bytes_accessed=8 << 20, transcendentals=0),
        name=name,
    )(*[placed(space, array) for space, array in inputs])


def hbm(*arrays):
    return [(pltpu.HBM, array) for array in arrays]


def near(*arrays):
    return [(pltpu.VMEM, array) for array in arrays]


def scalars(*arrays):
    return [(pltpu.SMEM, array) for array in arrays]


def like(*shape, dtype=BF):
    return jax.ShapeDtypeStruct(shape, dtype)


def partners(count):
    return (
        [(i, i + 1 - 2 * (i % 2)) for i in range(count)],
        [(i, (i - 1 + 2 * (i % 2)) % count) for i in range(count)],
    )


def across(pairs):
    return [(2 * a + lat, 2 * b + 1 - lat) for a, b in pairs for lat in range(2)]


def per_device(
    slab_features, upstream_gradient, rim_feature_rows, rim_presence_flags, feature_rescaling_coefficients,
    triple_projection_matrix, final_projection_matrix, score_sharpness, column_group_decoder_longitude,
):
    count = lax.axis_size("lon")
    cap = max(2, (2 * (TOKENS // SEG) + count - 1) // count)
    x = slab_features.reshape(TOKENS, D)
    up = upstream_gradient.reshape(TOKENS, D)
    rim = rim_feature_rows.reshape(2, BAND, D)
    gain = feature_rescaling_coefficients.reshape(1, D)
    w3, wo = triple_projection_matrix, final_projection_matrix
    table = selection_table()
    selection = jnp.asarray(table, BF)
    keys = jnp.asarray(key_table())
    flags = rim_presence_flags

    side_a, side_b = partners(count)

    def vmem(*shape, dtype=BF):
        return pltpu.VMEM(shape, dtype)

    def sems(n):
        return pltpu.SemaphoreType.DMA((n,))

    picks_shape = table.shape[1:]
    edge_a, edge_b, band, corner_a, corner_b = call(
        pack_kernel,
        hbm(x, up, rim, selection),
        near(like(EDGE + SIDE, D), like(EDGE + SIDE, D), like(BAND, D), like(CORNER, D), like(CORNER, D)),
        [vmem(TOKENS, D), vmem(TOKENS, D), vmem(BAND, D), vmem(*picks_shape), sems(6)],
        limit=24, name="edge_tokens",
    )
    band = lax.ppermute(band, "lat", [(0, 1), (1, 0)])
    corner_a = lax.ppermute(corner_a, ("lon", "lat"), across(side_a))
    corner_b = lax.ppermute(corner_b, ("lon", "lat"), across(side_b))
    edge_b = lax.ppermute(edge_b, "lon", side_b)
    edge_a = lax.ppermute(edge_a, "lon", side_a)

    quads = like(STEPS, TOKENS, QUAD)
    kv_like = like(STEPS, 2, TOKENS + BAND, QUAD)
    qhat_near, dout, wo_near, x_near, gain_near, qhat, rawq, rawk, kv = call(
        own_kernel,
        scalars(score_sharpness) + hbm(x, rim, up, gain, w3, wo),
        near(quads, quads, like(D, D), like(TOKENS, D), like(1, D, dtype=F32))
        + hbm(quads, quads, quads, kv_like),
        [vmem(STEPS, 2, TOKENS + BAND, QUAD), vmem(STEPS, D, 3 * QUAD), vmem(BAND, D), vmem(TOKENS, D),
         vmem(STEPS, TOKENS, QUAD), vmem(STEPS, TOKENS, QUAD), vmem(TOKENS + BAND, D), sems(6 + 4 * STEPS + 4 * STEPS)],
        limit=24, flops=2 * 1024 * 1024 * (192 * 2 + 288 * 2), name="own_projections",
    )

    kv_scratch = vmem(STEPS, 2, TOKENS + BAND, QUAD)
    stat_like, side_like = like(TOKENS, STATS, dtype=F32), like(SIDE, STATS, dtype=F32)
    mixed, stat_a, stat_b, halo_kv, stat, xn_halo, up_halo, weights, dprime = call(
        forward_kernel,
        scalars(flags) + hbm(keys, selection, w3, kv)
        + near(band, edge_a, edge_b, corner_a, corner_b, gain_near, qhat_near, dout),
        near(like(TOKENS, D), side_like, side_like)
        + hbm(like(STEPS, 2, HALO_ROWS, QUAD), stat_like, like(HALO_QUERIES, D), like(2 * SIDE, D),
              like(STEPS, 2, STACK, SPAN), quads),
        [vmem(1, 8, KEYS, dtype=jnp.int32), vmem(*picks_shape), vmem(STEPS, D, 2 * QUAD), kv_scratch, vmem(STEPS, 2, HALO_ROWS, QUAD),
         vmem(TOKENS, STATS, dtype=F32),
         vmem(HALO_ROWS, D), vmem(2 * SIDE, D), vmem(STEPS, 2, STACK, SPAN), vmem(STEPS, TOKENS, QUAD),
         vmem(2, HALF, SPAN, dtype=F32), vmem(2, KEYS, QUAD), vmem(2, KEYS, QUAD), vmem(STEPS, TOKENS, QUAD, dtype=F32),
         sems(2 + 3 * STEPS + 4 * STEPS + 3)],
        limit=24, flops=2 * 1024 * 1024 * 2000, name="attention_forward",
    )
    stat_b = lax.ppermute(stat_b, "lon", side_b)
    stat_a = lax.ppermute(stat_a, "lon", side_a)

    (going,) = call(
        output_kernel,
        scalars(column_group_decoder_longitude) + near(x_near, mixed, wo_near),
        hbm(like(count, cap, SEG, D)),
        [vmem(TOKENS, D, dtype=F32), vmem(count, cap, SEG, D), pltpu.SMEM((count,), jnp.int32), sems(1)],
        limit=24, flops=2 * 1024 * 1024 * 200, name="output_segments",
    )
    going, stat_a, stat_b = lax.optimization_barrier((going, stat_a, stat_b))
    arrived = lax.all_to_all(going, "lon", split_axis=0, concat_axis=0, tiled=True)

    (message,) = call(
        message_kernel,
        hbm(up, up_halo, stat, stat_a, stat_b),
        near(like(PAD_SIDE, MESSAGE)),
        [vmem(BAND, D), vmem(2 * SIDE, D), vmem(BAND, STATS, dtype=F32), vmem(SIDE, STATS, dtype=F32), vmem(SIDE, STATS, dtype=F32),
         sems(5)],
        limit=24, flops=1024, name="boundary_message",
    )
    message = lax.ppermute(message, "lat", [(0, 1), (1, 0)])

    handed = call(
        query_kernel,
        scalars(score_sharpness, flags)
        + hbm(xn_halo, up_halo, keys, w3, wo, qhat, kv, halo_kv, weights, dprime, rawq, rawk, stat, stat_a, stat_b),
        near(like(TOKENS, D, dtype=F32), like(STEPS, SPAN, QUAD), like(STEPS, MIDDLE, QUAD), like(STEPS, 2, HALF, QUAD, dtype=F32),
             like(2, HALF, SPAN, dtype=F32), like(D, 2 * D), like(D, D), kv_like, quads, like(STATS, MIDDLE, dtype=F32)),
        [vmem(HALO_QUERIES, D), vmem(2 * SIDE, D), vmem(1, 8, KEYS, dtype=jnp.int32), vmem(D, D),
         vmem(STEPS, TOKENS, QUAD), vmem(STEPS, 2, HALO_ROWS, QUAD), vmem(STEPS, 2, STACK, SPAN), vmem(STEPS, TOKENS, QUAD),
         vmem(STEPS, TOKENS, QUAD), vmem(TOKENS, STATS, dtype=F32), vmem(SIDE, STATS, dtype=F32),
         vmem(SIDE, STATS, dtype=F32), vmem(2, KEYS, QUAD), vmem(2, KEYS, QUAD), vmem(2, TOKENS, QUAD, dtype=F32),
         vmem(HALO_QUERIES, D, dtype=F32), vmem(2 * SIDE, D), vmem(TOKENS, D), sems(4 + 5 + 6 * STEPS + 2)],
        limit=24, flops=2 * 1024 * 1024 * 4000, name="query_gradient",
    )

    (input_grad,) = call(
        key_kernel,
        hbm(x, up, gain) + near(*handed, message),
        hbm(like(TOKENS, D)),
        [vmem(TOKENS, D), vmem(TOKENS, D), vmem(1, D, dtype=F32), vmem(TOKENS, D), vmem(STATS, SPAN, dtype=F32),
         vmem(2, SPAN, QUAD), vmem(2, TOKENS, QUAD, dtype=F32), vmem(PAD_SIDE, D), vmem(TOKENS, 2 * D), sems(7)],
        limit=24, flops=2 * 1024 * 1024 * 2000, name="key_gradient",
    )
    return (
        arrived.reshape(1, 1, count, cap, SEG, D),
        input_grad.reshape(ROWS, COLS, D),
    )


def solution(mesh):
    return jax.shard_map(
        per_device,
        mesh=mesh,
        in_specs=(
            P("lat", "lon", None),
            P("lat", "lon", None),
            P(None, None, "lon", None),
            P(),
            P(),
            P(),
            P(),
            P(),
            P("lat", "lon"),
        ),
        out_specs=(P("lat", "lon", None, None, None, None), P("lat", "lon", None)),
        check_vma=False,
    )
```

```python
import functools

import jax
import jax.numpy as jnp
import numpy as np
from jax import lax
from jax.experimental import pallas as pl
from jax.experimental.pallas import tpu as pltpu
from jax.sharding import PartitionSpec as P

HEADS = 16
HALO = 6
ROWS = 12
COLS = 16
SEG = 4
D = 1024
HEAD_DIM = D // HEADS
TOKENS = ROWS * COLS
HALF = TOKENS // 2
BAND = HALO * COLS
SIDE = ROWS * HALO
CORNER = 40
QUAD = 256
QUAD_HEADS = QUAD // HEAD_DIM
STEPS = D // QUAD
STACK = QUAD_HEADS * HALF
PAD_SIDE = BAND + 2 * CORNER
MIDDLE = TOKENS + 2 * SIDE
SPAN = PAD_SIDE + MIDDLE
KEYS = SPAN + PAD_SIDE
HALO_ROWS = 2 * PAD_SIDE + 2 * SIDE - BAND
HALO_QUERIES = PAD_SIDE + 2 * SIDE
EDGE = SIDE + CORNER
STATS = 128
MESSAGE = D + STATS
MIB = 1024 * 1024
BF = jnp.bfloat16
F32 = jnp.float32


def dot(a, b):
    return jnp.dot(a, b, preferred_element_type=F32)


def dot_nt(a, b):
    return lax.dot_general(a, b, (((1,), (1,)), ((), ())), preferred_element_type=F32)


def dot_tn(a, b):
    return lax.dot_general(a, b, (((0,), (0,)), ((), ())), preferred_element_type=F32)


def first_column(side, parity):
    return COLS - HALO if side == parity else 0


def inner_row(lat, row):
    return (row + HALO * (1 - lat)) % ROWS


def selection_table():
    table = np.zeros((4, 2 * EDGE + 2 * CORNER, TOKENS + BAND), np.float32)
    for lat in range(2):
        for parity in range(2):
            for side in range(2):
                first, base = first_column(side, parity), side * EDGE
                picks = table[2 * lat + parity]
                for c in range(HALO):
                    for r in range(ROWS):
                        picks[base + r * HALO + c, inner_row(lat, r) * COLS + first + c] = 1
                    for i in range(HALO):
                        picks[base + SIDE + i * HALO + c, TOKENS + i * COLS + first + c] = 1
                        row = i + HALO * (1 - lat)
                        picks[2 * EDGE + side * CORNER + i * HALO + c, inner_row(lat, row) * COLS + first + c] = 1
    return table


def key_table():
    table = np.full((4, 8, KEYS), 1000, np.int32)
    table[:, 2] = -1
    for lat in range(2):
        for parity in range(2):
            picks = table[2 * lat + parity]
            low = {"lat": ROWS if lat == 0 else -HALO, "own": 0, "rim": -HALO if lat == 0 else ROWS}

            def put(at, count, width, first_col, kind):
                for k in range(count * width):
                    i, c = divmod(k, width)
                    picks[0, at + k] = low[kind] + i
                    picks[1, at + k] = first_col + c
                    if kind == "rim":
                        picks[2, at + k] = i

            put(0, HALO, COLS, 0, "lat")
            put(PAD_SIDE, ROWS, COLS, 0, "own")
            picks[0, PAD_SIDE : PAD_SIDE + TOKENS] = np.repeat([r for _, r in sorted((inner_row(lat, r), r) for r in range(ROWS))], COLS)
            put(SPAN, HALO, COLS, 0, "rim")
            for side in range(2):
                col = COLS if side == parity else -HALO
                put(BAND + side * CORNER, HALO, HALO, col, "lat")
                put(PAD_SIDE + TOKENS + side * SIDE, ROWS, HALO, col, "own")
                put(SPAN + BAND + side * CORNER, HALO, HALO, col, "rim")
    return table


def head_mask(h, dtype):
    lane = lax.broadcasted_iota(jnp.int32, (1, QUAD), 1)
    return jnp.where(lane // HEAD_DIM == h, 1.0, 0.0).astype(dtype)


def head_mean(values):
    a = lax.broadcasted_iota(jnp.int32, (QUAD, QUAD), 0) // HEAD_DIM
    b = lax.broadcasted_iota(jnp.int32, (QUAD, QUAD), 1) // HEAD_DIM
    block = jnp.where(a == b, 1.0 / HEAD_DIM, 0.0).astype(BF)
    return dot(values.astype(BF), block)


def unit(raw):
    return raw * lax.rsqrt(head_mean(raw * raw) + 1e-06)


def unit_back(raw, grad):
    raw = raw.astype(F32)
    inverse = lax.rsqrt(head_mean(raw * raw) + 1e-06)
    value = raw * inverse
    return inverse * (grad - value * head_mean(value * grad))


def normed(tokens, gain):
    tokens = tokens.astype(F32)
    return tokens * lax.rsqrt(jnp.mean(tokens * tokens, axis=-1, keepdims=True) + 1e-05) * gain


def multiplier(sharp_ref, j):
    out = jnp.zeros((1, QUAD), F32)
    for h in range(QUAD_HEADS):
        out = out + head_mask(h, F32) * (sharp_ref[j * QUAD_HEADS + h] / HEAD_DIM)
    return out


def stacked(block):
    return jnp.concatenate([block * head_mask(h, BF) for h in range(QUAD_HEADS)], axis=0)


def unstacked(stack):
    out = stack[:HALF] * head_mask(0, F32)
    for h in range(1, QUAD_HEADS):
        out = out + stack[h * HALF : (h + 1) * HALF] * head_mask(h, F32)
    return out


def repeated(block):
    return jnp.concatenate([block] * QUAD_HEADS, axis=0)


def head_lanes(first, pick_one):
    a = lax.broadcasted_iota(jnp.int32, (QUAD, STATS), 0)
    b = lax.broadcasted_iota(jnp.int32, (QUAD, STATS), 1)
    hit = b == a // HEAD_DIM + first
    if pick_one:
        hit = hit & (a % HEAD_DIM == 0)
    return jnp.where(hit, 1.0, 0.0).astype(BF)


def spread(stat, j):
    a = lax.broadcasted_iota(jnp.int32, (STATS, QUAD), 0)
    b = lax.broadcasted_iota(jnp.int32, (STATS, QUAD), 1)
    picks = jnp.where(a == b // HEAD_DIM + j * QUAD_HEADS, 1.0, 0.0).astype(BF)
    return dot(stat.astype(BF), picks)


def where():
    lat = lax.axis_index("lat")
    return lat, 2 * lat + lax.axis_index("lon") % 2


def half_start(lat, half):
    return pl.multiple_of(HALF * ((1 - lat) if half == 0 else lat), 16)


def near_mask(mask_ref, tab_ref, flag_ref, lat):
    rows, cols, place = tab_ref[0, 0:1], tab_ref[0, 1:2], tab_ref[0, 2:3]
    keep = jnp.where(place < 0, 1.0, 0.0)
    for i in range(HALO):
        keep = keep + jnp.where(place == i, flag_ref[lat, i].astype(F32), 0.0)
    for half in range(2):
        at = half * PAD_SIDE
        token = lax.broadcasted_iota(jnp.int32, (HALF, SPAN), 0) + half_start(lat, half)
        near = (jnp.abs(rows[:, at : at + SPAN] - token // COLS) <= HALO) & (
            jnp.abs(cols[:, at : at + SPAN] - token % COLS) <= HALO
        )
        mask_ref[half] = jnp.where(near, keep[:, at : at + SPAN], 0.0)


def lay_keys(ref, own, halo):
    ref[:PAD_SIDE] = halo[:PAD_SIDE]
    ref[PAD_SIDE : PAD_SIDE + TOKENS] = own[:TOKENS]
    ref[PAD_SIDE + TOKENS : SPAN] = halo[PAD_SIDE:HALO_QUERIES]
    ref[SPAN : SPAN + BAND] = own[TOKENS:]
    ref[SPAN + BAND :] = halo[HALO_QUERIES:]


class Copies:
    def __init__(self, sems):
        self.sems, self.used = sems, 0

    def start(self, source, target):
        copy = pltpu.make_async_copy(source, target, self.sems.at[self.used])
        self.used += 1
        copy.start()
        return copy

    def load_tokens(self, hbm, ref, lat):
        return [self.start(hbm.at[pl.ds(half_start(lat, k), HALF)], ref.at[pl.ds(k * HALF, HALF)]) for k in range(2)]

    def by_step(self, pairs):
        base, width = self.used, len(pairs(0))
        self.used += STEPS * width

        def copies(j):
            return [pltpu.make_async_copy(a, b, self.sems.at[base + j * width + k]) for k, (a, b) in enumerate(pairs(j))]

        def start(j):
            for copy in copies(j):
                copy.start()

        def wait(j):
            for copy in copies(j):
                copy.wait()

        return start, wait


def wait_all(copies):
    for copy in copies:
        copy.wait()


def lane_block(at, j):
    return pl.ds(pl.multiple_of((at + j) * QUAD, QUAD), QUAD)


def rows_at(j):
    return pl.ds(j * QUAD, QUAD)


def pack_kernel(
    x_hbm, up_hbm, rim_hbm, sel_hbm, edge_a_ref, edge_b_ref, band_ref, corner_a_ref, corner_b_ref,
    x_ref, up_ref, rim_ref, sel_ref, sems,
):
    lat, spot = where()
    copies = Copies(sems)
    loads = copies.load_tokens(x_hbm, x_ref, lat)
    loads += [copies.start(sel_hbm.at[spot], sel_ref), copies.start(rim_hbm.at[lat], rim_ref)]
    grad_loads = copies.load_tokens(up_hbm, up_ref, lat)
    wait_all(loads)
    band_ref[...] = x_ref[:BAND]
    picks = sel_ref[...]
    features = dot(picks, jnp.concatenate([x_ref[...], rim_ref[...]], axis=0))
    wait_all(grad_loads)
    grads = dot(picks[: 2 * EDGE, :TOKENS], up_ref[...])
    for side, (ref, corner_ref) in enumerate(((edge_a_ref, corner_a_ref), (edge_b_ref, corner_b_ref))):
        at = side * EDGE
        ref[...] = jnp.concatenate([features[at : at + EDGE], grads[at : at + SIDE]], axis=0).astype(BF)
        at = 2 * EDGE + side * CORNER
        corner_ref[...] = features[at : at + CORNER].astype(BF)


def own_kernel(
    sharp_ref, x_hbm, rim_hbm, up_hbm, gain_hbm, w3_hbm, wo_hbm,
    qhat_ref, dout_ref, wo_ref, x_ref, gain_ref, qhat_hbm, rawq_hbm, rawk_hbm, kv_hbm,
    kv_ref, w3_ref, rim_ref, up_ref, rawq_ref, rawk_ref, xn_ref, sems,
):
    copies = Copies(sems)
    lat, spot = where()
    loads = copies.load_tokens(x_hbm, x_ref, lat) + [copies.start(rim_hbm.at[lat], rim_ref), copies.start(gain_hbm, gain_ref)]
    start, wait = copies.by_step(
        lambda j: [(w3_hbm.at[:, lane_block(k * STEPS, j)], w3_ref.at[j, :, pl.ds(k * QUAD, QUAD)]) for k in range(3)]
    )
    for j in range(STEPS):
        start(j)
    grad_loads = copies.load_tokens(up_hbm, up_ref, lat) + [copies.start(wo_hbm, wo_ref)]
    outputs = [(qhat_ref, qhat_hbm), (rawq_ref, rawq_hbm), (rawk_ref, rawk_hbm), (kv_ref, kv_hbm)]
    store, stored = copies.by_step(lambda j: [(ref.at[j], hbm.at[j]) for ref, hbm in outputs])
    wait_all(loads)
    xn_ref[:TOKENS] = normed(x_ref[...], gain_ref[...]).astype(BF)
    xn_ref[TOKENS:] = normed(rim_ref[...], gain_ref[...]).astype(BF)
    for j in range(STEPS):
        wait(j)
        raw = dot(xn_ref[...], w3_ref[j])
        raw_q, raw_k = raw[:TOKENS, :QUAD], raw[:, QUAD : 2 * QUAD]
        units = unit(jnp.concatenate([raw_q, raw_k], axis=0))
        rawq_ref[j] = raw_q.astype(BF)
        rawk_ref[j] = raw_k[:TOKENS].astype(BF)
        qhat_ref[j] = (units[:TOKENS] * multiplier(sharp_ref, j)).astype(BF)
        kv_ref[j, 0] = units[TOKENS:].astype(BF)
        kv_ref[j, 1] = raw[:, 2 * QUAD :].astype(BF)
        store(j)
    wait_all(grad_loads)
    dout = dot_nt(up_ref[...], wo_ref[...]).astype(BF)
    for j in range(STEPS):
        dout_ref[j] = dout[:, j * QUAD : (j + 1) * QUAD]
    for j in range(STEPS):
        stored(j)


def forward_kernel(
    flag_ref, tab_hbm, sel_hbm, w3_hbm, kv_hbm, band_ref, edge_a_ref, edge_b_ref, corner_a_ref, corner_b_ref, gain_ref,
    qhat_ref, dout_ref,
    mixed_ref, stat_a_ref, stat_b_ref, halo_hbm, stat_hbm, xn_hbm, upn_hbm, weight_hbm, dprime_hbm,
    tab_ref, sel_ref, wkv_ref, kv_ref, halo_ref, stat_ref, xn_ref, upn_ref, weight_ref, dprime_ref, mask_ref, key_ref, value_ref, linv_ref, sems,
):
    lat, spot = where()
    copies = Copies(sems)
    loads = [copies.start(tab_hbm.at[spot], tab_ref.at[0])]
    start, wait = copies.by_step(
        lambda j: [(w3_hbm.at[:, lane_block(k * STEPS, j)], wkv_ref.at[j, :, pl.ds((k - 1) * QUAD, QUAD)]) for k in (1, 2)]
    )
    start_kv, wait_kv = copies.by_step(lambda j: [(kv_hbm.at[j], kv_ref.at[j])])
    for j in range(STEPS):
        start(j)
        start_kv(j)
    loads.append(copies.start(sel_hbm.at[spot], sel_ref))
    store, stored = copies.by_step(
        lambda j: [(halo_ref.at[j], halo_hbm.at[j]), (dprime_ref.at[j], dprime_hbm.at[j])]
    )
    weight_stores = []
    gain = gain_ref[...]
    edge_a, edge_b = edge_a_ref[...].astype(F32), edge_b_ref[...].astype(F32)
    pieces = [ref[...].astype(F32) for ref in (band_ref, corner_a_ref, corner_b_ref)]
    pieces += [edge_a[:SIDE], edge_b[:SIDE], edge_a[SIDE:EDGE], edge_b[SIDE:EDGE]]
    xn_ref[...] = normed(jnp.concatenate(pieces, axis=0), gain).astype(BF)
    upn_ref[...] = jnp.concatenate([edge_a[EDGE:], edge_b[EDGE:]], axis=0).astype(BF)
    stores = [copies.start(xn_ref.at[pl.ds(0, HALO_QUERIES)], xn_hbm), copies.start(upn_ref, upn_hbm)]
    loads[0].wait()
    near_mask(mask_ref, tab_ref, flag_ref, lat)
    stat = jnp.zeros((TOKENS, STATS), F32)
    for j in range(STEPS):
        if j < 2:
            for k in (0,) if j == 0 else range(1, STEPS):
                wait(k)
                wait_kv(k)
        raw = dot(xn_ref[...], wkv_ref[j])
        halo_k = unit(raw[:, :QUAD]).astype(BF)
        halo_v = raw[:, QUAD:].astype(BF)
        halo_ref[j, 0] = halo_k
        halo_ref[j, 1] = halo_v
        lay_keys(key_ref.at[j % 2], kv_ref[j, 0], halo_k)
        lay_keys(value_ref.at[j % 2], kv_ref[j, 1], halo_v)
        for half in range(2):
            at, piece = half * PAD_SIDE, slice(half * HALF, (half + 1) * HALF)
            scores = dot_nt(stacked(qhat_ref[j, piece, :]), key_ref[j % 2, at : at + SPAN])
            weights = jnp.exp(scores) * repeated(mask_ref[half])
            inverse = jnp.broadcast_to(1.0 / jnp.sum(weights, axis=-1, keepdims=True), (STACK, QUAD))
            weights = weights.astype(BF)
            weight_ref[j, half] = weights
            weight_stores.append(copies.start(weight_ref.at[j, half], weight_hbm.at[j, half]))
            mixed = unstacked(dot(weights, value_ref[j % 2, at : at + SPAN]) * inverse)
            mixed_ref[piece, rows_at(j)] = mixed.astype(BF)
            linv_ref[j, piece, :] = unstacked(inverse)
        dprime = (dout_ref[j].astype(F32) * linv_ref[j]).astype(BF)
        dprime_ref[j] = dprime
        inner = dprime.astype(F32) * mixed_ref[:, rows_at(j)].astype(F32)
        stat = stat + dot(linv_ref[j].astype(BF), head_lanes(j * QUAD_HEADS, True))
        stat = stat + dot(inner.astype(BF), head_lanes(HEADS + j * QUAD_HEADS, False))
        store(j)
    stat_ref[...] = stat
    stores.append(copies.start(stat_ref, stat_hbm))
    loads[1].wait()
    picked = dot(sel_ref[: 2 * EDGE, :TOKENS], stat.astype(BF))
    stat_a_ref[...] = picked[:SIDE]
    stat_b_ref[...] = picked[EDGE : EDGE + SIDE]
    for j in range(STEPS):
        stored(j)
    wait_all(stores + weight_stores)


def output_kernel(owner_ref, x_ref, mixed_ref, wo_ref, going_hbm, acc_ref, going_ref, count_ref, sems):
    lat, spot = where()
    copies = Copies(sems)
    for o in range(going_ref.shape[0]):
        count_ref[o] = 0
    slots = []
    for s in range(TOKENS // SEG):
        owner = owner_ref[s // (COLS // SEG), s % (COLS // SEG)]
        slots.append((owner, count_ref[owner]))
        count_ref[owner] = slots[-1][1] + 1
    stores = []
    for part in range(2):
        cols = pl.ds(part * D // 2, D // 2)
        going_ref[:, :, :, cols] = jnp.zeros(going_ref.shape[:3] + (D // 2,), BF)
        rows = x_ref[:, cols].astype(F32) + dot(mixed_ref[...], wo_ref[:, cols])
        for half in range(2):
            acc_ref[pl.ds(half_start(lat, half), HALF), cols] = rows[half * HALF : (half + 1) * HALF]
        for s, (owner, slot) in enumerate(slots):
            going_ref[owner, slot, :, cols] = acc_ref[s * SEG : (s + 1) * SEG, cols].astype(BF)
        stores.append(copies.start(going_ref.at[:, :, :, cols], going_hbm.at[:, :, :, cols]))
    wait_all(stores)


def message_kernel(
    up_hbm, upn_hbm, stat_hbm, stat_a_hbm, stat_b_hbm, out_ref, up_ref, upn_ref, stat_ref, stat_a_ref, stat_b_ref, sems
):
    lat, spot = where()
    piece = pl.ds(half_start(lat, 0), BAND)
    copies = Copies(sems)
    wait_all(
        [
            copies.start(hbm, ref)
            for hbm, ref in (
                (up_hbm.at[piece], up_ref), (upn_hbm, upn_ref), (stat_hbm.at[pl.ds(0, BAND)], stat_ref), (stat_a_hbm, stat_a_ref),
                (stat_b_hbm, stat_b_ref),
            )
        ]
    )
    a = lax.broadcasted_iota(jnp.int32, (2 * CORNER, 2 * SIDE), 0)
    b = lax.broadcasted_iota(jnp.int32, (2 * CORNER, 2 * SIDE), 1)
    side, inside = a // CORNER, HALO * HALO
    row = a - side * CORNER
    picks = jnp.where((b == row + inside * (1 - lat) + side * SIDE) & (row < inside), 1.0, 0.0).astype(BF)
    out_ref[:BAND, :D] = up_ref[...]
    out_ref[BAND:, :D] = dot(picks, upn_ref[...]).astype(BF)
    edges = jnp.concatenate([stat_a_ref[...], stat_b_ref[...]], axis=0).astype(BF)
    out_ref[:BAND, D:] = stat_ref[...].astype(BF)
    out_ref[BAND:, D:] = dot(picks, edges).astype(BF)


def inner_rows(row_ref, j):
    row = HEADS + j * QUAD_HEADS
    width = row_ref.shape[1]
    parts = [jnp.broadcast_to(row_ref[row + h : row + h + 1, :], (HALF, width)) for h in range(QUAD_HEADS)]
    return jnp.concatenate(parts, axis=0)


def key_pass(keys, values, queries, grads, mask, inner):
    weights = jnp.exp(dot_nt(stacked(keys), queries)) * repeated(mask)
    grad_scores = weights * (dot_nt(stacked(values), grads) - inner)
    return unstacked(dot(grad_scores.astype(BF), queries)), unstacked(dot(weights.astype(BF), grads))


def query_kernel(
    sharp_ref, flag_ref, xn_hbm, upn_hbm, tab_hbm, w3_hbm, wo_hbm, qhat_hbm, kv_hbm, halo_hbm, weight_hbm, dprime_hbm,
    rawq_hbm, rawk_hbm, stat_hbm, stat_a_hbm, stat_b_hbm,
    gqn_ref, query_ref, grad_ref, far_ref, mask_ref, wkv_ref, wo_ref, kv_ref, rawk_ref, row_ref,
    xn_ref, upn_ref, tab_ref, wq_ref, qhat_ref, halo_ref, weight_ref, dprime_ref, rawq_ref, stat_ref, stat_a_ref, stat_b_ref,
    key_ref, value_ref, dq_ref, raw_ref, dout_ref, grad_q_ref, sems,
):
    lat, spot = where()
    copies = Copies(sems)
    early = [
        copies.start(hbm, ref)
        for hbm, ref in (
            (tab_hbm.at[spot], tab_ref.at[0]), (stat_hbm, stat_ref), (stat_a_hbm, stat_a_ref), (stat_b_hbm, stat_b_ref),
        )
    ]
    first = [copies.start(xn_hbm, xn_ref)]
    pieces = [pl.ds(k * D // 2, D // 2) for k in range(2)]
    query_loads = [copies.start(w3_hbm.at[:, piece], wq_ref.at[:, piece]) for piece in pieces]
    first.append(copies.start(upn_hbm, upn_ref))
    output_load = copies.start(wo_hbm, wo_ref)
    start, wait = copies.by_step(
        lambda j: [
            (qhat_hbm.at[j], qhat_ref.at[j]),
            (dprime_hbm.at[j], dprime_ref.at[j]),
            (kv_hbm.at[j], kv_ref.at[j]),
            (halo_hbm.at[j], halo_ref.at[j]),
            (weight_hbm.at[j], weight_ref.at[j]),
            (rawq_hbm.at[j], rawq_ref.at[j]),
        ]
    )
    start(0)
    for j in range(1, STEPS):
        start(j)
    later = [
        copies.start(rawk_hbm, rawk_ref),
        copies.start(w3_hbm.at[:, pl.ds(D, 2 * D)], wkv_ref),
    ]
    wait_all(early)
    near_mask(mask_ref, tab_ref, flag_ref, lat)
    edges = jnp.concatenate([stat_a_ref[...], stat_b_ref[...]], axis=0)
    row_ref[...] = jnp.concatenate([stat_ref[...], edges], axis=0).T
    wait_all(first)
    for piece, load in zip(pieces, query_loads):
        load.wait()
        raw_ref[:, piece] = dot(xn_ref[...], wq_ref[:, piece])
    output_load.wait()
    dout_ref[...] = dot_nt(upn_ref[...], wo_ref[...]).astype(BF)
    for j in range(STEPS):
        halo_q = (unit(raw_ref[:, rows_at(j)]) * multiplier(sharp_ref, j)).astype(BF)
        query_ref[j, :PAD_SIDE] = halo_q[:PAD_SIDE]
        query_ref[j, PAD_SIDE + TOKENS :] = halo_q[PAD_SIDE:]
        grad_ref[j, TOKENS:] = (dout_ref[:, rows_at(j)].astype(F32) * spread(edges, j)).astype(BF)
        if j < 2:
            for k in (0,) if j == 0 else range(1, STEPS):
                wait(k)
        query_ref[j, PAD_SIDE : PAD_SIDE + TOKENS] = qhat_ref[j]
        grad_ref[j, :TOKENS] = dprime_ref[j]
        lay_keys(key_ref.at[j % 2], kv_ref[j, 0], halo_ref[j, 0])
        lay_keys(value_ref.at[j % 2], kv_ref[j, 1], halo_ref[j, 1])
        for half in range(2):
            at, piece = half * PAD_SIDE, slice(half * HALF, (half + 1) * HALF)
            stat = stat_ref[piece, :]
            lane = HEADS + j * QUAD_HEADS
            inner = jnp.concatenate([stat[:, lane + h : lane + h + 1] for h in range(QUAD_HEADS)], axis=0)
            grad_probs = dot_nt(stacked(dprime_ref[j, piece, :]), value_ref[j % 2, at : at + SPAN])
            grad_scores = weight_ref[j, half].astype(F32) * (grad_probs - inner)
            dq_ref[j % 2, piece, :] = unstacked(dot(grad_scores.astype(BF), key_ref[j % 2, at : at + SPAN]))
        piece = slice(HALF, TOKENS)
        far_ref[j, 0], far_ref[j, 1] = key_pass(
            kv_ref[j, 0, piece, :], kv_ref[j, 1, piece, :], query_ref[j, PAD_SIDE:], grad_ref[j], mask_ref[1, :, :MIDDLE],
            inner_rows(row_ref, j),
        )
        grad_q = unit_back(rawq_ref[j], dq_ref[j % 2] * multiplier(sharp_ref, j))
        grad_q_ref[:, rows_at(j)] = grad_q.astype(BF)
    gqn_ref[...] = dot_nt(grad_q_ref[...], wq_ref[...])
    wait_all(later)


def key_kernel(
    x_hbm, up_hbm, gain_hbm, gqn_ref, query_ref, grad_ref, far_ref, mask_ref, wkv_ref, wo_ref, kv_ref, rawk_ref, row_ref,
    message_ref,
    out_hbm,
    x_ref, up_ref, gain_ref, out_ref, all_row_ref, all_ref, dk_ref, dout_ref, grad_kv_ref, sems,
):
    lat, spot = where()
    copies = Copies(sems)
    loads = copies.load_tokens(x_hbm, x_ref, lat) + copies.load_tokens(up_hbm, up_ref, lat)
    loads.append(copies.start(gain_hbm, gain_ref))
    message = message_ref[:, D:].astype(F32)
    all_row_ref[...] = jnp.concatenate([message.T, row_ref[...]], axis=1)
    dout_ref[...] = dot_nt(message_ref[:, :D], wo_ref[...]).astype(BF)
    for j in range(STEPS):
        slot = j % 2
        all_ref[slot, :PAD_SIDE] = (dout_ref[:, rows_at(j)].astype(F32) * spread(message, j)).astype(BF)
        all_ref[slot, PAD_SIDE:] = grad_ref[j]
        dk_ref[slot, :HALF, :], near_dv = key_pass(
            kv_ref[j, 0, :HALF, :], kv_ref[j, 1, :HALF, :], query_ref[j], all_ref[slot], mask_ref[0], inner_rows(all_row_ref, j)
        )
        dk_ref[slot, HALF:, :] = far_ref[j, 0]
        grad_kv_ref[:, rows_at(j)] = unit_back(rawk_ref[j], dk_ref[slot]).astype(BF)
        grad_kv_ref[:HALF, rows_at(STEPS + j)] = near_dv.astype(BF)
        grad_kv_ref[HALF:, rows_at(STEPS + j)] = far_ref[j, 1].astype(BF)
    total = gqn_ref[...] + dot_nt(grad_kv_ref[...], wkv_ref[...])
    wait_all(loads)
    stores = []
    for half in range(2):
        piece = slice(half * HALF, (half + 1) * HALF)
        tokens = x_ref[piece, :].astype(F32)
        inverse = lax.rsqrt(jnp.mean(tokens * tokens, axis=-1, keepdims=True) + 1e-05)
        grad = total[piece] * gain_ref[...]
        value = tokens * inverse
        back = inverse * (grad - value * jnp.mean(value * grad, axis=-1, keepdims=True))
        out_ref[piece, :] = (up_ref[piece, :].astype(F32) + back).astype(BF)
        stores.append(copies.start(out_ref.at[pl.ds(half * HALF, HALF)], out_hbm.at[pl.ds(half_start(lat, half), HALF)]))
    wait_all(stores)


def call(kernel, inputs, outputs, scratch=(), limit=32, flops=0, name=None):
    def specs(pairs):
        return [pl.BlockSpec(memory_space=space) for space, _ in pairs]

    def placed(space, array):
        return array if space == pltpu.SMEM else pltpu.with_memory_space_constraint(array, space)

    return pl.pallas_call(
        kernel,
        in_specs=specs(inputs),
        out_specs=specs(outputs),
        out_shape=[space(shape.shape, shape.dtype) for space, shape in outputs],
        scratch_shapes=list(scratch),
        compiler_params=pltpu.CompilerParams(vmem_limit_bytes=limit * MIB),
        cost_estimate=pl.CostEstimate(flops=flops, bytes_accessed=8 << 20, transcendentals=0),
        name=name,
    )(*[placed(space, array) for space, array in inputs])


def hbm(*arrays):
    return [(pltpu.HBM, array) for array in arrays]


def near(*arrays):
    return [(pltpu.VMEM, array) for array in arrays]


def scalars(*arrays):
    return [(pltpu.SMEM, array) for array in arrays]


def like(*shape, dtype=BF):
    return jax.ShapeDtypeStruct(shape, dtype)


def partners(count):
    return (
        [(i, i + 1 - 2 * (i % 2)) for i in range(count)],
        [(i, (i - 1 + 2 * (i % 2)) % count) for i in range(count)],
    )


def across(pairs):
    return [(2 * a + lat, 2 * b + 1 - lat) for a, b in pairs for lat in range(2)]


def per_device(
    slab_features, upstream_gradient, rim_feature_rows, rim_presence_flags, feature_rescaling_coefficients,
    triple_projection_matrix, final_projection_matrix, score_sharpness, column_group_decoder_longitude,
):
    count = lax.axis_size("lon")
    cap = max(2, (2 * (TOKENS // SEG) + count - 1) // count)
    x = slab_features.reshape(TOKENS, D)
    up = upstream_gradient.reshape(TOKENS, D)
    rim = rim_feature_rows.reshape(2, BAND, D)
    gain = feature_rescaling_coefficients.reshape(1, D)
    w3, wo = triple_projection_matrix, final_projection_matrix
    table = selection_table()
    selection = jnp.asarray(table, BF)
    keys = jnp.asarray(key_table())
    flags = rim_presence_flags

    side_a, side_b = partners(count)

    def vmem(*shape, dtype=BF):
        return pltpu.VMEM(shape, dtype)

    def sems(n):
        return pltpu.SemaphoreType.DMA((n,))

    picks_shape = table.shape[1:]
    edge_a, edge_b, band, corner_a, corner_b = call(
        pack_kernel,
        hbm(x, up, rim, selection),
        near(like(EDGE + SIDE, D), like(EDGE + SIDE, D), like(BAND, D), like(CORNER, D), like(CORNER, D)),
        [vmem(TOKENS, D), vmem(TOKENS, D), vmem(BAND, D), vmem(*picks_shape), sems(6)],
        limit=24, name="edge_tokens",
    )
    band = lax.ppermute(band, "lat", [(0, 1), (1, 0)])
    corner_a = lax.ppermute(corner_a, ("lon", "lat"), across(side_a))
    corner_b = lax.ppermute(corner_b, ("lon", "lat"), across(side_b))
    edge_b = lax.ppermute(edge_b, "lon", side_b)
    edge_a = lax.ppermute(edge_a, "lon", side_a)

    quads = like(STEPS, TOKENS, QUAD)
    kv_like = like(STEPS, 2, TOKENS + BAND, QUAD)
    qhat_near, dout, wo_near, x_near, gain_near, qhat, rawq, rawk, kv = call(
        own_kernel,
        scalars(score_sharpness) + hbm(x, rim, up, gain, w3, wo),
        near(quads, quads, like(D, D), like(TOKENS, D), like(1, D, dtype=F32))
        + hbm(quads, quads, quads, kv_like),
        [vmem(STEPS, 2, TOKENS + BAND, QUAD), vmem(STEPS, D, 3 * QUAD), vmem(BAND, D), vmem(TOKENS, D),
         vmem(STEPS, TOKENS, QUAD), vmem(STEPS, TOKENS, QUAD), vmem(TOKENS + BAND, D), sems(6 + 4 * STEPS + 4 * STEPS)],
        limit=24, flops=2 * 1024 * 1024 * (192 * 2 + 288 * 2), name="own_projections",
    )

    kv_scratch = vmem(STEPS, 2, TOKENS + BAND, QUAD)
    stat_like, side_like = like(TOKENS, STATS, dtype=F32), like(SIDE, STATS, dtype=F32)
    mixed, stat_a, stat_b, halo_kv, stat, xn_halo, up_halo, weights, dprime = call(
        forward_kernel,
        scalars(flags) + hbm(keys, selection, w3, kv)
        + near(band, edge_a, edge_b, corner_a, corner_b, gain_near, qhat_near, dout),
        near(like(TOKENS, D), side_like, side_like)
        + hbm(like(STEPS, 2, HALO_ROWS, QUAD), stat_like, like(HALO_QUERIES, D), like(2 * SIDE, D),
              like(STEPS, 2, STACK, SPAN), quads),
        [vmem(1, 8, KEYS, dtype=jnp.int32), vmem(*picks_shape), vmem(STEPS, D, 2 * QUAD), kv_scratch, vmem(STEPS, 2, HALO_ROWS, QUAD),
         vmem(TOKENS, STATS, dtype=F32),
         vmem(HALO_ROWS, D), vmem(2 * SIDE, D), vmem(STEPS, 2, STACK, SPAN), vmem(STEPS, TOKENS, QUAD),
         vmem(2, HALF, SPAN, dtype=F32), vmem(2, KEYS, QUAD), vmem(2, KEYS, QUAD), vmem(STEPS, TOKENS, QUAD, dtype=F32),
         sems(2 + 3 * STEPS + 4 * STEPS + 3)],
        limit=24, flops=2 * 1024 * 1024 * 2000, name="attention_forward",
    )
    stat_b = lax.ppermute(stat_b, "lon", side_b)
    stat_a = lax.ppermute(stat_a, "lon", side_a)

    (going,) = call(
        output_kernel,
        scalars(column_group_decoder_longitude) + near(x_near, mixed, wo_near),
        hbm(like(count, cap, SEG, D)),
        [vmem(TOKENS, D, dtype=F32), vmem(count, cap, SEG, D), pltpu.SMEM((count,), jnp.int32), sems(2)],
        limit=24, flops=2 * 1024 * 1024 * 200, name="output_segments",
    )
    going, stat_a, stat_b = lax.optimization_barrier((going, stat_a, stat_b))
    arrived = lax.all_to_all(going, "lon", split_axis=0, concat_axis=0, tiled=True)

    (message,) = call(
        message_kernel,
        hbm(up, up_halo, stat, stat_a, stat_b),
        near(like(PAD_SIDE, MESSAGE)),
        [vmem(BAND, D), vmem(2 * SIDE, D), vmem(BAND, STATS, dtype=F32), vmem(SIDE, STATS, dtype=F32), vmem(SIDE, STATS, dtype=F32),
         sems(5)],
        limit=24, flops=1024, name="boundary_message",
    )
    message = lax.ppermute(message, "lat", [(0, 1), (1, 0)])

    handed = call(
        query_kernel,
        scalars(score_sharpness, flags)
        + hbm(xn_halo, up_halo, keys, w3, wo, qhat, kv, halo_kv, weights, dprime, rawq, rawk, stat, stat_a, stat_b),
        near(like(TOKENS, D, dtype=F32), like(STEPS, SPAN, QUAD), like(STEPS, MIDDLE, QUAD), like(STEPS, 2, HALF, QUAD, dtype=F32),
             like(2, HALF, SPAN, dtype=F32), like(D, 2 * D), like(D, D), kv_like, quads, like(STATS, MIDDLE, dtype=F32)),
        [vmem(HALO_QUERIES, D), vmem(2 * SIDE, D), vmem(1, 8, KEYS, dtype=jnp.int32), vmem(D, D),
         vmem(STEPS, TOKENS, QUAD), vmem(STEPS, 2, HALO_ROWS, QUAD), vmem(STEPS, 2, STACK, SPAN), vmem(STEPS, TOKENS, QUAD),
         vmem(STEPS, TOKENS, QUAD), vmem(TOKENS, STATS, dtype=F32), vmem(SIDE, STATS, dtype=F32),
         vmem(SIDE, STATS, dtype=F32), vmem(2, KEYS, QUAD), vmem(2, KEYS, QUAD), vmem(2, TOKENS, QUAD, dtype=F32),
         vmem(HALO_QUERIES, D, dtype=F32), vmem(2 * SIDE, D), vmem(TOKENS, D), sems(4 + 5 + 6 * STEPS + 2)],
        limit=24, flops=2 * 1024 * 1024 * 4000, name="query_gradient",
    )

    (input_grad,) = call(
        key_kernel,
        hbm(x, up, gain) + near(*handed, message),
        hbm(like(TOKENS, D)),
        [vmem(TOKENS, D), vmem(TOKENS, D), vmem(1, D, dtype=F32), vmem(TOKENS, D), vmem(STATS, SPAN, dtype=F32),
         vmem(2, SPAN, QUAD), vmem(2, TOKENS, QUAD, dtype=F32), vmem(PAD_SIDE, D), vmem(TOKENS, 2 * D), sems(7)],
        limit=24, flops=2 * 1024 * 1024 * 2000, name="key_gradient",
    )
    return (
        arrived.reshape(1, 1, count, cap, SEG, D),
        input_grad.reshape(ROWS, COLS, D),
    )


def solution(mesh):
    return jax.shard_map(
        per_device,
        mesh=mesh,
        in_specs=(
            P("lat", "lon", None),
            P("lat", "lon", None),
            P(None, None, "lon", None),
            P(),
            P(),
            P(),
            P(),
            P(),
            P("lat", "lon"),
        ),
        out_specs=(P("lat", "lon", None, None, None, None), P("lat", "lon", None)),
        check_vma=False,
    )
```

```python
import functools

import jax
import jax.numpy as jnp
import numpy as np
from jax import lax
from jax.experimental import pallas as pl
from jax.experimental.pallas import tpu as pltpu
from jax.sharding import PartitionSpec as P

HEADS = 16
HALO = 6
ROWS = 12
COLS = 16
SEG = 4
D = 1024
HEAD_DIM = D // HEADS
TOKENS = ROWS * COLS
HALF = TOKENS // 2
BAND = HALO * COLS
SIDE = ROWS * HALO
CORNER = 40
QUAD = 256
QUAD_HEADS = QUAD // HEAD_DIM
STEPS = D // QUAD
STACK = QUAD_HEADS * HALF
PAD_SIDE = BAND + 2 * CORNER
MIDDLE = TOKENS + 2 * SIDE
SPAN = PAD_SIDE + MIDDLE
KEYS = SPAN + PAD_SIDE
HALO_ROWS = 2 * PAD_SIDE + 2 * SIDE - BAND
HALO_QUERIES = PAD_SIDE + 2 * SIDE
EDGE = SIDE + CORNER
STATS = 128
MESSAGE = D + STATS
MIB = 1024 * 1024
BF = jnp.bfloat16
F32 = jnp.float32


def dot(a, b):
    return jnp.dot(a, b, preferred_element_type=F32)


def dot_nt(a, b):
    return lax.dot_general(a, b, (((1,), (1,)), ((), ())), preferred_element_type=F32)


def dot_tn(a, b):
    return lax.dot_general(a, b, (((0,), (0,)), ((), ())), preferred_element_type=F32)


def first_column(side, parity):
    return COLS - HALO if side == parity else 0


def inner_row(lat, row):
    return (row + HALO * (1 - lat)) % ROWS


def selection_table():
    table = np.zeros((4, 2 * EDGE + 2 * CORNER, TOKENS + BAND), np.float32)
    for lat in range(2):
        for parity in range(2):
            for side in range(2):
                first, base = first_column(side, parity), side * EDGE
                picks = table[2 * lat + parity]
                for c in range(HALO):
                    for r in range(ROWS):
                        picks[base + r * HALO + c, inner_row(lat, r) * COLS + first + c] = 1
                    for i in range(HALO):
                        picks[base + SIDE + i * HALO + c, TOKENS + i * COLS + first + c] = 1
                        row = i + HALO * (1 - lat)
                        picks[2 * EDGE + side * CORNER + i * HALO + c, inner_row(lat, row) * COLS + first + c] = 1
    return table


def key_table():
    table = np.full((4, 8, KEYS), 1000, np.int32)
    table[:, 2] = -1
    for lat in range(2):
        for parity in range(2):
            picks = table[2 * lat + parity]
            low = {"lat": ROWS if lat == 0 else -HALO, "own": 0, "rim": -HALO if lat == 0 else ROWS}

            def put(at, count, width, first_col, kind):
                for k in range(count * width):
                    i, c = divmod(k, width)
                    picks[0, at + k] = low[kind] + i
                    picks[1, at + k] = first_col + c
                    if kind == "rim":
                        picks[2, at + k] = i

            put(0, HALO, COLS, 0, "lat")
            put(PAD_SIDE, ROWS, COLS, 0, "own")
            picks[0, PAD_SIDE : PAD_SIDE + TOKENS] = np.repeat([r for _, r in sorted((inner_row(lat, r), r) for r in range(ROWS))], COLS)
            put(SPAN, HALO, COLS, 0, "rim")
            for side in range(2):
                col = COLS if side == parity else -HALO
                put(BAND + side * CORNER, HALO, HALO, col, "lat")
                put(PAD_SIDE + TOKENS + side * SIDE, ROWS, HALO, col, "own")
                put(SPAN + BAND + side * CORNER, HALO, HALO, col, "rim")
    return table


def head_mask(h, dtype):
    lane = lax.broadcasted_iota(jnp.int32, (1, QUAD), 1)
    return jnp.where(lane // HEAD_DIM == h, 1.0, 0.0).astype(dtype)


def head_mean(values):
    a = lax.broadcasted_iota(jnp.int32, (QUAD, QUAD), 0) // HEAD_DIM
    b = lax.broadcasted_iota(jnp.int32, (QUAD, QUAD), 1) // HEAD_DIM
    block = jnp.where(a == b, 1.0 / HEAD_DIM, 0.0).astype(BF)
    return dot(values.astype(BF), block)


def unit(raw):
    return raw * lax.rsqrt(head_mean(raw * raw) + 1e-06)


def unit_back(raw, grad):
    raw = raw.astype(F32)
    inverse = lax.rsqrt(head_mean(raw * raw) + 1e-06)
    value = raw * inverse
    return inverse * (grad - value * head_mean(value * grad))


def normed(tokens, gain):
    tokens = tokens.astype(F32)
    return tokens * lax.rsqrt(jnp.mean(tokens * tokens, axis=-1, keepdims=True) + 1e-05) * gain


def multiplier(sharp_ref, j):
    out = jnp.zeros((1, QUAD), F32)
    for h in range(QUAD_HEADS):
        out = out + head_mask(h, F32) * (sharp_ref[j * QUAD_HEADS + h] / HEAD_DIM)
    return out


def stacked(block):
    return jnp.concatenate([block * head_mask(h, BF) for h in range(QUAD_HEADS)], axis=0)


def unstacked(stack):
    out = stack[:HALF] * head_mask(0, F32)
    for h in range(1, QUAD_HEADS):
        out = out + stack[h * HALF : (h + 1) * HALF] * head_mask(h, F32)
    return out


def repeated(block):
    return jnp.concatenate([block] * QUAD_HEADS, axis=0)


def head_lanes(first, pick_one):
    a = lax.broadcasted_iota(jnp.int32, (QUAD, STATS), 0)
    b = lax.broadcasted_iota(jnp.int32, (QUAD, STATS), 1)
    hit = b == a // HEAD_DIM + first
    if pick_one:
        hit = hit & (a % HEAD_DIM == 0)
    return jnp.where(hit, 1.0, 0.0).astype(BF)


def spread(stat, j):
    a = lax.broadcasted_iota(jnp.int32, (STATS, QUAD), 0)
    b = lax.broadcasted_iota(jnp.int32, (STATS, QUAD), 1)
    picks = jnp.where(a == b // HEAD_DIM + j * QUAD_HEADS, 1.0, 0.0).astype(BF)
    return dot(stat.astype(BF), picks)


def where():
    lat = lax.axis_index("lat")
    return lat, 2 * lat + lax.axis_index("lon") % 2


def half_start(lat, half):
    return pl.multiple_of(HALF * ((1 - lat) if half == 0 else lat), 16)


def near_mask(mask_ref, tab_ref, flag_ref, lat):
    rows, cols, place = tab_ref[0, 0:1], tab_ref[0, 1:2], tab_ref[0, 2:3]
    keep = jnp.where(place < 0, 1.0, 0.0)
    for i in range(HALO):
        keep = keep + jnp.where(place == i, flag_ref[lat, i].astype(F32), 0.0)
    for half in range(2):
        at = half * PAD_SIDE
        token = lax.broadcasted_iota(jnp.int32, (HALF, SPAN), 0) + half_start(lat, half)
        near = (jnp.abs(rows[:, at : at + SPAN] - token // COLS) <= HALO) & (
            jnp.abs(cols[:, at : at + SPAN] - token % COLS) <= HALO
        )
        mask_ref[half] = jnp.where(near, keep[:, at : at + SPAN], 0.0)


def lay_keys(ref, own, halo):
    ref[:PAD_SIDE] = halo[:PAD_SIDE]
    ref[PAD_SIDE : PAD_SIDE + TOKENS] = own[:TOKENS]
    ref[PAD_SIDE + TOKENS : SPAN] = halo[PAD_SIDE:HALO_QUERIES]
    ref[SPAN : SPAN + BAND] = own[TOKENS:]
    ref[SPAN + BAND :] = halo[HALO_QUERIES:]


class Copies:
    def __init__(self, sems):
        self.sems, self.used = sems, 0

    def start(self, source, target):
        copy = pltpu.make_async_copy(source, target, self.sems.at[self.used])
        self.used += 1
        copy.start()
        return copy

    def load_tokens(self, hbm, ref, lat):
        return [self.start(hbm.at[pl.ds(half_start(lat, k), HALF)], ref.at[pl.ds(k * HALF, HALF)]) for k in range(2)]

    def by_step(self, pairs):
        base, width = self.used, len(pairs(0))
        self.used += STEPS * width

        def copies(j):
            return [pltpu.make_async_copy(a, b, self.sems.at[base + j * width + k]) for k, (a, b) in enumerate(pairs(j))]

        def start(j):
            for copy in copies(j):
                copy.start()

        def wait(j):
            for copy in copies(j):
                copy.wait()

        return start, wait


def wait_all(copies):
    for copy in copies:
        copy.wait()


def lane_block(at, j):
    return pl.ds(pl.multiple_of((at + j) * QUAD, QUAD), QUAD)


def rows_at(j):
    return pl.ds(j * QUAD, QUAD)


def pack_kernel(
    x_hbm, up_hbm, rim_hbm, sel_hbm, edge_a_ref, edge_b_ref, band_ref, corner_a_ref, corner_b_ref,
    x_ref, up_ref, rim_ref, sel_ref, sems,
):
    lat, spot = where()
    copies = Copies(sems)
    loads = copies.load_tokens(x_hbm, x_ref, lat)
    loads += [copies.start(sel_hbm.at[spot], sel_ref), copies.start(rim_hbm.at[lat], rim_ref)]
    grad_loads = copies.load_tokens(up_hbm, up_ref, lat)
    wait_all(loads)
    band_ref[...] = x_ref[:BAND]
    picks = sel_ref[...]
    features = dot(picks, jnp.concatenate([x_ref[...], rim_ref[...]], axis=0))
    wait_all(grad_loads)
    grads = dot(picks[: 2 * EDGE, :TOKENS], up_ref[...])
    for side, (ref, corner_ref) in enumerate(((edge_a_ref, corner_a_ref), (edge_b_ref, corner_b_ref))):
        at = side * EDGE
        ref[...] = jnp.concatenate([features[at : at + EDGE], grads[at : at + SIDE]], axis=0).astype(BF)
        at = 2 * EDGE + side * CORNER
        corner_ref[...] = features[at : at + CORNER].astype(BF)


def own_kernel(
    sharp_ref, x_hbm, rim_hbm, up_hbm, gain_hbm, w3_hbm, wo_hbm,
    qhat_ref, dout_ref, wo_ref, x_ref, gain_ref, qhat_hbm, rawq_hbm, rawk_hbm, kv_hbm,
    kv_ref, w3_ref, rim_ref, up_ref, rawq_ref, rawk_ref, xn_ref, sems,
):
    copies = Copies(sems)
    lat, spot = where()
    loads = copies.load_tokens(x_hbm, x_ref, lat) + [copies.start(rim_hbm.at[lat], rim_ref), copies.start(gain_hbm, gain_ref)]
    start, wait = copies.by_step(
        lambda j: [(w3_hbm.at[:, lane_block(k * STEPS, j)], w3_ref.at[j, :, pl.ds(k * QUAD, QUAD)]) for k in range(3)]
    )
    for j in range(STEPS):
        start(j)
    grad_loads = copies.load_tokens(up_hbm, up_ref, lat) + [copies.start(wo_hbm, wo_ref)]
    outputs = [(qhat_ref, qhat_hbm), (rawq_ref, rawq_hbm), (rawk_ref, rawk_hbm), (kv_ref, kv_hbm)]
    store, stored = copies.by_step(lambda j: [(ref.at[j], hbm.at[j]) for ref, hbm in outputs])
    wait_all(loads)
    xn_ref[:TOKENS] = normed(x_ref[...], gain_ref[...]).astype(BF)
    xn_ref[TOKENS:] = normed(rim_ref[...], gain_ref[...]).astype(BF)
    for j in range(STEPS):
        for k in ((0,), (1,), (2, 3), ())[j]:
            wait(k)
        raw = dot(xn_ref[...], w3_ref[j])
        raw_q, raw_k = raw[:TOKENS, :QUAD], raw[:, QUAD : 2 * QUAD]
        units = unit(jnp.concatenate([raw_q, raw_k], axis=0))
        rawq_ref[j] = raw_q.astype(BF)
        rawk_ref[j] = raw_k[:TOKENS].astype(BF)
        qhat_ref[j] = (units[:TOKENS] * multiplier(sharp_ref, j)).astype(BF)
        kv_ref[j, 0] = units[TOKENS:].astype(BF)
        kv_ref[j, 1] = raw[:, 2 * QUAD :].astype(BF)
        store(j)
    wait_all(grad_loads)
    dout = dot_nt(up_ref[...], wo_ref[...]).astype(BF)
    for j in range(STEPS):
        dout_ref[j] = dout[:, j * QUAD : (j + 1) * QUAD]
    for j in range(STEPS):
        stored(j)


def forward_kernel(
    flag_ref, tab_hbm, sel_hbm, w3_hbm, kv_hbm, band_ref, edge_a_ref, edge_b_ref, corner_a_ref, corner_b_ref, gain_ref,
    qhat_ref, dout_ref,
    mixed_ref, stat_a_ref, stat_b_ref, halo_hbm, stat_hbm, xn_hbm, upn_hbm, weight_hbm, dprime_hbm,
    tab_ref, sel_ref, wkv_ref, kv_ref, halo_ref, stat_ref, xn_ref, upn_ref, weight_ref, dprime_ref, mask_ref, key_ref, value_ref, linv_ref, sems,
):
    lat, spot = where()
    copies = Copies(sems)
    loads = [copies.start(tab_hbm.at[spot], tab_ref.at[0])]
    start, wait = copies.by_step(
        lambda j: [(w3_hbm.at[:, lane_block(k * STEPS, j)], wkv_ref.at[j, :, pl.ds((k - 1) * QUAD, QUAD)]) for k in (1, 2)]
    )
    start_kv, wait_kv = copies.by_step(lambda j: [(kv_hbm.at[j], kv_ref.at[j])])
    for j in range(STEPS):
        start(j)
        start_kv(j)
    loads.append(copies.start(sel_hbm.at[spot], sel_ref))
    store, stored = copies.by_step(
        lambda j: [(halo_ref.at[j], halo_hbm.at[j]), (dprime_ref.at[j], dprime_hbm.at[j])]
    )
    weight_stores = []
    gain = gain_ref[...]
    edge_a, edge_b = edge_a_ref[...].astype(F32), edge_b_ref[...].astype(F32)
    pieces = [ref[...].astype(F32) for ref in (band_ref, corner_a_ref, corner_b_ref)]
    pieces += [edge_a[:SIDE], edge_b[:SIDE], edge_a[SIDE:EDGE], edge_b[SIDE:EDGE]]
    xn_ref[...] = normed(jnp.concatenate(pieces, axis=0), gain).astype(BF)
    upn_ref[...] = jnp.concatenate([edge_a[EDGE:], edge_b[EDGE:]], axis=0).astype(BF)
    stores = [copies.start(xn_ref.at[pl.ds(0, HALO_QUERIES)], xn_hbm), copies.start(upn_ref, upn_hbm)]
    loads[0].wait()
    near_mask(mask_ref, tab_ref, flag_ref, lat)
    stat = jnp.zeros((TOKENS, STATS), F32)
    for j in range(STEPS):
        if j < 2:
            for k in (0,) if j == 0 else range(1, STEPS):
                wait(k)
                wait_kv(k)
        raw = dot(xn_ref[...], wkv_ref[j])
        halo_k = unit(raw[:, :QUAD]).astype(BF)
        halo_v = raw[:, QUAD:].astype(BF)
        halo_ref[j, 0] = halo_k
        halo_ref[j, 1] = halo_v
        lay_keys(key_ref.at[j % 2], kv_ref[j, 0], halo_k)
        lay_keys(value_ref.at[j % 2], kv_ref[j, 1], halo_v)
        for half in range(2):
            at, piece = half * PAD_SIDE, slice(half * HALF, (half + 1) * HALF)
            scores = dot_nt(stacked(qhat_ref[j, piece, :]), key_ref[j % 2, at : at + SPAN])
            weights = jnp.exp(scores) * repeated(mask_ref[half])
            inverse = jnp.broadcast_to(1.0 / jnp.sum(weights, axis=-1, keepdims=True), (STACK, QUAD))
            weights = weights.astype(BF)
            weight_ref[j, half] = weights
            weight_stores.append(copies.start(weight_ref.at[j, half], weight_hbm.at[j, half]))
            mixed = unstacked(dot(weights, value_ref[j % 2, at : at + SPAN]) * inverse)
            mixed_ref[piece, rows_at(j)] = mixed.astype(BF)
            linv_ref[j, piece, :] = unstacked(inverse)
        dprime = (dout_ref[j].astype(F32) * linv_ref[j]).astype(BF)
        dprime_ref[j] = dprime
        inner = dprime.astype(F32) * mixed_ref[:, rows_at(j)].astype(F32)
        stat = stat + dot(linv_ref[j].astype(BF), head_lanes(j * QUAD_HEADS, True))
        stat = stat + dot(inner.astype(BF), head_lanes(HEADS + j * QUAD_HEADS, False))
        store(j)
    stat_ref[...] = stat
    stores.append(copies.start(stat_ref, stat_hbm))
    loads[1].wait()
    picked = dot(sel_ref[: 2 * EDGE, :TOKENS], stat.astype(BF))
    stat_a_ref[...] = picked[:SIDE]
    stat_b_ref[...] = picked[EDGE : EDGE + SIDE]
    for j in range(STEPS):
        stored(j)
    wait_all(stores + weight_stores)


def output_kernel(owner_ref, x_ref, mixed_ref, wo_ref, going_hbm, acc_ref, going_ref, count_ref, sems):
    lat, spot = where()
    copies = Copies(sems)
    for o in range(going_ref.shape[0]):
        count_ref[o] = 0
    slots = []
    for s in range(TOKENS // SEG):
        owner = owner_ref[s // (COLS // SEG), s % (COLS // SEG)]
        slots.append((owner, count_ref[owner]))
        count_ref[owner] = slots[-1][1] + 1
    stores = []
    for part in range(2):
        cols = pl.ds(part * D // 2, D // 2)
        going_ref[:, :, :, cols] = jnp.zeros(going_ref.shape[:3] + (D // 2,), BF)
        rows = x_ref[:, cols].astype(F32) + dot(mixed_ref[...], wo_ref[:, cols])
        for half in range(2):
            acc_ref[pl.ds(half_start(lat, half), HALF), cols] = rows[half * HALF : (half + 1) * HALF]
        for s, (owner, slot) in enumerate(slots):
            going_ref[owner, slot, :, cols] = acc_ref[s * SEG : (s + 1) * SEG, cols].astype(BF)
        stores.append(copies.start(going_ref.at[:, :, :, cols], going_hbm.at[:, :, :, cols]))
    wait_all(stores)


def message_kernel(
    up_hbm, upn_hbm, stat_hbm, stat_a_hbm, stat_b_hbm, out_ref, up_ref, upn_ref, stat_ref, stat_a_ref, stat_b_ref, sems
):
    lat, spot = where()
    piece = pl.ds(half_start(lat, 0), BAND)
    copies = Copies(sems)
    wait_all(
        [
            copies.start(hbm, ref)
            for hbm, ref in (
                (up_hbm.at[piece], up_ref), (upn_hbm, upn_ref), (stat_hbm.at[pl.ds(0, BAND)], stat_ref), (stat_a_hbm, stat_a_ref),
                (stat_b_hbm, stat_b_ref),
            )
        ]
    )
    a = lax.broadcasted_iota(jnp.int32, (2 * CORNER, 2 * SIDE), 0)
    b = lax.broadcasted_iota(jnp.int32, (2 * CORNER, 2 * SIDE), 1)
    side, inside = a // CORNER, HALO * HALO
    row = a - side * CORNER
    picks = jnp.where((b == row + inside * (1 - lat) + side * SIDE) & (row < inside), 1.0, 0.0).astype(BF)
    out_ref[:BAND, :D] = up_ref[...]
    out_ref[BAND:, :D] = dot(picks, upn_ref[...]).astype(BF)
    edges = jnp.concatenate([stat_a_ref[...], stat_b_ref[...]], axis=0).astype(BF)
    out_ref[:BAND, D:] = stat_ref[...].astype(BF)
    out_ref[BAND:, D:] = dot(picks, edges).astype(BF)


def inner_rows(row_ref, j):
    row = HEADS + j * QUAD_HEADS
    width = row_ref.shape[1]
    parts = [jnp.broadcast_to(row_ref[row + h : row + h + 1, :], (HALF, width)) for h in range(QUAD_HEADS)]
    return jnp.concatenate(parts, axis=0)


def key_pass(keys, values, queries, grads, mask, inner):
    weights = jnp.exp(dot_nt(stacked(keys), queries)) * repeated(mask)
    grad_scores = weights * (dot_nt(stacked(values), grads) - inner)
    return unstacked(dot(grad_scores.astype(BF), queries)), unstacked(dot(weights.astype(BF), grads))


def query_kernel(
    sharp_ref, flag_ref, xn_hbm, upn_hbm, tab_hbm, w3_hbm, wo_hbm, qhat_hbm, kv_hbm, halo_hbm, weight_hbm, dprime_hbm,
    rawq_hbm, rawk_hbm, stat_hbm, stat_a_hbm, stat_b_hbm,
    gqn_ref, query_ref, grad_ref, far_ref, mask_ref, wkv_ref, wo_ref, kv_ref, rawk_ref, row_ref,
    xn_ref, upn_ref, tab_ref, wq_ref, qhat_ref, halo_ref, weight_ref, dprime_ref, rawq_ref, stat_ref, stat_a_ref, stat_b_ref,
    key_ref, value_ref, dq_ref, raw_ref, dout_ref, grad_q_ref, sems,
):
    lat, spot = where()
    copies = Copies(sems)
    early = [
        copies.start(hbm, ref)
        for hbm, ref in (
            (tab_hbm.at[spot], tab_ref.at[0]), (stat_hbm, stat_ref), (stat_a_hbm, stat_a_ref), (stat_b_hbm, stat_b_ref),
        )
    ]
    first = [copies.start(xn_hbm, xn_ref)]
    pieces = [pl.ds(k * D // 2, D // 2) for k in range(2)]
    query_loads = [copies.start(w3_hbm.at[:, piece], wq_ref.at[:, piece]) for piece in pieces]
    first.append(copies.start(upn_hbm, upn_ref))
    output_load = copies.start(wo_hbm, wo_ref)
    start, wait = copies.by_step(
        lambda j: [
            (qhat_hbm.at[j], qhat_ref.at[j]),
            (dprime_hbm.at[j], dprime_ref.at[j]),
            (kv_hbm.at[j], kv_ref.at[j]),
            (halo_hbm.at[j], halo_ref.at[j]),
            (weight_hbm.at[j], weight_ref.at[j]),
            (rawq_hbm.at[j], rawq_ref.at[j]),
        ]
    )
    start(0)
    for j in range(1, STEPS):
        start(j)
    later = [
        copies.start(rawk_hbm, rawk_ref),
        copies.start(w3_hbm.at[:, pl.ds(D, 2 * D)], wkv_ref),
    ]
    wait_all(early)
    near_mask(mask_ref, tab_ref, flag_ref, lat)
    edges = jnp.concatenate([stat_a_ref[...], stat_b_ref[...]], axis=0)
    row_ref[...] = jnp.concatenate([stat_ref[...], edges], axis=0).T
    wait_all(first)
    for piece, load in zip(pieces, query_loads):
        load.wait()
        raw_ref[:, piece] = dot(xn_ref[...], wq_ref[:, piece])
    output_load.wait()
    dout_ref[...] = dot_nt(upn_ref[...], wo_ref[...]).astype(BF)
    for j in range(STEPS):
        halo_q = (unit(raw_ref[:, rows_at(j)]) * multiplier(sharp_ref, j)).astype(BF)
        query_ref[j, :PAD_SIDE] = halo_q[:PAD_SIDE]
        query_ref[j, PAD_SIDE + TOKENS :] = halo_q[PAD_SIDE:]
        grad_ref[j, TOKENS:] = (dout_ref[:, rows_at(j)].astype(F32) * spread(edges, j)).astype(BF)
        if j < 2:
            for k in (0,) if j == 0 else range(1, STEPS):
                wait(k)
        query_ref[j, PAD_SIDE : PAD_SIDE + TOKENS] = qhat_ref[j]
        grad_ref[j, :TOKENS] = dprime_ref[j]
        lay_keys(key_ref.at[j % 2], kv_ref[j, 0], halo_ref[j, 0])
        lay_keys(value_ref.at[j % 2], kv_ref[j, 1], halo_ref[j, 1])
        for half in range(2):
            at, piece = half * PAD_SIDE, slice(half * HALF, (half + 1) * HALF)
            stat = stat_ref[piece, :]
            lane = HEADS + j * QUAD_HEADS
            inner = jnp.concatenate([stat[:, lane + h : lane + h + 1] for h in range(QUAD_HEADS)], axis=0)
            grad_probs = dot_nt(stacked(dprime_ref[j, piece, :]), value_ref[j % 2, at : at + SPAN])
            grad_scores = weight_ref[j, half].astype(F32) * (grad_probs - inner)
            dq_ref[j % 2, piece, :] = unstacked(dot(grad_scores.astype(BF), key_ref[j % 2, at : at + SPAN]))
        piece = slice(HALF, TOKENS)
        far_ref[j, 0], far_ref[j, 1] = key_pass(
            kv_ref[j, 0, piece, :], kv_ref[j, 1, piece, :], query_ref[j, PAD_SIDE:], grad_ref[j], mask_ref[1, :, :MIDDLE],
            inner_rows(row_ref, j),
        )
        grad_q = unit_back(rawq_ref[j], dq_ref[j % 2] * multiplier(sharp_ref, j))
        grad_q_ref[:, rows_at(j)] = grad_q.astype(BF)
    gqn_ref[...] = dot_nt(grad_q_ref[...], wq_ref[...])
    wait_all(later)


def key_kernel(
    x_hbm, up_hbm, gain_hbm, gqn_ref, query_ref, grad_ref, far_ref, mask_ref, wkv_ref, wo_ref, kv_ref, rawk_ref, row_ref,
    message_ref,
    out_hbm,
    x_ref, up_ref, gain_ref, out_ref, all_row_ref, all_ref, dk_ref, dout_ref, grad_kv_ref, sems,
):
    lat, spot = where()
    copies = Copies(sems)
    loads = copies.load_tokens(x_hbm, x_ref, lat) + copies.load_tokens(up_hbm, up_ref, lat)
    loads.append(copies.start(gain_hbm, gain_ref))
    message = message_ref[:, D:].astype(F32)
    all_row_ref[...] = jnp.concatenate([message.T, row_ref[...]], axis=1)
    dout_ref[...] = dot_nt(message_ref[:, :D], wo_ref[...]).astype(BF)
    for j in range(STEPS):
        slot = j % 2
        all_ref[slot, :PAD_SIDE] = (dout_ref[:, rows_at(j)].astype(F32) * spread(message, j)).astype(BF)
        all_ref[slot, PAD_SIDE:] = grad_ref[j]
        dk_ref[slot, :HALF, :], near_dv = key_pass(
            kv_ref[j, 0, :HALF, :], kv_ref[j, 1, :HALF, :], query_ref[j], all_ref[slot], mask_ref[0], inner_rows(all_row_ref, j)
        )
        dk_ref[slot, HALF:, :] = far_ref[j, 0]
        grad_kv_ref[:, rows_at(j)] = unit_back(rawk_ref[j], dk_ref[slot]).astype(BF)
        grad_kv_ref[:HALF, rows_at(STEPS + j)] = near_dv.astype(BF)
        grad_kv_ref[HALF:, rows_at(STEPS + j)] = far_ref[j, 1].astype(BF)
    total = gqn_ref[...] + dot_nt(grad_kv_ref[...], wkv_ref[...])
    wait_all(loads)
    stores = []
    for half in range(2):
        piece = slice(half * HALF, (half + 1) * HALF)
        tokens = x_ref[piece, :].astype(F32)
        inverse = lax.rsqrt(jnp.mean(tokens * tokens, axis=-1, keepdims=True) + 1e-05)
        grad = total[piece] * gain_ref[...]
        value = tokens * inverse
        back = inverse * (grad - value * jnp.mean(value * grad, axis=-1, keepdims=True))
        out_ref[piece, :] = (up_ref[piece, :].astype(F32) + back).astype(BF)
        stores.append(copies.start(out_ref.at[pl.ds(half * HALF, HALF)], out_hbm.at[pl.ds(half_start(lat, half), HALF)]))
    wait_all(stores)


def call(kernel, inputs, outputs, scratch=(), limit=32, flops=0, name=None):
    def specs(pairs):
        return [pl.BlockSpec(memory_space=space) for space, _ in pairs]

    def placed(space, array):
        return array if space == pltpu.SMEM else pltpu.with_memory_space_constraint(array, space)

    return pl.pallas_call(
        kernel,
        in_specs=specs(inputs),
        out_specs=specs(outputs),
        out_shape=[space(shape.shape, shape.dtype) for space, shape in outputs],
        scratch_shapes=list(scratch),
        compiler_params=pltpu.CompilerParams(vmem_limit_bytes=limit * MIB),
        cost_estimate=pl.CostEstimate(flops=flops, bytes_accessed=8 << 20, transcendentals=0),
        name=name,
    )(*[placed(space, array) for space, array in inputs])


def hbm(*arrays):
    return [(pltpu.HBM, array) for array in arrays]


def near(*arrays):
    return [(pltpu.VMEM, array) for array in arrays]


def scalars(*arrays):
    return [(pltpu.SMEM, array) for array in arrays]


def like(*shape, dtype=BF):
    return jax.ShapeDtypeStruct(shape, dtype)


def partners(count):
    return (
        [(i, i + 1 - 2 * (i % 2)) for i in range(count)],
        [(i, (i - 1 + 2 * (i % 2)) % count) for i in range(count)],
    )


def across(pairs):
    return [(2 * a + lat, 2 * b + 1 - lat) for a, b in pairs for lat in range(2)]


def per_device(
    slab_features, upstream_gradient, rim_feature_rows, rim_presence_flags, feature_rescaling_coefficients,
    triple_projection_matrix, final_projection_matrix, score_sharpness, column_group_decoder_longitude,
):
    count = lax.axis_size("lon")
    cap = max(2, (2 * (TOKENS // SEG) + count - 1) // count)
    x = slab_features.reshape(TOKENS, D)
    up = upstream_gradient.reshape(TOKENS, D)
    rim = rim_feature_rows.reshape(2, BAND, D)
    gain = feature_rescaling_coefficients.reshape(1, D)
    w3, wo = triple_projection_matrix, final_projection_matrix
    table = selection_table()
    selection = jnp.asarray(table, BF)
    keys = jnp.asarray(key_table())
    flags = rim_presence_flags

    side_a, side_b = partners(count)

    def vmem(*shape, dtype=BF):
        return pltpu.VMEM(shape, dtype)

    def sems(n):
        return pltpu.SemaphoreType.DMA((n,))

    picks_shape = table.shape[1:]
    edge_a, edge_b, band, corner_a, corner_b = call(
        pack_kernel,
        hbm(x, up, rim, selection),
        near(like(EDGE + SIDE, D), like(EDGE + SIDE, D), like(BAND, D), like(CORNER, D), like(CORNER, D)),
        [vmem(TOKENS, D), vmem(TOKENS, D), vmem(BAND, D), vmem(*picks_shape), sems(6)],
        limit=24, name="edge_tokens",
    )
    band = lax.ppermute(band, "lat", [(0, 1), (1, 0)])
    corner_a = lax.ppermute(corner_a, ("lon", "lat"), across(side_a))
    corner_b = lax.ppermute(corner_b, ("lon", "lat"), across(side_b))
    edge_b = lax.ppermute(edge_b, "lon", side_b)
    edge_a = lax.ppermute(edge_a, "lon", side_a)

    quads = like(STEPS, TOKENS, QUAD)
    kv_like = like(STEPS, 2, TOKENS + BAND, QUAD)
    qhat_near, dout, wo_near, x_near, gain_near, qhat, rawq, rawk, kv = call(
        own_kernel,
        scalars(score_sharpness) + hbm(x, rim, up, gain, w3, wo),
        near(quads, quads, like(D, D), like(TOKENS, D), like(1, D, dtype=F32))
        + hbm(quads, quads, quads, kv_like),
        [vmem(STEPS, 2, TOKENS + BAND, QUAD), vmem(STEPS, D, 3 * QUAD), vmem(BAND, D), vmem(TOKENS, D),
         vmem(STEPS, TOKENS, QUAD), vmem(STEPS, TOKENS, QUAD), vmem(TOKENS + BAND, D), sems(6 + 4 * STEPS + 4 * STEPS)],
        limit=24, flops=2 * 1024 * 1024 * (192 * 2 + 288 * 2), name="own_projections",
    )

    kv_scratch = vmem(STEPS, 2, TOKENS + BAND, QUAD)
    stat_like, side_like = like(TOKENS, STATS, dtype=F32), like(SIDE, STATS, dtype=F32)
    mixed, stat_a, stat_b, halo_kv, stat, xn_halo, up_halo, weights, dprime = call(
        forward_kernel,
        scalars(flags) + hbm(keys, selection, w3, kv)
        + near(band, edge_a, edge_b, corner_a, corner_b, gain_near, qhat_near, dout),
        near(like(TOKENS, D), side_like, side_like)
        + hbm(like(STEPS, 2, HALO_ROWS, QUAD), stat_like, like(HALO_QUERIES, D), like(2 * SIDE, D),
              like(STEPS, 2, STACK, SPAN), quads),
        [vmem(1, 8, KEYS, dtype=jnp.int32), vmem(*picks_shape), vmem(STEPS, D, 2 * QUAD), kv_scratch, vmem(STEPS, 2, HALO_ROWS, QUAD),
         vmem(TOKENS, STATS, dtype=F32),
         vmem(HALO_ROWS, D), vmem(2 * SIDE, D), vmem(STEPS, 2, STACK, SPAN), vmem(STEPS, TOKENS, QUAD),
         vmem(2, HALF, SPAN, dtype=F32), vmem(2, KEYS, QUAD), vmem(2, KEYS, QUAD), vmem(STEPS, TOKENS, QUAD, dtype=F32),
         sems(2 + 3 * STEPS + 4 * STEPS + 3)],
        limit=24, flops=2 * 1024 * 1024 * 2000, name="attention_forward",
    )
    stat_b = lax.ppermute(stat_b, "lon", side_b)
    stat_a = lax.ppermute(stat_a, "lon", side_a)

    (going,) = call(
        output_kernel,
        scalars(column_group_decoder_longitude) + near(x_near, mixed, wo_near),
        hbm(like(count, cap, SEG, D)),
        [vmem(TOKENS, D, dtype=F32), vmem(count, cap, SEG, D), pltpu.SMEM((count,), jnp.int32), sems(2)],
        limit=24, flops=2 * 1024 * 1024 * 200, name="output_segments",
    )
    going, stat_a, stat_b = lax.optimization_barrier((going, stat_a, stat_b))
    arrived = lax.all_to_all(going, "lon", split_axis=0, concat_axis=0, tiled=True)

    (message,) = call(
        message_kernel,
        hbm(up, up_halo, stat, stat_a, stat_b),
        near(like(PAD_SIDE, MESSAGE)),
        [vmem(BAND, D), vmem(2 * SIDE, D), vmem(BAND, STATS, dtype=F32), vmem(SIDE, STATS, dtype=F32), vmem(SIDE, STATS, dtype=F32),
         sems(5)],
        limit=24, flops=1024, name="boundary_message",
    )
    message = lax.ppermute(message, "lat", [(0, 1), (1, 0)])

    handed = call(
        query_kernel,
        scalars(score_sharpness, flags)
        + hbm(xn_halo, up_halo, keys, w3, wo, qhat, kv, halo_kv, weights, dprime, rawq, rawk, stat, stat_a, stat_b),
        near(like(TOKENS, D, dtype=F32), like(STEPS, SPAN, QUAD), like(STEPS, MIDDLE, QUAD), like(STEPS, 2, HALF, QUAD, dtype=F32),
             like(2, HALF, SPAN, dtype=F32), like(D, 2 * D), like(D, D), kv_like, quads, like(STATS, MIDDLE, dtype=F32)),
        [vmem(HALO_QUERIES, D), vmem(2 * SIDE, D), vmem(1, 8, KEYS, dtype=jnp.int32), vmem(D, D),
         vmem(STEPS, TOKENS, QUAD), vmem(STEPS, 2, HALO_ROWS, QUAD), vmem(STEPS, 2, STACK, SPAN), vmem(STEPS, TOKENS, QUAD),
         vmem(STEPS, TOKENS, QUAD), vmem(TOKENS, STATS, dtype=F32), vmem(SIDE, STATS, dtype=F32),
         vmem(SIDE, STATS, dtype=F32), vmem(2, KEYS, QUAD), vmem(2, KEYS, QUAD), vmem(2, TOKENS, QUAD, dtype=F32),
         vmem(HALO_QUERIES, D, dtype=F32), vmem(2 * SIDE, D), vmem(TOKENS, D), sems(4 + 5 + 6 * STEPS + 2)],
        limit=24, flops=2 * 1024 * 1024 * 4000, name="query_gradient",
    )

    (input_grad,) = call(
        key_kernel,
        hbm(x, up, gain) + near(*handed, message),
        hbm(like(TOKENS, D)),
        [vmem(TOKENS, D), vmem(TOKENS, D), vmem(1, D, dtype=F32), vmem(TOKENS, D), vmem(STATS, SPAN, dtype=F32),
         vmem(2, SPAN, QUAD), vmem(2, TOKENS, QUAD, dtype=F32), vmem(PAD_SIDE, D), vmem(TOKENS, 2 * D), sems(7)],
        limit=24, flops=2 * 1024 * 1024 * 2000, name="key_gradient",
    )
    return (
        arrived.reshape(1, 1, count, cap, SEG, D),
        input_grad.reshape(ROWS, COLS, D),
    )


def solution(mesh):
    return jax.shard_map(
        per_device,
        mesh=mesh,
        in_specs=(
            P("lat", "lon", None),
            P("lat", "lon", None),
            P(None, None, "lon", None),
            P(),
            P(),
            P(),
            P(),
            P(),
            P("lat", "lon"),
        ),
        out_specs=(P("lat", "lon", None, None, None, None), P("lat", "lon", None)),
        check_vma=False,
    )
```

```python
import functools

import jax
import jax.numpy as jnp
import numpy as np
from jax import lax
from jax.experimental import pallas as pl
from jax.experimental.pallas import tpu as pltpu
from jax.sharding import PartitionSpec as P

HEADS = 16
HALO = 6
ROWS = 12
COLS = 16
SEG = 4
D = 1024
HEAD_DIM = D // HEADS
TOKENS = ROWS * COLS
HALF = TOKENS // 2
BAND = HALO * COLS
SIDE = ROWS * HALO
CORNER = 40
QUAD = 256
QUAD_HEADS = QUAD // HEAD_DIM
STEPS = D // QUAD
STACK = QUAD_HEADS * HALF
PAD_SIDE = BAND + 2 * CORNER
MIDDLE = TOKENS + 2 * SIDE
SPAN = PAD_SIDE + MIDDLE
KEYS = SPAN + PAD_SIDE
HALO_ROWS = 2 * PAD_SIDE + 2 * SIDE - BAND
HALO_QUERIES = PAD_SIDE + 2 * SIDE
EDGE = SIDE + CORNER
STATS = 128
MESSAGE = D + STATS
MIB = 1024 * 1024
BF = jnp.bfloat16
F32 = jnp.float32


def dot(a, b):
    return jnp.dot(a, b, preferred_element_type=F32)


def dot_nt(a, b):
    return lax.dot_general(a, b, (((1,), (1,)), ((), ())), preferred_element_type=F32)


def dot_tn(a, b):
    return lax.dot_general(a, b, (((0,), (0,)), ((), ())), preferred_element_type=F32)


def first_column(side, parity):
    return COLS - HALO if side == parity else 0


def inner_row(lat, row):
    return (row + HALO * (1 - lat)) % ROWS


def selection_table():
    table = np.zeros((4, 2 * EDGE + 2 * CORNER, TOKENS + BAND), np.float32)
    for lat in range(2):
        for parity in range(2):
            for side in range(2):
                first, base = first_column(side, parity), side * EDGE
                picks = table[2 * lat + parity]
                for c in range(HALO):
                    for r in range(ROWS):
                        picks[base + r * HALO + c, inner_row(lat, r) * COLS + first + c] = 1
                    for i in range(HALO):
                        picks[base + SIDE + i * HALO + c, TOKENS + i * COLS + first + c] = 1
                        row = i + HALO * (1 - lat)
                        picks[2 * EDGE + side * CORNER + i * HALO + c, inner_row(lat, row) * COLS + first + c] = 1
    return table


def key_table():
    table = np.full((4, 8, KEYS), 1000, np.int32)
    table[:, 2] = -1
    for lat in range(2):
        for parity in range(2):
            picks = table[2 * lat + parity]
            low = {"lat": ROWS if lat == 0 else -HALO, "own": 0, "rim": -HALO if lat == 0 else ROWS}

            def put(at, count, width, first_col, kind):
                for k in range(count * width):
                    i, c = divmod(k, width)
                    picks[0, at + k] = low[kind] + i
                    picks[1, at + k] = first_col + c
                    if kind == "rim":
                        picks[2, at + k] = i

            put(0, HALO, COLS, 0, "lat")
            put(PAD_SIDE, ROWS, COLS, 0, "own")
            picks[0, PAD_SIDE : PAD_SIDE + TOKENS] = np.repeat([r for _, r in sorted((inner_row(lat, r), r) for r in range(ROWS))], COLS)
            put(SPAN, HALO, COLS, 0, "rim")
            for side in range(2):
                col = COLS if side == parity else -HALO
                put(BAND + side * CORNER, HALO, HALO, col, "lat")
                put(PAD_SIDE + TOKENS + side * SIDE, ROWS, HALO, col, "own")
                put(SPAN + BAND + side * CORNER, HALO, HALO, col, "rim")
    return table


def head_mask(h, dtype):
    lane = lax.broadcasted_iota(jnp.int32, (1, QUAD), 1)
    return jnp.where(lane // HEAD_DIM == h, 1.0, 0.0).astype(dtype)


def head_mean(values):
    a = lax.broadcasted_iota(jnp.int32, (QUAD, QUAD), 0) // HEAD_DIM
    b = lax.broadcasted_iota(jnp.int32, (QUAD, QUAD), 1) // HEAD_DIM
    block = jnp.where(a == b, 1.0 / HEAD_DIM, 0.0).astype(BF)
    return dot(values.astype(BF), block)


def unit(raw):
    return raw * lax.rsqrt(head_mean(raw * raw) + 1e-06)


def unit_back(raw, grad):
    raw = raw.astype(F32)
    inverse = lax.rsqrt(head_mean(raw * raw) + 1e-06)
    value = raw * inverse
    return inverse * (grad - value * head_mean(value * grad))


def normed(tokens, gain):
    tokens = tokens.astype(F32)
    return tokens * lax.rsqrt(jnp.mean(tokens * tokens, axis=-1, keepdims=True) + 1e-05) * gain


def multiplier(sharp_ref, j):
    out = jnp.zeros((1, QUAD), F32)
    for h in range(QUAD_HEADS):
        out = out + head_mask(h, F32) * (sharp_ref[j * QUAD_HEADS + h] / HEAD_DIM)
    return out


def stacked(block):
    return jnp.concatenate([block * head_mask(h, BF) for h in range(QUAD_HEADS)], axis=0)


def unstacked(stack):
    out = stack[:HALF] * head_mask(0, F32)
    for h in range(1, QUAD_HEADS):
        out = out + stack[h * HALF : (h + 1) * HALF] * head_mask(h, F32)
    return out


def repeated(block):
    return jnp.concatenate([block] * QUAD_HEADS, axis=0)


def head_lanes(first, pick_one):
    a = lax.broadcasted_iota(jnp.int32, (QUAD, STATS), 0)
    b = lax.broadcasted_iota(jnp.int32, (QUAD, STATS), 1)
    hit = b == a // HEAD_DIM + first
    if pick_one:
        hit = hit & (a % HEAD_DIM == 0)
    return jnp.where(hit, 1.0, 0.0).astype(BF)


def spread(stat, j):
    a = lax.broadcasted_iota(jnp.int32, (STATS, QUAD), 0)
    b = lax.broadcasted_iota(jnp.int32, (STATS, QUAD), 1)
    picks = jnp.where(a == b // HEAD_DIM + j * QUAD_HEADS, 1.0, 0.0).astype(BF)
    return dot(stat.astype(BF), picks)


def where():
    lat = lax.axis_index("lat")
    return lat, 2 * lat + lax.axis_index("lon") % 2


def half_start(lat, half):
    return pl.multiple_of(HALF * ((1 - lat) if half == 0 else lat), 16)


def near_mask(mask_ref, tab_ref, flag_ref, lat):
    rows, cols, place = tab_ref[0, 0:1], tab_ref[0, 1:2], tab_ref[0, 2:3]
    keep = jnp.where(place < 0, 1.0, 0.0)
    for i in range(HALO):
        keep = keep + jnp.where(place == i, flag_ref[lat, i].astype(F32), 0.0)
    for half in range(2):
        at = half * PAD_SIDE
        token = lax.broadcasted_iota(jnp.int32, (HALF, SPAN), 0) + half_start(lat, half)
        near = (jnp.abs(rows[:, at : at + SPAN] - token // COLS) <= HALO) & (
            jnp.abs(cols[:, at : at + SPAN] - token % COLS) <= HALO
        )
        mask_ref[half] = jnp.where(near, keep[:, at : at + SPAN], 0.0)


def lay_keys(ref, own, halo):
    ref[:PAD_SIDE] = halo[:PAD_SIDE]
    ref[PAD_SIDE : PAD_SIDE + TOKENS] = own[:TOKENS]
    ref[PAD_SIDE + TOKENS : SPAN] = halo[PAD_SIDE:HALO_QUERIES]
    ref[SPAN : SPAN + BAND] = own[TOKENS:]
    ref[SPAN + BAND :] = halo[HALO_QUERIES:]


class Copies:
    def __init__(self, sems):
        self.sems, self.used = sems, 0

    def start(self, source, target):
        copy = pltpu.make_async_copy(source, target, self.sems.at[self.used])
        self.used += 1
        copy.start()
        return copy

    def load_tokens(self, hbm, ref, lat):
        return [self.start(hbm.at[pl.ds(half_start(lat, k), HALF)], ref.at[pl.ds(k * HALF, HALF)]) for k in range(2)]

    def by_step(self, pairs):
        base, width = self.used, len(pairs(0))
        self.used += STEPS * width

        def copies(j):
            return [pltpu.make_async_copy(a, b, self.sems.at[base + j * width + k]) for k, (a, b) in enumerate(pairs(j))]

        def start(j):
            for copy in copies(j):
                copy.start()

        def wait(j):
            for copy in copies(j):
                copy.wait()

        return start, wait


def wait_all(copies):
    for copy in copies:
        copy.wait()


def lane_block(at, j):
    return pl.ds(pl.multiple_of((at + j) * QUAD, QUAD), QUAD)


def rows_at(j):
    return pl.ds(j * QUAD, QUAD)


def pack_kernel(
    x_hbm, up_hbm, rim_hbm, sel_hbm, edge_a_ref, edge_b_ref, band_ref, corner_a_ref, corner_b_ref,
    x_ref, up_ref, rim_ref, sel_ref, sems,
):
    lat, spot = where()
    copies = Copies(sems)
    loads = copies.load_tokens(x_hbm, x_ref, lat)
    loads += [copies.start(sel_hbm.at[spot], sel_ref), copies.start(rim_hbm.at[lat], rim_ref)]
    grad_loads = copies.load_tokens(up_hbm, up_ref, lat)
    wait_all(loads)
    band_ref[...] = x_ref[:BAND]
    picks = sel_ref[...]
    features = dot(picks, jnp.concatenate([x_ref[...], rim_ref[...]], axis=0))
    wait_all(grad_loads)
    grads = dot(picks[: 2 * EDGE, :TOKENS], up_ref[...])
    for side, (ref, corner_ref) in enumerate(((edge_a_ref, corner_a_ref), (edge_b_ref, corner_b_ref))):
        at = side * EDGE
        ref[...] = jnp.concatenate([features[at : at + EDGE], grads[at : at + SIDE]], axis=0).astype(BF)
        at = 2 * EDGE + side * CORNER
        corner_ref[...] = features[at : at + CORNER].astype(BF)


def own_kernel(
    sharp_ref, x_hbm, rim_hbm, up_hbm, gain_hbm, w3_hbm, wo_hbm,
    qhat_ref, dout_ref, wo_ref, x_ref, gain_ref, qhat_hbm, rawq_hbm, rawk_hbm, kv_hbm,
    kv_ref, w3_ref, rim_ref, up_ref, rawq_ref, rawk_ref, xn_ref, sems,
):
    copies = Copies(sems)
    lat, spot = where()
    loads = copies.load_tokens(x_hbm, x_ref, lat) + [copies.start(rim_hbm.at[lat], rim_ref), copies.start(gain_hbm, gain_ref)]
    start, wait = copies.by_step(
        lambda j: [(w3_hbm.at[:, lane_block(k * STEPS, j)], w3_ref.at[j, :, pl.ds(k * QUAD, QUAD)]) for k in range(3)]
    )
    for j in range(STEPS):
        start(j)
    grad_loads = copies.load_tokens(up_hbm, up_ref, lat)
    parts = [pl.ds(k * D // 2, D // 2) for k in range(2)]
    wo_loads = [copies.start(wo_hbm.at[part], wo_ref.at[part]) for part in parts]
    outputs = [(qhat_ref, qhat_hbm), (rawq_ref, rawq_hbm), (rawk_ref, rawk_hbm), (kv_ref, kv_hbm)]
    store, stored = copies.by_step(lambda j: [(ref.at[j], hbm.at[j]) for ref, hbm in outputs])
    wait_all(loads)
    xn_ref[:TOKENS] = normed(x_ref[...], gain_ref[...]).astype(BF)
    xn_ref[TOKENS:] = normed(rim_ref[...], gain_ref[...]).astype(BF)
    for j in range(STEPS):
        for k in ((0,), (1,), (2, 3), ())[j]:
            wait(k)
        raw = dot(xn_ref[...], w3_ref[j])
        raw_q, raw_k = raw[:TOKENS, :QUAD], raw[:, QUAD : 2 * QUAD]
        units = unit(jnp.concatenate([raw_q, raw_k], axis=0))
        rawq_ref[j] = raw_q.astype(BF)
        rawk_ref[j] = raw_k[:TOKENS].astype(BF)
        qhat_ref[j] = (units[:TOKENS] * multiplier(sharp_ref, j)).astype(BF)
        kv_ref[j, 0] = units[TOKENS:].astype(BF)
        kv_ref[j, 1] = raw[:, 2 * QUAD :].astype(BF)
        store(j)
    wait_all(grad_loads)
    for k, load in enumerate(wo_loads):
        load.wait()
        dout = dot_nt(up_ref[...], wo_ref[parts[k]]).astype(BF)
        for j in range(STEPS // 2):
            dout_ref[k * STEPS // 2 + j] = dout[:, j * QUAD : (j + 1) * QUAD]
    for j in range(STEPS):
        stored(j)


def forward_kernel(
    flag_ref, tab_hbm, sel_hbm, w3_hbm, kv_hbm, band_ref, edge_a_ref, edge_b_ref, corner_a_ref, corner_b_ref, gain_ref,
    qhat_ref, dout_ref,
    mixed_ref, stat_a_ref, stat_b_ref, halo_hbm, stat_hbm, xn_hbm, upn_hbm, weight_hbm, dprime_hbm,
    tab_ref, sel_ref, wkv_ref, kv_ref, halo_ref, stat_ref, xn_ref, upn_ref, weight_ref, dprime_ref, mask_ref, key_ref, value_ref, linv_ref, sems,
):
    lat, spot = where()
    copies = Copies(sems)
    loads = [copies.start(tab_hbm.at[spot], tab_ref.at[0])]
    start, wait = copies.by_step(
        lambda j: [(w3_hbm.at[:, lane_block(k * STEPS, j)], wkv_ref.at[j, :, pl.ds((k - 1) * QUAD, QUAD)]) for k in (1, 2)]
    )
    start_kv, wait_kv = copies.by_step(lambda j: [(kv_hbm.at[j], kv_ref.at[j])])
    for j in range(STEPS):
        start(j)
        start_kv(j)
    loads.append(copies.start(sel_hbm.at[spot], sel_ref))
    store, stored = copies.by_step(
        lambda j: [(halo_ref.at[j], halo_hbm.at[j]), (dprime_ref.at[j], dprime_hbm.at[j])]
    )
    weight_stores = []
    gain = gain_ref[...]
    edge_a, edge_b = edge_a_ref[...].astype(F32), edge_b_ref[...].astype(F32)
    pieces = [ref[...].astype(F32) for ref in (band_ref, corner_a_ref, corner_b_ref)]
    pieces += [edge_a[:SIDE], edge_b[:SIDE], edge_a[SIDE:EDGE], edge_b[SIDE:EDGE]]
    xn_ref[...] = normed(jnp.concatenate(pieces, axis=0), gain).astype(BF)
    upn_ref[...] = jnp.concatenate([edge_a[EDGE:], edge_b[EDGE:]], axis=0).astype(BF)
    stores = [copies.start(xn_ref.at[pl.ds(0, HALO_QUERIES)], xn_hbm), copies.start(upn_ref, upn_hbm)]
    loads[0].wait()
    near_mask(mask_ref, tab_ref, flag_ref, lat)
    stat = jnp.zeros((TOKENS, STATS), F32)
    for j in range(STEPS):
        if j < 2:
            for k in (0,) if j == 0 else range(1, STEPS):
                wait(k)
                wait_kv(k)
        raw = dot(xn_ref[...], wkv_ref[j])
        halo_k = unit(raw[:, :QUAD]).astype(BF)
        halo_v = raw[:, QUAD:].astype(BF)
        halo_ref[j, 0] = halo_k
        halo_ref[j, 1] = halo_v
        lay_keys(key_ref.at[j % 2], kv_ref[j, 0], halo_k)
        lay_keys(value_ref.at[j % 2], kv_ref[j, 1], halo_v)
        for half in range(2):
            at, piece = half * PAD_SIDE, slice(half * HALF, (half + 1) * HALF)
            scores = dot_nt(stacked(qhat_ref[j, piece, :]), key_ref[j % 2, at : at + SPAN])
            weights = jnp.exp(scores) * repeated(mask_ref[half])
            inverse = jnp.broadcast_to(1.0 / jnp.sum(weights, axis=-1, keepdims=True), (STACK, QUAD))
            weights = weights.astype(BF)
            weight_ref[j, half] = weights
            weight_stores.append(copies.start(weight_ref.at[j, half], weight_hbm.at[j, half]))
            mixed = unstacked(dot(weights, value_ref[j % 2, at : at + SPAN]) * inverse)
            mixed_ref[piece, rows_at(j)] = mixed.astype(BF)
            linv_ref[j, piece, :] = unstacked(inverse)
        dprime = (dout_ref[j].astype(F32) * linv_ref[j]).astype(BF)
        dprime_ref[j] = dprime
        inner = dprime.astype(F32) * mixed_ref[:, rows_at(j)].astype(F32)
        stat = stat + dot(linv_ref[j].astype(BF), head_lanes(j * QUAD_HEADS, True))
        stat = stat + dot(inner.astype(BF), head_lanes(HEADS + j * QUAD_HEADS, False))
        store(j)
    stat_ref[...] = stat
    stores.append(copies.start(stat_ref, stat_hbm))
    loads[1].wait()
    picked = dot(sel_ref[: 2 * EDGE, :TOKENS], stat.astype(BF))
    stat_a_ref[...] = picked[:SIDE]
    stat_b_ref[...] = picked[EDGE : EDGE + SIDE]
    for j in range(STEPS):
        stored(j)
    wait_all(stores + weight_stores)


def output_kernel(owner_ref, x_ref, mixed_ref, wo_ref, going_hbm, acc_ref, going_ref, count_ref, sems):
    lat, spot = where()
    copies = Copies(sems)
    for o in range(going_ref.shape[0]):
        count_ref[o] = 0
    slots = []
    for s in range(TOKENS // SEG):
        owner = owner_ref[s // (COLS // SEG), s % (COLS // SEG)]
        slots.append((owner, count_ref[owner]))
        count_ref[owner] = slots[-1][1] + 1
    stores = []
    for part in range(2):
        cols = pl.ds(part * D // 2, D // 2)
        going_ref[:, :, :, cols] = jnp.zeros(going_ref.shape[:3] + (D // 2,), BF)
        rows = x_ref[:, cols].astype(F32) + dot(mixed_ref[...], wo_ref[:, cols])
        for half in range(2):
            acc_ref[pl.ds(half_start(lat, half), HALF), cols] = rows[half * HALF : (half + 1) * HALF]
        for s, (owner, slot) in enumerate(slots):
            going_ref[owner, slot, :, cols] = acc_ref[s * SEG : (s + 1) * SEG, cols].astype(BF)
        stores.append(copies.start(going_ref.at[:, :, :, cols], going_hbm.at[:, :, :, cols]))
    wait_all(stores)


def message_kernel(
    up_hbm, upn_hbm, stat_hbm, stat_a_hbm, stat_b_hbm, out_ref, up_ref, upn_ref, stat_ref, stat_a_ref, stat_b_ref, sems
):
    lat, spot = where()
    piece = pl.ds(half_start(lat, 0), BAND)
    copies = Copies(sems)
    wait_all(
        [
            copies.start(hbm, ref)
            for hbm, ref in (
                (up_hbm.at[piece], up_ref), (upn_hbm, upn_ref), (stat_hbm.at[pl.ds(0, BAND)], stat_ref), (stat_a_hbm, stat_a_ref),
                (stat_b_hbm, stat_b_ref),
            )
        ]
    )
    a = lax.broadcasted_iota(jnp.int32, (2 * CORNER, 2 * SIDE), 0)
    b = lax.broadcasted_iota(jnp.int32, (2 * CORNER, 2 * SIDE), 1)
    side, inside = a // CORNER, HALO * HALO
    row = a - side * CORNER
    picks = jnp.where((b == row + inside * (1 - lat) + side * SIDE) & (row < inside), 1.0, 0.0).astype(BF)
    out_ref[:BAND, :D] = up_ref[...]
    out_ref[BAND:, :D] = dot(picks, upn_ref[...]).astype(BF)
    edges = jnp.concatenate([stat_a_ref[...], stat_b_ref[...]], axis=0).astype(BF)
    out_ref[:BAND, D:] = stat_ref[...].astype(BF)
    out_ref[BAND:, D:] = dot(picks, edges).astype(BF)


def inner_rows(row_ref, j):
    row = HEADS + j * QUAD_HEADS
    width = row_ref.shape[1]
    parts = [jnp.broadcast_to(row_ref[row + h : row + h + 1, :], (HALF, width)) for h in range(QUAD_HEADS)]
    return jnp.concatenate(parts, axis=0)


def key_pass(keys, values, queries, grads, mask, inner):
    weights = jnp.exp(dot_nt(stacked(keys), queries)) * repeated(mask)
    grad_scores = weights * (dot_nt(stacked(values), grads) - inner)
    return unstacked(dot(grad_scores.astype(BF), queries)), unstacked(dot(weights.astype(BF), grads))


def query_kernel(
    sharp_ref, flag_ref, xn_hbm, upn_hbm, tab_hbm, w3_hbm, wo_hbm, qhat_hbm, kv_hbm, halo_hbm, weight_hbm, dprime_hbm,
    rawq_hbm, rawk_hbm, stat_hbm, stat_a_hbm, stat_b_hbm,
    gqn_ref, query_ref, grad_ref, far_ref, mask_ref, wkv_ref, wo_ref, kv_ref, rawk_ref, row_ref,
    xn_ref, upn_ref, tab_ref, wq_ref, qhat_ref, halo_ref, weight_ref, dprime_ref, rawq_ref, stat_ref, stat_a_ref, stat_b_ref,
    key_ref, value_ref, dq_ref, raw_ref, dout_ref, grad_q_ref, sems,
):
    lat, spot = where()
    copies = Copies(sems)
    early = [
        copies.start(hbm, ref)
        for hbm, ref in (
            (tab_hbm.at[spot], tab_ref.at[0]), (stat_hbm, stat_ref), (stat_a_hbm, stat_a_ref), (stat_b_hbm, stat_b_ref),
        )
    ]
    first = [copies.start(xn_hbm, xn_ref)]
    pieces = [pl.ds(k * D // 2, D // 2) for k in range(2)]
    query_loads = [copies.start(w3_hbm.at[:, piece], wq_ref.at[:, piece]) for piece in pieces]
    first.append(copies.start(upn_hbm, upn_ref))
    output_load = copies.start(wo_hbm, wo_ref)
    start, wait = copies.by_step(
        lambda j: [
            (qhat_hbm.at[j], qhat_ref.at[j]),
            (dprime_hbm.at[j], dprime_ref.at[j]),
            (kv_hbm.at[j], kv_ref.at[j]),
            (halo_hbm.at[j], halo_ref.at[j]),
            (weight_hbm.at[j], weight_ref.at[j]),
            (rawq_hbm.at[j], rawq_ref.at[j]),
        ]
    )
    start(0)
    for j in range(1, STEPS):
        start(j)
    later = [
        copies.start(rawk_hbm, rawk_ref),
        copies.start(w3_hbm.at[:, pl.ds(D, 2 * D)], wkv_ref),
    ]
    wait_all(early)
    near_mask(mask_ref, tab_ref, flag_ref, lat)
    edges = jnp.concatenate([stat_a_ref[...], stat_b_ref[...]], axis=0)
    row_ref[...] = jnp.concatenate([stat_ref[...], edges], axis=0).T
    wait_all(first)
    for piece, load in zip(pieces, query_loads):
        load.wait()
        raw_ref[:, piece] = dot(xn_ref[...], wq_ref[:, piece])
    output_load.wait()
    dout_ref[...] = dot_nt(upn_ref[...], wo_ref[...]).astype(BF)
    for j in range(STEPS):
        halo_q = (unit(raw_ref[:, rows_at(j)]) * multiplier(sharp_ref, j)).astype(BF)
        query_ref[j, :PAD_SIDE] = halo_q[:PAD_SIDE]
        query_ref[j, PAD_SIDE + TOKENS :] = halo_q[PAD_SIDE:]
        grad_ref[j, TOKENS:] = (dout_ref[:, rows_at(j)].astype(F32) * spread(edges, j)).astype(BF)
        if j < 2:
            for k in (0,) if j == 0 else range(1, STEPS):
                wait(k)
        query_ref[j, PAD_SIDE : PAD_SIDE + TOKENS] = qhat_ref[j]
        grad_ref[j, :TOKENS] = dprime_ref[j]
        lay_keys(key_ref.at[j % 2], kv_ref[j, 0], halo_ref[j, 0])
        lay_keys(value_ref.at[j % 2], kv_ref[j, 1], halo_ref[j, 1])
        for half in range(2):
            at, piece = half * PAD_SIDE, slice(half * HALF, (half + 1) * HALF)
            stat = stat_ref[piece, :]
            lane = HEADS + j * QUAD_HEADS
            inner = jnp.concatenate([stat[:, lane + h : lane + h + 1] for h in range(QUAD_HEADS)], axis=0)
            grad_probs = dot_nt(stacked(dprime_ref[j, piece, :]), value_ref[j % 2, at : at + SPAN])
            grad_scores = weight_ref[j, half].astype(F32) * (grad_probs - inner)
            dq_ref[j % 2, piece, :] = unstacked(dot(grad_scores.astype(BF), key_ref[j % 2, at : at + SPAN]))
        piece = slice(HALF, TOKENS)
        far_ref[j, 0], far_ref[j, 1] = key_pass(
            kv_ref[j, 0, piece, :], kv_ref[j, 1, piece, :], query_ref[j, PAD_SIDE:], grad_ref[j], mask_ref[1, :, :MIDDLE],
            inner_rows(row_ref, j),
        )
        grad_q = unit_back(rawq_ref[j], dq_ref[j % 2] * multiplier(sharp_ref, j))
        grad_q_ref[:, rows_at(j)] = grad_q.astype(BF)
    gqn_ref[...] = dot_nt(grad_q_ref[...], wq_ref[...])
    wait_all(later)


def key_kernel(
    x_hbm, up_hbm, gain_hbm, gqn_ref, query_ref, grad_ref, far_ref, mask_ref, wkv_ref, wo_ref, kv_ref, rawk_ref, row_ref,
    message_ref,
    out_hbm,
    x_ref, up_ref, gain_ref, out_ref, all_row_ref, all_ref, dk_ref, dout_ref, grad_kv_ref, sems,
):
    lat, spot = where()
    copies = Copies(sems)
    loads = copies.load_tokens(x_hbm, x_ref, lat) + copies.load_tokens(up_hbm, up_ref, lat)
    loads.append(copies.start(gain_hbm, gain_ref))
    message = message_ref[:, D:].astype(F32)
    all_row_ref[...] = jnp.concatenate([message.T, row_ref[...]], axis=1)
    dout_ref[...] = dot_nt(message_ref[:, :D], wo_ref[...]).astype(BF)
    for j in range(STEPS):
        slot = j % 2
        all_ref[slot, :PAD_SIDE] = (dout_ref[:, rows_at(j)].astype(F32) * spread(message, j)).astype(BF)
        all_ref[slot, PAD_SIDE:] = grad_ref[j]
        dk_ref[slot, :HALF, :], near_dv = key_pass(
            kv_ref[j, 0, :HALF, :], kv_ref[j, 1, :HALF, :], query_ref[j], all_ref[slot], mask_ref[0], inner_rows(all_row_ref, j)
        )
        dk_ref[slot, HALF:, :] = far_ref[j, 0]
        grad_kv_ref[:, rows_at(j)] = unit_back(rawk_ref[j], dk_ref[slot]).astype(BF)
        grad_kv_ref[:HALF, rows_at(STEPS + j)] = near_dv.astype(BF)
        grad_kv_ref[HALF:, rows_at(STEPS + j)] = far_ref[j, 1].astype(BF)
    total = gqn_ref[...] + dot_nt(grad_kv_ref[...], wkv_ref[...])
    wait_all(loads)
    stores = []
    for half in range(2):
        piece = slice(half * HALF, (half + 1) * HALF)
        tokens = x_ref[piece, :].astype(F32)
        inverse = lax.rsqrt(jnp.mean(tokens * tokens, axis=-1, keepdims=True) + 1e-05)
        grad = total[piece] * gain_ref[...]
        value = tokens * inverse
        back = inverse * (grad - value * jnp.mean(value * grad, axis=-1, keepdims=True))
        out_ref[piece, :] = (up_ref[piece, :].astype(F32) + back).astype(BF)
        stores.append(copies.start(out_ref.at[pl.ds(half * HALF, HALF)], out_hbm.at[pl.ds(half_start(lat, half), HALF)]))
    wait_all(stores)


def call(kernel, inputs, outputs, scratch=(), limit=32, flops=0, name=None):
    def specs(pairs):
        return [pl.BlockSpec(memory_space=space) for space, _ in pairs]

    def placed(space, array):
        return array if space == pltpu.SMEM else pltpu.with_memory_space_constraint(array, space)

    return pl.pallas_call(
        kernel,
        in_specs=specs(inputs),
        out_specs=specs(outputs),
        out_shape=[space(shape.shape, shape.dtype) for space, shape in outputs],
        scratch_shapes=list(scratch),
        compiler_params=pltpu.CompilerParams(vmem_limit_bytes=limit * MIB),
        cost_estimate=pl.CostEstimate(flops=flops, bytes_accessed=8 << 20, transcendentals=0),
        name=name,
    )(*[placed(space, array) for space, array in inputs])


def hbm(*arrays):
    return [(pltpu.HBM, array) for array in arrays]


def near(*arrays):
    return [(pltpu.VMEM, array) for array in arrays]


def scalars(*arrays):
    return [(pltpu.SMEM, array) for array in arrays]


def like(*shape, dtype=BF):
    return jax.ShapeDtypeStruct(shape, dtype)


def partners(count):
    return (
        [(i, i + 1 - 2 * (i % 2)) for i in range(count)],
        [(i, (i - 1 + 2 * (i % 2)) % count) for i in range(count)],
    )


def across(pairs):
    return [(2 * a + lat, 2 * b + 1 - lat) for a, b in pairs for lat in range(2)]


def per_device(
    slab_features, upstream_gradient, rim_feature_rows, rim_presence_flags, feature_rescaling_coefficients,
    triple_projection_matrix, final_projection_matrix, score_sharpness, column_group_decoder_longitude,
):
    count = lax.axis_size("lon")
    cap = max(2, (2 * (TOKENS // SEG) + count - 1) // count)
    x = slab_features.reshape(TOKENS, D)
    up = upstream_gradient.reshape(TOKENS, D)
    rim = rim_feature_rows.reshape(2, BAND, D)
    gain = feature_rescaling_coefficients.reshape(1, D)
    w3, wo = triple_projection_matrix, final_projection_matrix
    table = selection_table()
    selection = jnp.asarray(table, BF)
    keys = jnp.asarray(key_table())
    flags = rim_presence_flags

    side_a, side_b = partners(count)

    def vmem(*shape, dtype=BF):
        return pltpu.VMEM(shape, dtype)

    def sems(n):
        return pltpu.SemaphoreType.DMA((n,))

    picks_shape = table.shape[1:]
    edge_a, edge_b, band, corner_a, corner_b = call(
        pack_kernel,
        hbm(x, up, rim, selection),
        near(like(EDGE + SIDE, D), like(EDGE + SIDE, D), like(BAND, D), like(CORNER, D), like(CORNER, D)),
        [vmem(TOKENS, D), vmem(TOKENS, D), vmem(BAND, D), vmem(*picks_shape), sems(6)],
        limit=24, name="edge_tokens",
    )
    band = lax.ppermute(band, "lat", [(0, 1), (1, 0)])
    corner_a = lax.ppermute(corner_a, ("lon", "lat"), across(side_a))
    corner_b = lax.ppermute(corner_b, ("lon", "lat"), across(side_b))
    edge_b = lax.ppermute(edge_b, "lon", side_b)
    edge_a = lax.ppermute(edge_a, "lon", side_a)

    quads = like(STEPS, TOKENS, QUAD)
    kv_like = like(STEPS, 2, TOKENS + BAND, QUAD)
    qhat_near, dout, wo_near, x_near, gain_near, qhat, rawq, rawk, kv = call(
        own_kernel,
        scalars(score_sharpness) + hbm(x, rim, up, gain, w3, wo),
        near(quads, quads, like(D, D), like(TOKENS, D), like(1, D, dtype=F32))
        + hbm(quads, quads, quads, kv_like),
        [vmem(STEPS, 2, TOKENS + BAND, QUAD), vmem(STEPS, D, 3 * QUAD), vmem(BAND, D), vmem(TOKENS, D),
         vmem(STEPS, TOKENS, QUAD), vmem(STEPS, TOKENS, QUAD), vmem(TOKENS + BAND, D), sems(6 + 4 * STEPS + 4 * STEPS)],
        limit=24, flops=2 * 1024 * 1024 * (192 * 2 + 288 * 2), name="own_projections",
    )

    kv_scratch = vmem(STEPS, 2, TOKENS + BAND, QUAD)
    stat_like, side_like = like(TOKENS, STATS, dtype=F32), like(SIDE, STATS, dtype=F32)
    mixed, stat_a, stat_b, halo_kv, stat, xn_halo, up_halo, weights, dprime = call(
        forward_kernel,
        scalars(flags) + hbm(keys, selection, w3, kv)
        + near(band, edge_a, edge_b, corner_a, corner_b, gain_near, qhat_near, dout),
        near(like(TOKENS, D), side_like, side_like)
        + hbm(like(STEPS, 2, HALO_ROWS, QUAD), stat_like, like(HALO_QUERIES, D), like(2 * SIDE, D),
              like(STEPS, 2, STACK, SPAN), quads),
        [vmem(1, 8, KEYS, dtype=jnp.int32), vmem(*picks_shape), vmem(STEPS, D, 2 * QUAD), kv_scratch, vmem(STEPS, 2, HALO_ROWS, QUAD),
         vmem(TOKENS, STATS, dtype=F32),
         vmem(HALO_ROWS, D), vmem(2 * SIDE, D), vmem(STEPS, 2, STACK, SPAN), vmem(STEPS, TOKENS, QUAD),
         vmem(2, HALF, SPAN, dtype=F32), vmem(2, KEYS, QUAD), vmem(2, KEYS, QUAD), vmem(STEPS, TOKENS, QUAD, dtype=F32),
         sems(2 + 3 * STEPS + 4 * STEPS + 3)],
        limit=24, flops=2 * 1024 * 1024 * 2000, name="attention_forward",
    )
    stat_b = lax.ppermute(stat_b, "lon", side_b)
    stat_a = lax.ppermute(stat_a, "lon", side_a)

    (going,) = call(
        output_kernel,
        scalars(column_group_decoder_longitude) + near(x_near, mixed, wo_near),
        hbm(like(count, cap, SEG, D)),
        [vmem(TOKENS, D, dtype=F32), vmem(count, cap, SEG, D), pltpu.SMEM((count,), jnp.int32), sems(2)],
        limit=24, flops=2 * 1024 * 1024 * 200, name="output_segments",
    )
    going, stat_a, stat_b = lax.optimization_barrier((going, stat_a, stat_b))
    arrived = lax.all_to_all(going, "lon", split_axis=0, concat_axis=0, tiled=True)

    (message,) = call(
        message_kernel,
        hbm(up, up_halo, stat, stat_a, stat_b),
        near(like(PAD_SIDE, MESSAGE)),
        [vmem(BAND, D), vmem(2 * SIDE, D), vmem(BAND, STATS, dtype=F32), vmem(SIDE, STATS, dtype=F32), vmem(SIDE, STATS, dtype=F32),
         sems(5)],
        limit=24, flops=1024, name="boundary_message",
    )
    message = lax.ppermute(message, "lat", [(0, 1), (1, 0)])

    handed = call(
        query_kernel,
        scalars(score_sharpness, flags)
        + hbm(xn_halo, up_halo, keys, w3, wo, qhat, kv, halo_kv, weights, dprime, rawq, rawk, stat, stat_a, stat_b),
        near(like(TOKENS, D, dtype=F32), like(STEPS, SPAN, QUAD), like(STEPS, MIDDLE, QUAD), like(STEPS, 2, HALF, QUAD, dtype=F32),
             like(2, HALF, SPAN, dtype=F32), like(D, 2 * D), like(D, D), kv_like, quads, like(STATS, MIDDLE, dtype=F32)),
        [vmem(HALO_QUERIES, D), vmem(2 * SIDE, D), vmem(1, 8, KEYS, dtype=jnp.int32), vmem(D, D),
         vmem(STEPS, TOKENS, QUAD), vmem(STEPS, 2, HALO_ROWS, QUAD), vmem(STEPS, 2, STACK, SPAN), vmem(STEPS, TOKENS, QUAD),
         vmem(STEPS, TOKENS, QUAD), vmem(TOKENS, STATS, dtype=F32), vmem(SIDE, STATS, dtype=F32),
         vmem(SIDE, STATS, dtype=F32), vmem(2, KEYS, QUAD), vmem(2, KEYS, QUAD), vmem(2, TOKENS, QUAD, dtype=F32),
         vmem(HALO_QUERIES, D, dtype=F32), vmem(2 * SIDE, D), vmem(TOKENS, D), sems(4 + 5 + 6 * STEPS + 2)],
        limit=24, flops=2 * 1024 * 1024 * 4000, name="query_gradient",
    )

    (input_grad,) = call(
        key_kernel,
        hbm(x, up, gain) + near(*handed, message),
        hbm(like(TOKENS, D)),
        [vmem(TOKENS, D), vmem(TOKENS, D), vmem(1, D, dtype=F32), vmem(TOKENS, D), vmem(STATS, SPAN, dtype=F32),
         vmem(2, SPAN, QUAD), vmem(2, TOKENS, QUAD, dtype=F32), vmem(PAD_SIDE, D), vmem(TOKENS, 2 * D), sems(7)],
        limit=24, flops=2 * 1024 * 1024 * 2000, name="key_gradient",
    )
    return (
        arrived.reshape(1, 1, count, cap, SEG, D),
        input_grad.reshape(ROWS, COLS, D),
    )


def solution(mesh):
    return jax.shard_map(
        per_device,
        mesh=mesh,
        in_specs=(
            P("lat", "lon", None),
            P("lat", "lon", None),
            P(None, None, "lon", None),
            P(),
            P(),
            P(),
            P(),
            P(),
            P("lat", "lon"),
        ),
        out_specs=(P("lat", "lon", None, None, None, None), P("lat", "lon", None)),
        check_vma=False,
    )
```
